32 devices in a mesh: section: 2 (over x), fsdp: 4 (over z), replica: 4 (over y, core).
Axes of the slice: x: 2, y: 2, z: 4, core: 2. Of those that a mesh axis runs over, the one named last changes fastest.
Arguments:
- ends: bfloat16 [2, 96, 160, 1152], P('section', ('fsdp', 'replica')), may hold values from -6 to 6
- first_gain: bfloat16 [2, 1152], P('section', 'fsdp'), may hold values from 0.5 to 1.5
- first_shift: bfloat16 [2, 1152], P('section', 'fsdp'), may hold values from -2 to 2
- qkv_weight: bfloat16 [2, 1152, 3456], P('section', 'fsdp'), may hold values from -0.1875 to 0.1875
- qv_bias: bfloat16 [2, 2, 1152], P('section', None, 'fsdp'), may hold values from -3 to 3
- out_weight: bfloat16 [2, 1152, 1152], P('section', 'fsdp'), may hold values from -0.5 to 0.5
- out_bias: bfloat16 [2, 1152], P('section', 'fsdp'), may hold values from -2 to 2
- second_gain: bfloat16 [2, 1152], P('section', 'fsdp'), may hold values from 0.5 to 1.5
- second_shift: bfloat16 [2, 1152], P('section', 'fsdp'), may hold values from -2 to 2
- up_weight: bfloat16 [2, 1152, 4304], P('section', 'fsdp'), may hold values from -0.1875 to 0.1875
- up_bias: bfloat16 [2, 4304], P('section', 'fsdp'), may hold values from -3 to 3
- down_weight: bfloat16 [2, 4304, 1152], P('section', None, 'fsdp'), may hold values from -0.09375 to 0.09375
- down_bias: bfloat16 [2, 1152], P('section', 'fsdp'), may hold values from -2 to 2
Outputs:
- result_ends: float32 [2, 96, 160, 1152], P('section', ('fsdp', 'replica'))
- grad_first_gain: float32 [2, 1152], P('section', 'fsdp')
- grad_first_shift: float32 [2, 1152], P('section', 'fsdp')
- grad_qkv_weight: float32 [2, 1152, 3456], P('section', 'fsdp')
- grad_qv_bias: float32 [2, 2, 1152], P('section', None, 'fsdp')
- grad_out_weight: float32 [2, 1152, 1152], P('section', 'fsdp')
- grad_out_bias: float32 [2, 1152], P('section', 'fsdp')
- grad_second_gain: float32 [2, 1152], P('section', 'fsdp')
- grad_second_shift: float32 [2, 1152], P('section', 'fsdp')
- grad_up_weight: float32 [2, 1152, 4304], P('section', 'fsdp')
- grad_up_bias: float32 [2, 4304], P('section', 'fsdp')
- grad_down_weight: float32 [2, 4304, 1152], P('section', None, 'fsdp')
- grad_down_bias: float32 [2, 1152], P('section', 'fsdp')
The draws below stay inside these ranges and needn't reach their ends.
All inputs are finite; a program needn't handle non-finite values.
Results may differ from the reference program's by a relative error of at most 0.009.
Values may be sent and summed in bfloat16 or wider, within the bound.
A program may use at most 320 MiB of HBM per device.

```python
import math
import jax
import jax.numpy as jnp
from jax import lax

D = 1152
HEADS = 16
HEAD_DIM = 72
FF = 4304
LAYERS = 2
TOK = 160
IMG_DEV = 6
IMAGES = 96


def levels(stream_key, extent, pieces, smallest, largest):
    factor_of = 1.0
    for position, parts in pieces:
        steps = jax.random.uniform(jax.random.fold_in(jax.random.fold_in(stream_key, 6), position), (parts,), jnp.float32, smallest / len(pieces), largest / len(pieces))
        factor_of = factor_of * jnp.repeat(jnp.exp(steps), extent[position] // parts).reshape((-1,) + (1,) * (len(extent) - 1 - position))
    return factor_of


def normal_values(key, extent, width, most, shards=(), dtype=jnp.bfloat16):
    loudness = levels(key, extent, shards, -0.22, 0.18) if shards else 1.0
    values = jax.random.normal(key, extent, jnp.float32) * width * loudness
    return jnp.minimum(jnp.maximum(values, -most), most).astype(dtype)


def setup_inputs(seed: int = 0) -> dict:
    seeds = jax.random.split(jax.random.key(seed), 14)
    return {
        "ends": normal_values(seeds[0], (2, IMAGES, TOK, D), 1.0, 6.0, ((0, 2), (1, 16))),
        "first_gain": jnp.clip(1.0 + 0.1 * jax.random.normal(seeds[1], (LAYERS, D), jnp.float32), 0.5, 1.5).astype(jnp.bfloat16),
        "first_shift": normal_values(seeds[2], (LAYERS, D), 0.3, 2.0, ((0, 2), (1, 4))),
        "qkv_weight": normal_values(seeds[3], (LAYERS, D, 3 * D), D ** -0.5, 0.1875, ((0, 2), (1, 4))),
        "qv_bias": normal_values(seeds[4], (LAYERS, 2, D), 0.5, 3.0, ((0, 2), (2, 4))),
        "out_weight": normal_values(seeds[5], (LAYERS, D, D), (D // 8) ** -0.5, 0.5, ((0, 2), (1, 4))),
        "out_bias": normal_values(seeds[6], (LAYERS, D), 0.3, 2.0, ((0, 2), (1, 4))),
        "second_gain": jnp.clip(1.0 + 0.1 * jax.random.normal(seeds[7], (LAYERS, D), jnp.float32), 0.5, 1.5).astype(jnp.bfloat16),
        "second_shift": normal_values(seeds[8], (LAYERS, D), 0.3, 2.0, ((0, 2), (1, 4))),
        "up_weight": normal_values(seeds[9], (LAYERS, D, FF), D ** -0.5, 0.1875, ((0, 2), (1, 4))),
        "up_bias": normal_values(seeds[10], (LAYERS, FF), 0.5, 3.0, ((0, 2), (1, 4))),
        "down_weight": normal_values(seeds[11], (LAYERS, FF, D), FF ** -0.5, 0.09375, ((0, 2), (2, 4))),
        "down_bias": normal_values(seeds[12], (LAYERS, D), 0.3, 2.0, ((0, 2), (1, 4))),
    }


@jax.custom_vjp
def low(v):
    return lax.optimization_barrier(v.astype(jnp.bfloat16)).astype(jnp.float32)

@jax.custom_vjp
def low_back(v):
    return v

def low_keep(v):
    return (low(v), None)

def low_pass(kept, grad):
    return (grad,)

def back_keep(v):
    return (v, None)

def back_low(kept, grad):
    return (low(grad),)
low.defvjp(low_keep, low_pass)
low_back.defvjp(back_keep, back_low)
HIGH = lax.Precision.HIGHEST

def gelu_tanh(signal):
    return 0.5 * signal * (1.0 + jnp.tanh(math.sqrt(2.0 / math.pi) * (signal + 0.044715 * signal * signal * signal)))

def layer_norm(signal, gain, shift):
    center = signal - lax.optimization_barrier(jnp.mean(signal, axis=-1, keepdims=True))
    spread = lax.optimization_barrier(jnp.mean(center * center, axis=-1, keepdims=True))
    return center * lax.rsqrt(spread + 1e-06) * gain + shift

def project(left, right):
    return jnp.einsum('bsd,de->bse', left, right, precision=HIGH)

def layer(tokens_in, layer_params):
    gain_one, shift_one, weight_qkv, bias_qv, weight_out, bias_out, gain_two, shift_two, weight_up, bias_up, weight_down, bias_down = layer_params
    batches, seq_len, model_width = tokens_in.shape
    normed = low(layer_norm(tokens_in, gain_one, shift_one))
    qkv_bias = jnp.concatenate([bias_qv[0], jnp.zeros_like(bias_qv[0]), bias_qv[1]])
    joined = low(low_back(project(normed, weight_qkv) + qkv_bias))
    queries = joined[..., :model_width].reshape(batches, seq_len, HEADS, HEAD_DIM)
    key_rows = joined[..., model_width:2 * model_width].reshape(batches, seq_len, HEADS, HEAD_DIM)
    values = joined[..., 2 * model_width:].reshape(batches, seq_len, HEADS, HEAD_DIM)
    raw_scores = jnp.einsum('bqhc,bkhc->bhqk', queries, key_rows, precision=HIGH)
    scores = low_back(raw_scores * HEAD_DIM ** (-0.5))
    attn_probs = low(jax.nn.softmax(scores, axis=-1))
    context = jnp.einsum('bhqk,bkhc->bqhc', attn_probs, values, precision=HIGH).reshape(batches, seq_len, model_width)
    context = low(low_back(context))
    mixed_rows = tokens_in + low_back(project(context, weight_out) + bias_out)
    normed_two = low(layer_norm(mixed_rows, gain_two, shift_two))
    pre_act = low_back(project(normed_two, weight_up) + bias_up)
    activated = low(gelu_tanh(pre_act))
    return mixed_rows + low_back(project(activated, weight_down) + bias_down)

def reference(ends, first_gain, first_shift, qkv_weight, qv_bias, out_weight, out_bias, second_gain, second_shift, up_weight, up_bias, down_weight, down_bias):
    params = tuple((item.astype(jnp.float32) for item in (first_gain, first_shift, qkv_weight, qv_bias, out_weight, out_bias, second_gain, second_shift, up_weight, up_bias, down_weight, down_bias)))
    inputs = ends[0].astype(jnp.float32)
    cotangent = ends[1].astype(jnp.float32)
    groups = inputs.shape[0] // IMG_DEV

    def forward(tokens_in, layer_params):
        lower_layer = tuple((item[0] for item in layer_params))
        upper_layer = tuple((item[1] for item in layer_params))

        def one_group(image_block):
            middle = low_back(low(layer(image_block, lower_layer)))
            return layer(middle, upper_layer)
        grouped = tokens_in.reshape(groups, IMG_DEV, TOK, D)
        return lax.map(jax.checkpoint(one_group), grouped).reshape(tokens_in.shape)
    output, pullback = jax.vjp(forward, inputs, params)
    grad_inputs, grads = pullback(cotangent)
    g_first_gain, g_first_shift, g_qkv_weight, g_qv_bias, g_out_weight, g_out_bias, g_second_gain, g_second_shift, g_up_weight, g_up_bias, g_down_weight, g_down_bias = grads
    result_ends = jnp.stack([grad_inputs, output])
    return (result_ends, g_first_gain, g_first_shift, g_qkv_weight, g_qv_bias, g_out_weight, g_out_bias, g_second_gain, g_second_shift, g_up_weight, g_up_bias, g_down_weight, g_down_bias)
```

```python
import functools
import math

import jax
import jax.numpy as jnp
from jax import lax
from jax.experimental import pallas as pl
from jax.experimental.pallas import tpu as pltpu
from jax.sharding import PartitionSpec as P

MESH = pl.DeviceIdType.MESH
HEADS = 16
HEAD_DIM = 72
MICRO = 2


def powers(count):
    bits = []
    bit = count // 2
    while bit:
        bits.append(bit)
        bit //= 2
    return bits

def gather_kernel(n, R, qkv, out, up, down, small, G, S, stage, stage_small, lsem, ssem, rsem, small_send, small_recv):
    z = lax.axis_index("fsdp")
    r = lax.axis_index("replica")
    rows, wide = up.shape
    part = wide // R
    bits = powers(R)
    barrier = pltpu.get_barrier_semaphore()
    for hop in range(1, n):
        pl.semaphore_signal(barrier, inc=1, device_id={"fsdp": lax.rem(z + hop, n)}, device_id_type=MESH)
    for bit in bits:
        pl.semaphore_signal(barrier, inc=1, device_id={"replica": r ^ bit}, device_id_type=MESH)
    mine = pl.ds(pl.multiple_of(z * rows, 16), rows)
    first = qkv.shape[1]
    local = [
        pltpu.make_async_copy(qkv, stage.at[0, :, pl.ds(0, first)], lsem.at[0]),
        pltpu.make_async_copy(out, stage.at[0, :, pl.ds(first, out.shape[1])], lsem.at[1]),
        pltpu.make_async_copy(up, stage.at[1], lsem.at[2]),
        pltpu.make_async_copy(down, stage.at[2], lsem.at[3]),
        pltpu.make_async_copy(small, stage_small, lsem.at[4]),
    ]
    for copy in local:
        copy.start()
    keep = [pltpu.make_async_copy(stage.at[group], G.at[group, mine], lsem.at[5 + group]) for group in range(3)]
    keep.append(pltpu.make_async_copy(stage_small, S.at[z], lsem.at[8]))
    pl.semaphore_wait(barrier, n - 1 + len(bits))

    def piece(group, source, column):
        return G.at[group, pl.ds(pl.multiple_of(source * rows, 16), rows),
                    pl.ds(pl.multiple_of(column * part, 128), part)]

    def send(group, source, column, kind, target, origin=None):
        return pltpu.make_async_remote_copy(
            src_ref=piece(group, source, column) if origin is None else origin, dst_ref=piece(group, source, column),
            send_sem=ssem.at[group, source, column, kind], recv_sem=rsem.at[group, source, column],
            device_id=target, device_id_type=MESH)

    def to_right(group, source, origin=None):
        return send(group, source, r, 0, {"fsdp": z + 1}, origin)

    def to_left(group, source, origin=None):
        return send(group, source, r, 1, {"fsdp": z - 1}, origin)

    def own(group):
        return stage.at[group, :, pl.ds(pl.multiple_of(r * part, 128), part)]

    def share(group, source, column, level):
        return send(group, source, column, 2 + level, {"replica": r ^ bits[level]})

    def arrived(group, source, column):
        send(group, source, column, 0, {"replica": r ^ bits[0]}).wait_recv()

    def small_to(hop):
        return pltpu.make_async_remote_copy(
            src_ref=small, dst_ref=S.at[z], send_sem=small_send.at[hop],
            recv_sem=small_recv.at[z], device_id={"fsdp": lax.rem(z + hop, n)}, device_id_type=MESH)
    for hop in range(1, n):
        small_to(hop).start()
    for group in range(3):
        if group == 0:
            local[0].wait()
            local[1].wait()
        else:
            local[1 + group].wait()
        @pl.when(z + 1 < n)
        def _():
            to_right(group, z, own(group)).start()
        @pl.when(z > 0)
        def _():
            to_left(group, z, own(group)).start()
        keep[group].start()
    local[4].wait()
    keep[3].start()
    columns = {}
    for level, bit in enumerate(bits):
        masks = [0]
        for upper in bits[:level]:
            masks = masks + [m | upper for m in masks]
        columns[level] = [bit | m for m in masks]
    steps = [(hop, group) for hop in range(1, n) for group in range(3)]
    for turn in range(len(steps) + len(bits)):
        for level in range(-1, len(bits)):
            place = turn - 1 - level
            if place < 0 or place >= len(steps):
                continue
            hop, group = steps[place]
            for sign in (-1, 1):
                source = z + sign * hop
                @pl.when((source >= 0) & (source < n))
                def _():
                    if level < 0:
                        arrived(group, source, r)
                        for lower in range(len(bits)):
                            share(group, source, r, lower).start()
                        if sign < 0:
                            @pl.when(z + 1 < n)
                            def _():
                                to_right(group, source).start()
                        else:
                            @pl.when(z > 0)
                            def _():
                                to_left(group, source).start()
                    else:
                        for mask in columns[level]:
                            arrived(group, source, r ^ mask)
                            for lower in range(level + 1, len(bits)):
                                share(group, source, r ^ mask, lower).start()
    for copy in keep:
        copy.wait()
    for hop in range(1, n):
        pltpu.make_async_remote_copy(
            src_ref=small, dst_ref=S.at[lax.rem(z + hop, n)], send_sem=small_send.at[hop],
            recv_sem=small_recv.at[lax.rem(z + hop, n)], device_id={"fsdp": lax.rem(z + hop, n)}, device_id_type=MESH).wait_recv()
        small_to(hop).wait_send()
    for group in range(3):
        for source in range(n):
            @pl.when((source <= z) & (z + 1 < n))
            def _():
                to_right(group, source).wait_send()
            @pl.when((source >= z) & (z > 0))
            def _():
                to_left(group, source).wait_send()
            @pl.when(source != z)
            def _():
                for level in range(len(bits)):
                    share(group, source, r, level).wait_send()
                for level in range(len(bits)):
                    for mask in columns[level]:
                        for lower in range(level + 1, len(bits)):
                            share(group, source, r ^ mask, lower).wait_send()

def gather_weights(n, R, qkv, out, up, down, small):
    rows, wide = up.shape
    kinds = 2 + len(powers(R))
    return pl.pallas_call(
        functools.partial(gather_kernel, n, R),
        out_shape=(jax.ShapeDtypeStruct((3, n * rows, wide), qkv.dtype),
                   jax.ShapeDtypeStruct((n,) + small.shape, small.dtype)),
        in_specs=[pl.BlockSpec(memory_space=pl.ANY)] * 5,
        out_specs=(pl.BlockSpec(memory_space=pl.ANY),) * 2,
        scratch_shapes=[
            pltpu.VMEM((3, rows, wide), qkv.dtype),
            pltpu.VMEM(small.shape, small.dtype),
            pltpu.SemaphoreType.DMA((9,)),
            pltpu.SemaphoreType.DMA((3, n, R, kinds)),
            pltpu.SemaphoreType.DMA((3, n, R)),
            pltpu.SemaphoreType.DMA((n,)),
            pltpu.SemaphoreType.DMA((n,)),
        ],
        compiler_params=pltpu.CompilerParams(collective_id=0, has_side_effects=True, vmem_limit_bytes=32 * 1024 * 1024),
    )(qkv, out, up, down, small)


def reduce_kernel(n, R, sub, small_in, a_in, u_in, d_in, F, small_out, *scratch):
    bits = []
    while (1 << len(bits)) < R:
        bits.append(1 << len(bits))
    L = len(bits)
    held = scratch[:L]
    (xv, flow, small_z, small_r, small_sum, xsem, send_sem, recv_sem, zsend, zrecv, fsend, frecv, fkeep,
     ss_z, sr_z, ss_r, sr_r, ss_l) = scratch[L:]
    z = lax.axis_index("fsdp")
    r = lax.axis_index("replica")
    inputs = (a_in, u_in, d_in)
    full = a_in.shape[0]
    rows = full // n
    wide = a_in.shape[1]
    part = wide // R
    subs = part // sub
    K = 3 * subs
    barrier = pltpu.get_barrier_semaphore()
    for hop in range(1, n):
        pl.semaphore_signal(barrier, inc=1, device_id={"fsdp": lax.rem(z + hop, n)}, device_id_type=MESH)
    for hop in range(1, R):
        pl.semaphore_signal(barrier, inc=1, device_id={"replica": lax.rem(r + hop, R)}, device_id_type=MESH)

    def columns(k, p):
        return pl.ds(pl.multiple_of(p * part + (k % subs) * sub, 128), sub)

    def block(t):
        return pl.ds(pl.multiple_of(t * rows, 16), rows)

    def low(level):
        return r & ((1 << level) - 1)

    def kept(level, j):
        return low(level + 1) | (j << (level + 1))

    def load(k, j):
        return pltpu.make_async_copy(inputs[k // subs].at[:, columns(k, kept(0, j))], xv.at[k % 2, j], xsem.at[k % 2, j])

    def give(level, k, j):
        if level == 0:
            source = inputs[k // subs].at[:, columns(k, (r ^ 1) & 1 | (j << 1))]
        else:
            source = held[level - 1].at[k, 2 * j + (((r >> level) & 1) ^ 1)]
        return pltpu.make_async_remote_copy(
            src_ref=source, dst_ref=held[level].at[k, j], send_sem=send_sem.at[level, k, j],
            recv_sem=recv_sem.at[level, k, j], device_id={"replica": r ^ bits[level]}, device_id_type=MESH)

    STEP = 96 if full % 96 == 0 else 16

    def start(k):
        for j in range(R // 2):
            give(0, k, j).start()
            load(k, j).start()

    def merge(level, k):
        for j in range(R >> (level + 1)):
            give(level, k, j).wait_recv()
            if level == 0:
                load(k, j).wait()
            mine = held[level].at[k, j]
            other = xv.at[k % 2, j] if level == 0 else held[level - 1].at[k, 2 * j + ((r >> level) & 1)]
            def body(i, c):
                at = pl.ds(pl.multiple_of(i * STEP, 16), STEP)
                mine[at, :] = (mine[at, :].astype(jnp.float32) + other[at, :].astype(jnp.float32)).astype(mine.dtype)
                return c
            lax.fori_loop(0, full // STEP, body, 0)
        if level + 1 < L:
            for j in range(R >> (level + 2)):
                give(level + 1, k, j).start()

    def pass_on(k, t, side, source):
        return pltpu.make_async_remote_copy(
            src_ref=source, dst_ref=flow.at[k, side, t], send_sem=zsend.at[k, side, t], recv_sem=zrecv.at[k, side, t],
            device_id={"fsdp": z + 1 if side == 0 else z - 1}, device_id_type=MESH)

    def launch(k):
        total = held[L - 1].at[k, 0]
        @pl.when(z == 0)
        def _():
            for t in range(n - 1, 0, -1):
                pass_on(k, t, 0, total.at[block(t)]).start()
        @pl.when(z == n - 1)
        def _():
            for t in range(n - 1):
                pass_on(k, t, 1, total.at[block(t)]).start()

    RSTEP = 96 if rows % 96 == 0 else 16

    def add_block(target, other, at_other):
        def body(i, c):
            at = pl.ds(pl.multiple_of(i * RSTEP, 16), RSTEP)
            there = pl.ds(pl.multiple_of(at_other + i * RSTEP, 16), RSTEP)
            target[at, :] = (target[at, :].astype(jnp.float32) + other[there, :].astype(jnp.float32)).astype(target.dtype)
            return c
        lax.fori_loop(0, rows // RSTEP, body, 0)

    def flows(k):
        total = held[L - 1].at[k, 0]
        for step in range(n):
            t0, t1 = n - 1 - step, step
            @pl.when((z > 0) & (t0 >= z))
            def _():
                pass_on(k, t0, 0, flow.at[k, 0, t0]).wait_recv()
                add_block(flow.at[k, 0, t0], total, t0 * rows)
                @pl.when(t0 > z)
                def _():
                    pass_on(k, t0, 0, flow.at[k, 0, t0]).start()
            @pl.when((z < n - 1) & (t1 <= z))
            def _():
                pass_on(k, t1, 1, flow.at[k, 1, t1]).wait_recv()
                @pl.when(t1 < z)
                def _():
                    add_block(flow.at[k, 1, t1], total, t1 * rows)
                    pass_on(k, t1, 1, flow.at[k, 1, t1]).start()
        @pl.when(z == 0)
        def _():
            add_block(flow.at[k, 1, 0], total, 0)
        @pl.when((z > 0) & (z < n - 1))
        def _():
            add_block(flow.at[k, 1, z], flow.at[k, 0, z], 0)

    def finished(k, p):
        return F.at[k // subs, :, columns(k, p)]

    def share(k, p, level, source=None):
        return pltpu.make_async_remote_copy(
            src_ref=finished(k, p) if source is None else source, dst_ref=finished(k, p),
            send_sem=fsend.at[k, p, level], recv_sem=frecv.at[k, p], device_id={"replica": r ^ bits[level]}, device_id_type=MESH)

    def keep(k, side):
        return pltpu.make_async_copy(flow.at[k, side, z], finished(k, r), fkeep.at[k])

    def publish(k):
        @pl.when(z < n - 1)
        def _():
            for level in reversed(range(L)):
                share(k, r, level, flow.at[k, 1, z]).start()
            keep(k, 1).start()
        @pl.when(z == n - 1)
        def _():
            for level in reversed(range(L)):
                share(k, r, level, flow.at[k, 0, z]).start()
            keep(k, 0).start()

    def masks(level):
        found = [0]
        for upper in range(level + 1, L):
            found = found + [m | bits[upper] for m in found]
        return [m | bits[level] for m in found]

    def collect(level, k):
        for mask in masks(level):
            p = r ^ mask
            share(k, p, level).wait_recv()
            for lower in reversed(range(level)):
                share(k, p, lower).start()

    def small_to_z(t):
        return pltpu.make_async_remote_copy(
            src_ref=small_in.at[t], dst_ref=small_z.at[z], send_sem=ss_z.at[t], recv_sem=sr_z.at[z],
            device_id={"fsdp": t}, device_id_type=MESH)

    def small_to_r(p):
        return pltpu.make_async_remote_copy(
            src_ref=small_sum, dst_ref=small_r.at[r], send_sem=ss_r.at[p], recv_sem=sr_r.at[r],
            device_id={"replica": p}, device_id_type=MESH)

    pl.semaphore_wait(barrier, n - 1 + R - 1)
    own_small = pltpu.make_async_copy(small_in.at[z], small_z.at[z], ss_l)
    own_small.start()
    start(0)
    for hop in range(1, n):
        small_to_z(lax.rem(z + hop, n)).start()
    stages = 1 + L + 1 + L
    for turn in range(K + stages - 1):
        for stage in range(stages):
            k = turn - stage
            if k < 0 or k >= K:
                continue
            if stage == 0:
                if k > 0:
                    start(k)
            elif stage <= L:
                merge(stage - 1, k)
                if stage == L:
                    launch(k)
            elif stage == L + 1:
                flows(k)
                publish(k)
            else:
                collect(L - 1 - (stage - L - 2), k)
        if turn == 1:
            own_small.wait()
            for hop in range(1, n):
                source = lax.rem(z + hop, n)
                pltpu.make_async_remote_copy(
                    src_ref=small_in.at[source], dst_ref=small_z.at[source], send_sem=ss_z.at[source],
                    recv_sem=sr_z.at[source], device_id={"fsdp": source}, device_id_type=MESH).wait_recv()
            together = small_z[0]
            for t in range(1, n):
                together = together + small_z[t]
            small_sum[...] = together
            small_r[r] = together
            for hop in range(1, R):
                small_to_r(lax.rem(r + hop, R)).start()
    for hop in range(1, R):
        p = lax.rem(r + hop, R)
        pltpu.make_async_remote_copy(
            src_ref=small_sum, dst_ref=small_r.at[p], send_sem=ss_r.at[p], recv_sem=sr_r.at[p],
            device_id={"replica": p}, device_id_type=MESH).wait_recv()
    together = small_r[0]
    for p in range(1, R):
        together = together + small_r[p]
    small_out[...] = together
    for hop in range(1, R):
        small_to_r(lax.rem(r + hop, R)).wait_send()
    for hop in range(1, n):
        small_to_z(lax.rem(z + hop, n)).wait_send()
    for k in range(K):
        for level in range(L):
            for j in range(R >> (level + 1)):
                give(level, k, j).wait_send()
        for t in range(n):
            @pl.when((t > z))
            def _():
                pass_on(k, t, 0, flow.at[k, 0, t]).wait_send()
            @pl.when((t < z))
            def _():
                pass_on(k, t, 1, flow.at[k, 1, t]).wait_send()
        keep(k, 0).wait()
        for level in range(L):
            share(k, r, level).wait_send()
            for mask in masks(level):
                for lower in range(level):
                    share(k, r ^ mask, lower).wait_send()

def reduce_grads(n, R, small, a, u, d):
    full, wide = a.shape
    rows = full // n
    part = wide // R
    sub = next(s for s in (384, 256, 128) if part % s == 0)
    K = 3 * (part // sub)
    L = R.bit_length() - 1
    dma = pltpu.SemaphoreType.DMA
    return pl.pallas_call(
        functools.partial(reduce_kernel, n, R, sub),
        out_shape=(jax.ShapeDtypeStruct((3, rows, wide), a.dtype),
                   jax.ShapeDtypeStruct(small.shape[1:], small.dtype)),
        in_specs=[pl.BlockSpec(memory_space=pltpu.VMEM)] + [pl.BlockSpec(memory_space=pl.ANY)] * 3,
        out_specs=(pl.BlockSpec(memory_space=pl.ANY), pl.BlockSpec(memory_space=pltpu.VMEM)),
        scratch_shapes=[pltpu.VMEM((K, R >> (level + 1), full, sub), a.dtype) for level in range(L)] + [
            pltpu.VMEM((2, R // 2, full, sub), a.dtype),
            pltpu.VMEM((K, 2, n, rows, sub), a.dtype),
            pltpu.VMEM((n,) + small.shape[1:], small.dtype),
            pltpu.VMEM((R,) + small.shape[1:], small.dtype),
            pltpu.VMEM(small.shape[1:], small.dtype),
            dma((2, R // 2)),
            dma((L, K, R // 2)), dma((L, K, R // 2)),
            dma((K, 2, n)), dma((K, 2, n)),
            dma((K, R, L)), dma((K, R)), dma((K,)),
            dma((n,)), dma((n,)), dma((R,)), dma((R,)), dma(()),
        ],
        compiler_params=pltpu.CompilerParams(collective_id=1, has_side_effects=True, vmem_limit_bytes=60 * 1024 * 1024),
    )(small, a, u, d)


def shifted(value, axis, steps):
    count = lax.axis_size(axis)
    first, last = (max(0, -steps), min(count, count - steps))
    return lax.ppermute(value, axis, [(source, source + steps) for source in range(first, last)])


def gelu_tanh(signal):
    return (
        0.5
        * signal
        * (
            1.0
            + jnp.tanh(math.sqrt(2.0 / math.pi) * (signal + 0.044715 * signal * signal * signal))
        )
    )


def layer_norm(signal, gain, shift):
    center = signal - jnp.mean(signal, axis=-1, keepdims=True)
    spread = jnp.mean(center * center, axis=-1, keepdims=True)
    return center * lax.rsqrt(spread + 1e-06) * gain + shift


def pad_columns(value, wide):
    return jnp.pad(value, ((0, 0), (0, wide - value.shape[1])))


def packed_width(widths, count):
    unit = 128 * count
    return max(-(-width // unit) * unit for width in widths)


def gather_layer(shards, n, R):
    (gain_one, shift_one, weight_qkv, bias_qv, weight_out, bias_out, gain_two, shift_two,
     weight_up, bias_up, weight_down, bias_down) = shards
    model = gain_one.shape[0] * n
    hidden = weight_up.shape[1]
    wide = packed_width((weight_qkv.shape[1] + weight_out.shape[1], hidden), R)
    vector = jnp.concatenate([gain_one, shift_one, bias_qv[0], bias_qv[1], bias_out, gain_two, shift_two, bias_down, bias_up])
    lanes = -(-vector.shape[0] // (16 * 128)) * 128
    small = jnp.pad(vector, (0, 16 * lanes - vector.shape[0])).reshape(16, lanes)
    G, S = gather_weights(n, R, weight_qkv, weight_out, pad_columns(weight_up, wide), pad_columns(weight_down.T, wide), small)
    S = S.reshape(n, -1)
    piece = model // n
    vectors = S[:, : 8 * piece].reshape(n, 8, piece).transpose(1, 0, 2).reshape(8, model)
    up_bias = S[:, 8 * piece : 8 * piece + hidden // n].reshape(hidden)
    return (vectors[0], vectors[1], G[0][:, : 3 * model], vectors[2:4], G[0][:, 3 * model : 4 * model], vectors[4],
            vectors[5], vectors[6], G[1][:, :hidden], up_bias, G[2][:, :hidden].T, vectors[7])


def reduce_layer(grads, n, R):
    (gain_one, shift_one, weight_qkv, bias_qv, weight_out, bias_out, gain_two, shift_two,
     weight_up, bias_up, weight_down, bias_down) = grads
    model = gain_one.shape[0]
    hidden = weight_up.shape[1]
    wide = packed_width((4 * model, hidden), R)
    half = jnp.bfloat16
    a = pad_columns(jnp.concatenate([weight_qkv.astype(half), weight_out.astype(half)], axis=1), wide)
    u = pad_columns(weight_up.astype(half), wide)
    d = pad_columns(weight_down.astype(half), wide)
    piece = model // n
    vectors = jnp.stack([gain_one, shift_one, bias_qv[0], bias_qv[1], bias_out, gain_two, shift_two, bias_down])
    vectors = vectors.reshape(8, n, piece).transpose(1, 0, 2).reshape(n, 8 * piece)
    vectors = jnp.concatenate([vectors, bias_up.reshape(n, hidden // n)], axis=1)
    lanes = -(-vectors.shape[1] // (16 * 128)) * 128
    small = jnp.pad(vectors, ((0, 0), (0, 16 * lanes - vectors.shape[1]))).reshape(n, 16, lanes)
    F, s = reduce_grads(n, R, small, a, u, d)
    s = s.reshape(-1)
    v = s[: 8 * piece].reshape(8, piece)
    F = F.astype(jnp.float32)
    return (v[0], v[1], F[0][:, : 3 * model], v[2:4], F[0][:, 3 * model : 4 * model], v[4], v[5], v[6],
            F[1][:, :hidden], s[8 * piece : 8 * piece + hidden // n], F[2][:, :hidden].T, v[7])


def attention_scores(queries, key_rows):
    raw_scores = jnp.einsum(
        "bqhc,bkhc->bhqk", queries, key_rows, preferred_element_type=jnp.float32
    )
    return raw_scores * HEAD_DIM ** (-0.5)


def layer_forward(inputs, weights):
    (
        gain_one,
        shift_one,
        weight_qkv,
        bias_qv,
        weight_out,
        bias_out,
        gain_two,
        shift_two,
        weight_up,
        bias_up,
        weight_down,
        bias_down,
    ) = weights
    batches, seq_len, model_width = inputs.shape
    normed = layer_norm(inputs, gain_one.astype(jnp.float32), shift_one.astype(jnp.float32)).astype(
        jnp.bfloat16
    )
    joined = jnp.einsum("bsd,de->bse", normed, weight_qkv, preferred_element_type=jnp.float32)
    queries = (joined[..., :model_width] + bias_qv[0].astype(jnp.float32)).astype(jnp.bfloat16)
    key_rows = joined[..., model_width : 2 * model_width].astype(jnp.bfloat16)
    values = (joined[..., 2 * model_width :] + bias_qv[1].astype(jnp.float32)).astype(jnp.bfloat16)
    heads_q = queries.reshape(batches, seq_len, HEADS, HEAD_DIM)
    heads_k = key_rows.reshape(batches, seq_len, HEADS, HEAD_DIM)
    heads_v = values.reshape(batches, seq_len, HEADS, HEAD_DIM)
    scores = attention_scores(heads_q, heads_k)
    row_top = jnp.max(scores, axis=-1, keepdims=True)
    logsum = row_top + jnp.log(jnp.sum(jnp.exp(scores - row_top), axis=-1, keepdims=True))
    attn_probs = jnp.exp(scores - logsum).astype(jnp.bfloat16)
    context = jnp.einsum("bhqk,bkhc->bqhc", attn_probs, heads_v, preferred_element_type=jnp.float32)
    context = context.reshape(batches, seq_len, model_width).astype(jnp.bfloat16)
    attn_out = jnp.einsum(
        "bsd,de->bse", context, weight_out, preferred_element_type=jnp.float32
    ) + bias_out.astype(jnp.float32)
    mixed_rows = inputs + attn_out
    normed_two = layer_norm(
        mixed_rows, gain_two.astype(jnp.float32), shift_two.astype(jnp.float32)
    ).astype(jnp.bfloat16)
    pre_act = jnp.einsum(
        "bsd,df->bsf", normed_two, weight_up, preferred_element_type=jnp.float32
    ) + bias_up.astype(jnp.float32)
    activated = gelu_tanh(pre_act).astype(jnp.bfloat16)
    branch = jnp.einsum(
        "bsf,fd->bsd", activated, weight_down, preferred_element_type=jnp.float32
    ) + bias_down.astype(jnp.float32)
    result = mixed_rows + branch
    saved_acts = (
        inputs,
        normed,
        queries,
        key_rows,
        values,
        logsum,
        context,
        mixed_rows,
        normed_two,
        pre_act,
        activated,
    )
    return (result, saved_acts)


def layer_backward(grad_out, saved_acts, weights):
    (
        gain_one,
        shift_one,
        weight_qkv,
        bias_qv,
        weight_out,
        bias_out,
        gain_two,
        shift_two,
        weight_up,
        bias_up,
        weight_down,
        bias_down,
    ) = weights
    (
        inputs,
        normed,
        queries,
        key_rows,
        values,
        logsum,
        context,
        mixed_rows,
        normed_two,
        pre_act,
        activated,
    ) = saved_acts
    batches, seq_len, model_width = inputs.shape
    sum_axes = (0, 1)
    grad_branch = grad_out.astype(jnp.bfloat16)
    g_down_weight = jnp.einsum(
        "bsd,bsf->df", grad_branch, activated, preferred_element_type=jnp.float32
    )
    g_down_bias = jnp.sum(grad_branch.astype(jnp.float32), axis=sum_axes)
    grad_act = jnp.einsum(
        "bsd,fd->bsf", grad_branch, weight_down, preferred_element_type=jnp.float32
    )
    gelu_pull = jax.vjp(gelu_tanh, pre_act)[1]
    grad_pre = gelu_pull(grad_act)[0].astype(jnp.bfloat16)
    g_up_weight = jnp.einsum(
        "bsd,bsf->df", normed_two, grad_pre, preferred_element_type=jnp.float32
    )
    g_up_bias = jnp.sum(grad_pre.astype(jnp.float32), axis=sum_axes)
    grad_normed_two = jnp.einsum(
        "bsf,df->bsd", grad_pre, weight_up, preferred_element_type=jnp.float32
    )
    norm_pull = jax.vjp(
        layer_norm, mixed_rows, gain_two.astype(jnp.float32), shift_two.astype(jnp.float32)
    )[1]
    grad_mix_part, g_second_gain, g_second_shift = norm_pull(grad_normed_two)
    grad_mixed = grad_out + grad_mix_part
    grad_attn = grad_mixed.astype(jnp.bfloat16)
    g_out_weight = jnp.einsum("bsd,bse->de", context, grad_attn, preferred_element_type=jnp.float32)
    g_out_bias = jnp.sum(grad_attn.astype(jnp.float32), axis=sum_axes)
    grad_context = jnp.einsum(
        "bse,de->bsd", grad_attn, weight_out, preferred_element_type=jnp.float32
    ).astype(jnp.bfloat16)
    heads_q = queries.reshape(batches, seq_len, HEADS, HEAD_DIM)
    heads_k = key_rows.reshape(batches, seq_len, HEADS, HEAD_DIM)
    heads_v = values.reshape(batches, seq_len, HEADS, HEAD_DIM)
    grad_heads = grad_context.reshape(batches, seq_len, HEADS, HEAD_DIM)
    probs_full = jnp.exp(attention_scores(heads_q, heads_k) - logsum)
    probs_low = probs_full.astype(jnp.bfloat16)
    grad_probs = jnp.einsum(
        "bqhc,bkhc->bhqk", grad_heads, heads_v, preferred_element_type=jnp.float32
    )
    grad_values = jnp.einsum(
        "bhqk,bqhc->bkhc", probs_low, grad_heads, preferred_element_type=jnp.float32
    )
    row_total = jnp.sum(probs_full * grad_probs, axis=-1, keepdims=True)
    grad_scores = (probs_full * (grad_probs - row_total)).astype(jnp.bfloat16)
    score_scale = HEAD_DIM ** (-0.5)
    grad_queries = (
        jnp.einsum("bhqk,bkhc->bqhc", grad_scores, heads_k, preferred_element_type=jnp.float32)
        * score_scale
    )
    grad_keys = (
        jnp.einsum("bhqk,bqhc->bkhc", grad_scores, heads_q, preferred_element_type=jnp.float32)
        * score_scale
    )
    grad_joined = jnp.concatenate(
        [
            grad_queries.reshape(batches, seq_len, model_width),
            grad_keys.reshape(batches, seq_len, model_width),
            grad_values.reshape(batches, seq_len, model_width),
        ],
        axis=-1,
    ).astype(jnp.bfloat16)
    joined_wide = grad_joined.astype(jnp.float32)
    g_qv_bias = jnp.stack(
        [
            jnp.sum(joined_wide[..., :model_width], axis=sum_axes),
            jnp.sum(joined_wide[..., 2 * model_width :], axis=sum_axes),
        ]
    )
    g_qkv_weight = jnp.einsum(
        "bsd,bse->de", normed, grad_joined, preferred_element_type=jnp.float32
    )
    grad_normed = jnp.einsum(
        "bse,de->bsd", grad_joined, weight_qkv, preferred_element_type=jnp.float32
    )
    first_pull = jax.vjp(
        layer_norm, inputs, gain_one.astype(jnp.float32), shift_one.astype(jnp.float32)
    )[1]
    grad_in_part, g_first_gain, g_first_shift = first_pull(grad_normed)
    grad_inputs = grad_mixed + grad_in_part
    grads = (
        g_first_gain,
        g_first_shift,
        g_qkv_weight,
        g_qv_bias,
        g_out_weight,
        g_out_bias,
        g_second_gain,
        g_second_shift,
        g_up_weight,
        g_up_bias,
        g_down_weight,
        g_down_bias,
    )
    return (grad_inputs, grads)


def on_device(
    ends,
    first_gain,
    first_shift,
    qkv_weight,
    qv_bias,
    out_weight,
    out_bias,
    second_gain,
    second_shift,
    up_weight,
    up_bias,
    down_weight,
    down_bias,
):
    shards = tuple(
        (
            item[0]
            for item in (
                first_gain,
                first_shift,
                qkv_weight,
                qv_bias,
                out_weight,
                out_bias,
                second_gain,
                second_shift,
                up_weight,
                up_bias,
                down_weight,
                down_bias,
            )
        )
    )
    section_idx = lax.axis_index("section")
    at_first = section_idx == 0
    boundary = ends[0].astype(jnp.float32)
    images = boundary.shape[0]
    per_micro = images // MICRO
    pieces = [
        boundary[micro_index * per_micro : (micro_index + 1) * per_micro]
        for micro_index in range(MICRO)
    ]
    n, R = lax.axis_size("fsdp"), lax.axis_size("replica")
    weights = gather_layer(shards, n, R)
    received = jnp.zeros_like(pieces[0])
    saved_steps = []
    outputs = []
    for moment in range(MICRO + 1):
        source = pieces[min(moment, MICRO - 1)]
        inputs = jnp.where(at_first, source, received)
        result, saved_acts = layer_forward(inputs, weights)
        saved_steps.append(saved_acts)
        outputs.append(result)
        if moment < MICRO:
            received = shifted(result.astype(jnp.bfloat16), "section", 1).astype(jnp.float32)
    stacked = tuple((jnp.stack(items) for items in zip(*saved_steps)))
    back_received = jnp.zeros_like(pieces[0])
    totals = None
    in_grads = []
    for moment in range(MICRO + 1):
        slot_index = jnp.clip(moment - 1 + 2 * section_idx, 0, MICRO)
        saved_acts = tuple(
            (lax.dynamic_index_in_dim(item, slot_index, 0, keepdims=False) for item in stacked)
        )
        micro_index = moment - 1 + section_idx
        live_mask = ((micro_index >= 0) & (micro_index < MICRO)).astype(jnp.float32)
        grad_out = jnp.where(at_first, back_received, pieces[min(moment, MICRO - 1)]) * live_mask
        grad_inputs, grads = layer_backward(grad_out, saved_acts, weights)
        in_grads.append(grad_inputs)
        if moment < MICRO:
            back_received = shifted(grad_inputs.astype(jnp.bfloat16), "section", -1).astype(
                jnp.float32
            )
        totals = (
            grads if totals is None else tuple((left + right for left, right in zip(totals, grads)))
        )
    summed = reduce_layer(totals, n, R)
    grad_rows = jnp.concatenate(in_grads[1:], axis=0)
    out_rows = jnp.concatenate(outputs[1:], axis=0)
    result_ends = jnp.where(at_first, grad_rows, out_rows)[None]
    (
        g_first_gain,
        g_first_shift,
        g_qkv_weight,
        g_qv_bias,
        g_out_weight,
        g_out_bias,
        g_second_gain,
        g_second_shift,
        g_up_weight,
        g_up_bias,
        g_down_weight,
        g_down_bias,
    ) = summed
    return (
        result_ends,
        g_first_gain[None],
        g_first_shift[None],
        g_qkv_weight[None],
        g_qv_bias[None],
        g_out_weight[None],
        g_out_bias[None],
        g_second_gain[None],
        g_second_shift[None],
        g_up_weight[None],
        g_up_bias[None],
        g_down_weight[None],
        g_down_bias[None],
    )


def solution(mesh):
    placed = (
        P("section", ("fsdp", "replica"), None, None),
        P("section", "fsdp"),
        P("section", "fsdp"),
        P("section", "fsdp", None),
        P("section", None, "fsdp"),
        P("section", "fsdp", None),
        P("section", "fsdp"),
        P("section", "fsdp"),
        P("section", "fsdp"),
        P("section", "fsdp", None),
        P("section", "fsdp"),
        P("section", None, "fsdp"),
        P("section", "fsdp"),
    )
    return jax.shard_map(
        on_device,
        mesh=mesh,
        in_specs=placed,
        out_specs=(
            P("section", ("fsdp", "replica"), None, None),
            P("section", "fsdp"),
            P("section", "fsdp"),
            P("section", "fsdp", None),
            P("section", None, "fsdp"),
            P("section", "fsdp", None),
            P("section", "fsdp"),
            P("section", "fsdp"),
            P("section", "fsdp"),
            P("section", "fsdp", None),
            P("section", "fsdp"),
            P("section", None, "fsdp"),
            P("section", "fsdp"),
        ),
        check_vma=False,
    )
```

```python
import functools
import math

import jax
import jax.numpy as jnp
from jax import lax
from jax.experimental import pallas as pl
from jax.experimental.pallas import tpu as pltpu
from jax.sharding import PartitionSpec as P

MESH = pl.DeviceIdType.MESH
HEADS = 16
HEAD_DIM = 72
MICRO = 3
F32 = jnp.float32
HALF = jnp.bfloat16
EPS = 1e-06
ANY = pl.BlockSpec(memory_space=pl.ANY)
NN = (((1,), (0,)), ((), ()))
NT = (((1,), (1,)), ((), ()))
TN = (((0,), (0,)), ((), ()))


def mul(left, right, dims=NN):
    return lax.dot_general(left, right, dims, preferred_element_type=F32)


def row_loop(count, step, body):
    def run(i, carry):
        body(pl.ds(pl.multiple_of(i * step, step), step))
        return carry
    lax.fori_loop(0, count // step, run, 0)


def normal(value):
    center = value - jnp.mean(value, axis=-1, keepdims=True)
    scale = lax.rsqrt(jnp.mean(center * center, axis=-1, keepdims=True) + EPS)
    return center * scale, scale


def fold(value):
    return value.reshape(value.shape[0] // 8, 8, value.shape[1]).sum(axis=0)


def norm_back(value, grad, gain):
    hat, scale = normal(value)
    d = grad * gain
    low = d - jnp.mean(d, axis=-1, keepdims=True) - hat * jnp.mean(d * hat, axis=-1, keepdims=True)
    return low * scale, hat


def params(limit=56, **kw):
    return pltpu.CompilerParams(vmem_limit_bytes=limit * 1024 * 1024, **kw)


def shape(rows, columns, dtype):
    return jax.ShapeDtypeStruct((rows, columns), dtype)


def spans(h):
    a, b = h * HEAD_DIM, (h + 1) * HEAD_DIM
    lo = a // 128 * 128
    hi = -(-b // 128) * 128
    return a, b, lo, hi

def head_mask(h, rows):
    a, b, lo, hi = spans(h)
    lane = lax.broadcasted_iota(jnp.int32, (rows, hi - lo), 1) + lo
    return (lane >= a) & (lane < b)

def attn_image(qkv, P, c, D, tok, factor):
    for h in range(HEADS):
        a, b, lo, hi = spans(h)
        mask = head_mask(h, tok)
        q = jnp.where(mask, qkv[:, lo:hi], 0)
        k = qkv[:, D + lo:D + hi]
        v = qkv[:, 2 * D + lo:2 * D + hi]
        s = mul(k, q, NT)
        e = jnp.exp2((s - jnp.max(s, axis=0, keepdims=True)) * factor)
        p = (e * (1.0 / jnp.sum(e, axis=0, keepdims=True))).astype(HALF)
        P[h] = p
        o = mul(p, v, TN).astype(HALF)
        if a > lo:
            c[:, lo:hi] = jnp.where(mask, o, c[:, lo:hi])
        else:
            c[:, lo:hi] = o

def attn_back_image(qkv, P, dc, out, D, tok, factor):
    for h in range(HEADS):
        a, b, lo, hi = spans(h)
        mask = head_mask(h, tok)
        q = qkv[:, lo:hi]
        k = qkv[:, D + lo:D + hi]
        v = qkv[:, 2 * D + lo:2 * D + hi]
        d = dc[:, lo:hi]
        p = P[h]
        dv = mul(p, d).astype(HALF)
        wide = p.astype(F32)
        dp = mul(v, jnp.where(mask, d, 0), NT)
        ds = (wide * (dp - jnp.sum(wide * dp, axis=0, keepdims=True))).astype(HALF)
        dk = (mul(ds, q) * factor).astype(HALF)
        dq = (mul(ds, k, TN) * factor).astype(HALF)
        for base, value in ((0, dq), (D, dk), (2 * D, dv)):
            if a > lo:
                out[:, base + lo:base + hi] = jnp.where(mask, value, out[:, base + lo:base + hi])
            else:
                out[:, base + lo:base + hi] = value


TILE = 512
LANES = 256


def pieces(width, step):
    return [(a, min(step, width - a)) for a in range(0, width, step)]


def tiles(width, step, body):
    whole = width // step
    def run(i, carry):
        body(pl.multiple_of(i * step, step), step)
        return carry
    lax.fori_loop(0, whole, run, 0)
    if width % step:
        body(whole * step, width % step)


def f_layer(slots, total, wide, x, vec, qb, ub, G, tok, kept):
    T, D = x.shape
    hidden = ub.shape[1]
    images = T // tok
    factor = HEAD_DIM ** (-0.5) * math.log2(math.e)
    root = math.sqrt(2.0 / math.pi)
    cut = pieces(4 * D, 768)
    plain, spare = 5, sum(b is not None for b in kept)
    chunk = T // 2 if T % 32 == 0 else T

    def kernel(slot, *refs):
        @pl.when(slot[1] == 1)
        def _():
            work(slot, *refs)

    def work(slot, *refs):
        x, vec, qb, ub, G = refs[:plain]
        (n1o, qkvo, Po, co, r1o, n2o, go, gpo, reso, y,
         wa, wb, n1, qkv, P, c, r1, n2, g, gp, res, wsem, psem, gsem, osem) = refs[plain + spare:]
        save = pl.ds(pl.multiple_of(slot[0] * T, 16), T)

        def weight(j):
            a, w = cut[j]
            return pltpu.make_async_copy(G.at[0, :, pl.ds(a, w)], wa.at[:, pl.ds(a, w)], wsem.at[j])
        up = pltpu.make_async_copy(G.at[1, :, pl.ds(0, hidden)], wb, wsem.at[len(cut)])
        down = pltpu.make_async_copy(G.at[2, :, pl.ds(0, hidden)], wa.at[:, pl.ds(0, hidden)], wsem.at[len(cut) + 1])
        for j in range(len(cut)):
            weight(j).start()
        up.start()

        def out(source, target, at, k):
            return pltpu.make_async_copy(source, target.at[at], osem.at[k])
        outs = [out(n1, n1o, save, 0), out(qkv, qkvo, save, 1), out(c, co, save, 2), out(r1, r1o, save, 3),
                out(n2, n2o, save, 4), out(g, go, (save, pl.ds(0, hidden)), 5), out(res, reso, save, 6)]

        def first(at):
            n1[at, :] = (normal(x[at, :].astype(F32))[0] * vec[0:1, :] + vec[1:2, :]).astype(HALF)
        row_loop(T, tok, first)
        outs[0].start()
        for j, (a, w) in enumerate(cut):
            weight(j).wait()
            if a < 3 * D:
                b = min(a + w, 3 * D)
                qkv[:, a:b] = (mul(n1[...], wa[:, a:b]) + qb[:, a:b]).astype(HALF)
        outs[1].start()

        def probs(i):
            return pltpu.make_async_copy(P.at[i % 2], Po.at[slot[0] * images + i], psem.at[i % 2])

        def image(i, carry):
            @pl.when(i >= 2)
            def _():
                probs(i - 2).wait()
            rows = pl.ds(pl.multiple_of(i * tok, 16), tok)
            attn_image(qkv.at[rows], P.at[i % 2], c.at[rows], D, tok, factor)
            probs(i).start()
            return carry
        lax.fori_loop(0, images, image, 0)
        outs[2].start()
        r1[...] = mul(c[...], wa[:, 3 * D:4 * D])
        down.start()

        def second(at):
            value = r1[at, :] + vec[4:5, :] + x[at, :].astype(F32)
            r1[at, :] = value
            n2[at, :] = (normal(value)[0] * vec[5:6, :] + vec[6:7, :]).astype(HALF)
        row_loop(T, tok, second)
        outs[3].start()
        outs[4].start()
        up.wait()

        def slope(i, size):
            return pltpu.make_async_copy(
                gp.at[lax.rem(i, 2), :, pl.ds(0, size)], gpo.at[save, pl.ds(pl.multiple_of(i * TILE, 128), size)],
                gsem.at[lax.rem(i, 2)])

        def rise(start, size):
            i = start // TILE
            @pl.when(i >= 2)
            def _():
                slope(i - 2, TILE).wait()
            at = pl.ds(start, size)
            for a in range(0, T, chunk):
                u = mul(n2[a:a + chunk, :], wb[:, at]) + ub[:, at]
                square = u * u
                t = jnp.tanh(u * (root + (root * 0.044715) * square))
                half = 0.5 + 0.5 * t
                g[a:a + chunk, at] = (u * half).astype(HALF)
                gp[lax.rem(i, 2), a:a + chunk, 0:size] = (
                    half + (0.5 * u) * (1.0 - t * t) * (root + (3.0 * root * 0.044715) * square)).astype(HALF)
            slope(i, size).start()
        tiles(hidden, TILE, rise)
        outs[5].start()
        down.wait()
        for a, w in pieces(D, LANES):
            at = slice(a, a + w)
            value = mul(g[...], wa[a:a + w, 0:hidden], NT) + (r1[:, at] + vec[7:8, at])
            res[:, at] = value
            y[:, at] = value.astype(HALF)
        outs[6].start()
        for copy in outs:
            copy.wait()
        for i in range(max(0, images - 2), images):
            probs(i).wait()
        count = -(-hidden // TILE)
        for i in range(max(0, count - 2), count):
            slope(i, min(TILE, hidden - i * TILE)).wait()

    aliases = {}
    ins = [x, vec, qb, ub, G]
    for index, buffer in enumerate(kept):
        if buffer is not None:
            aliases[1 + len(ins)] = index
            ins.append(buffer)
    dma = pltpu.SemaphoreType.DMA
    whole = pl.BlockSpec(memory_space=pltpu.VMEM)
    return pl.pallas_call(
        kernel,
        out_shape=(shape(total, D, HALF), shape(total, 3 * D, HALF),
                   jax.ShapeDtypeStruct((total // tok, HEADS, tok, tok), HALF), shape(total, D, HALF), shape(total, D, F32),
                   shape(total, D, HALF), shape(total, wide, HALF), shape(total, hidden, HALF), shape(total, D, F32),
                   shape(T, D, HALF)),
        grid_spec=pltpu.PrefetchScalarGridSpec(
            num_scalar_prefetch=1, grid=(1,), in_specs=[whole] * 4 + [ANY] * (1 + spare), out_specs=(ANY,) * 9 + (whole,),
            scratch_shapes=[
                pltpu.VMEM((D, 4 * D), HALF), pltpu.VMEM((D, hidden), HALF), pltpu.VMEM((T, D), HALF),
                pltpu.VMEM((T, 3 * D), HALF), pltpu.VMEM((2, HEADS, tok, tok), HALF), pltpu.VMEM((T, D), HALF),
                pltpu.VMEM((T, D), F32), pltpu.VMEM((T, D), HALF), pltpu.VMEM((T, hidden), HALF),
                pltpu.VMEM((2, T, TILE), HALF), pltpu.VMEM((T, D), F32),
                dma((len(cut) + 2,)), dma((2,)), dma((2,)), dma((7,))]),
        input_output_aliases=aliases,
        compiler_params=params(60),
        cost_estimate=pl.CostEstimate(flops=T * D, bytes_accessed=T * D, transcendentals=0),
    )(slots, *ins)


def d_layer(slots, total, wide, final, e, x, vec, G, GP, R1, QKV, PP, tok, kept):
    T, D = x.shape
    hidden = GP.shape[1]
    images = T // tok
    scale = HEAD_DIM ** (-0.5)
    plain, spare = 8, sum(b is not None for b in kept)
    chunk = T // 2 if T % 32 == 0 else T

    def kernel(slot, *refs):
        @pl.when(slot[1] == 1)
        def _():
            work(slot, *refs)

    def work(slot, *refs):
        e, x, vec, G, GP, R1, QKV, PP = refs[:plain]
        (duo, lowo, dqkvo, reso, dx, stats, sums,
         wa, wb, gp, r1, qkv, P, du, grad, dr1, low, dc, dqkv, wsem, psem, isem, osem) = refs[plain + spare:]
        save = pl.ds(pl.multiple_of(slot[0] * T, 16), T)
        cuts = pieces(hidden, 2 * TILE)
        down = [pltpu.make_async_copy(G.at[2, :, pl.ds(a, w)], wa.at[:, pl.ds(a, w)], wsem.at[2 + j]) for j, (a, w) in enumerate(cuts)]
        slope = [pltpu.make_async_copy(GP.at[save, pl.ds(a, w)], gp.at[:, pl.ds(a, w)], isem.at[2 + j]) for j, (a, w) in enumerate(cuts)]
        up = pltpu.make_async_copy(G.at[1, :, pl.ds(0, hidden)], wb, wsem.at[0])
        rest = pltpu.make_async_copy(G.at[0, :, pl.ds(0, 4 * D)], wa, wsem.at[1])
        loads = [pltpu.make_async_copy(R1.at[save], r1, isem.at[0]), pltpu.make_async_copy(QKV.at[save], qkv, isem.at[1])]
        for weight, factor in zip(down, slope):
            weight.start()
            factor.start()
        up.start()
        for copy in loads:
            copy.start()

        def out(source, target, at, k):
            return pltpu.make_async_copy(source, target.at[at], osem.at[k])
        outs = [out(du, duo, (save, pl.ds(0, hidden)), 0), out(low, lowo, save, 1), out(dqkv, dqkvo, save, 2)]
        if final:
            outs.append(out(dr1, reso, save, 3))

        def probs(i):
            return pltpu.make_async_copy(PP.at[slot[0] * images + i], P.at[i % 2], psem.at[i % 2])
        for i in range(min(2, images)):
            probs(i).start()
        stats[...] = jnp.zeros_like(stats)

        def fall(start, size):
            at = pl.ds(start, size)
            total = None
            for a in range(0, T, chunk):
                d = (mul(e[a:a + chunk, :], wa[:, at]) * gp[a:a + chunk, at].astype(F32)).astype(HALF)
                du[a:a + chunk, at] = d
                part = jnp.sum(d.astype(F32), axis=0, keepdims=True)
                total = part if total is None else total + part
            sums[:, at] = total
        for j, (a, w) in enumerate(cuts):
            down[j].wait()
            slope[j].wait()
            for b in range(a, a + w, TILE):
                fall(b, min(TILE, a + w - b))
        rest.start()
        outs[0].start()
        up.wait()
        for a, w in pieces(D, LANES):
            grad[:, a:a + w] = mul(du[...], wb[a:a + w, :], NT)
        loads[0].wait()

        def second(at):
            g = grad[at, :]
            part, hat = norm_back(r1[at, :], g, vec[5:6, :])
            eb = e[at, :].astype(F32)
            value = eb + part
            rounded = value.astype(HALF)
            dr1[at, :] = value
            low[at, :] = rounded
            stats[0] += fold(g * hat)
            stats[1] += fold(g)
            stats[2] += fold(rounded.astype(F32))
            stats[3] += fold(eb)
        row_loop(T, tok, second)
        outs[1].start()
        rest.wait()
        for a, w in pieces(D, LANES):
            dc[:, a:a + w] = mul(low[...], wa[a:a + w, 3 * D:4 * D], NT).astype(HALF)
        loads[1].wait()

        def image(i, carry):
            probs(i).wait()
            rows = pl.ds(pl.multiple_of(i * tok, 16), tok)
            attn_back_image(qkv.at[rows], P.at[i % 2], dc.at[rows], dqkv.at[rows], D, tok, scale)
            @pl.when(i + 2 < images)
            def _():
                probs(i + 2).start()
            return carry
        lax.fori_loop(0, images, image, 0)
        outs[2].start()
        for a, w in pieces(D, LANES):
            grad[:, a:a + w] = mul(dqkv[...], wa[a:a + w, 0:3 * D], NT)

        def first(at):
            g = grad[at, :]
            part, hat = norm_back(x[at, :].astype(F32), g, vec[0:1, :])
            value = dr1[at, :] + part
            dr1[at, :] = value
            dx[at, :] = value.astype(HALF)
            stats[4] += fold(g * hat)
            stats[5] += fold(g)
            stats[6] += fold(dqkv[at, 0:D].astype(F32))
            stats[7] += fold(dqkv[at, 2 * D:3 * D].astype(F32))
        row_loop(T, tok, first)
        if final:
            outs[3].start()
        for copy in outs:
            copy.wait()

    aliases = {}
    ins = [e, x, vec, G, GP, R1, QKV, PP]
    for index, buffer in enumerate(kept):
        if buffer is not None:
            aliases[1 + len(ins)] = index
            ins.append(buffer)
    dma = pltpu.SemaphoreType.DMA
    whole = pl.BlockSpec(memory_space=pltpu.VMEM)
    return pl.pallas_call(
        kernel,
        out_shape=(shape(total, wide, HALF), shape(total, D, HALF), shape(total, 3 * D, HALF), shape(total, D, F32),
                   shape(T, D, HALF), jax.ShapeDtypeStruct((8, 8, D), F32), shape(1, hidden, F32)),
        grid_spec=pltpu.PrefetchScalarGridSpec(
            num_scalar_prefetch=1, grid=(1,), in_specs=[whole] * 3 + [ANY] * (5 + spare), out_specs=(ANY,) * 4 + (whole,) * 3,
            scratch_shapes=[
                pltpu.VMEM((D, 4 * D), HALF), pltpu.VMEM((D, hidden), HALF), pltpu.VMEM((T, hidden), HALF),
                pltpu.VMEM((T, D), F32), pltpu.VMEM((T, 3 * D), HALF), pltpu.VMEM((2, HEADS, tok, tok), HALF),
                pltpu.VMEM((T, hidden), HALF), pltpu.VMEM((T, D), F32), pltpu.VMEM((T, D), F32), pltpu.VMEM((T, D), HALF),
                pltpu.VMEM((T, D), HALF), pltpu.VMEM((T, 3 * D), HALF),
                dma((2 + len(pieces(hidden, 2 * TILE)),)), dma((2,)), dma((2 + len(pieces(hidden, 2 * TILE)),)), dma((4,))]),
        input_output_aliases=aliases,
        compiler_params=params(60),
        cost_estimate=pl.CostEstimate(flops=T * D, bytes_accessed=T * D, transcendentals=0),
    )(slots, *ins)


def powers(count):
    bits = []
    bit = count // 2
    while bit:
        bits.append(bit)
        bit //= 2
    return bits

def gather_kernel(n, R, qkv, out, up, down, small, G, S, stage, stage_small, lsem, ssem, rsem, small_send, small_recv):
    z = lax.axis_index("fsdp")
    r = lax.axis_index("replica")
    rows, wide = up.shape
    part = wide // R
    bits = powers(R)
    barrier = pltpu.get_barrier_semaphore()
    for hop in range(1, n):
        pl.semaphore_signal(barrier, inc=1, device_id={"fsdp": lax.rem(z + hop, n)}, device_id_type=MESH)
    for bit in bits:
        pl.semaphore_signal(barrier, inc=1, device_id={"replica": r ^ bit}, device_id_type=MESH)
    mine = pl.ds(pl.multiple_of(z * rows, 16), rows)
    first = qkv.shape[1]
    local = [
        pltpu.make_async_copy(qkv, stage.at[0, :, pl.ds(0, first)], lsem.at[0]),
        pltpu.make_async_copy(out, stage.at[0, :, pl.ds(first, out.shape[1])], lsem.at[1]),
        pltpu.make_async_copy(up, stage.at[1], lsem.at[2]),
        pltpu.make_async_copy(down, stage.at[2], lsem.at[3]),
        pltpu.make_async_copy(small, stage_small, lsem.at[4]),
    ]
    for copy in local:
        copy.start()
    keep = [pltpu.make_async_copy(stage.at[group], G.at[group, mine], lsem.at[5 + group]) for group in range(3)]
    keep.append(pltpu.make_async_copy(stage_small, S.at[z], lsem.at[8]))
    pl.semaphore_wait(barrier, n - 1 + len(bits))

    def piece(group, source, column):
        return G.at[group, pl.ds(pl.multiple_of(source * rows, 16), rows),
                    pl.ds(pl.multiple_of(column * part, 128), part)]

    def send(group, source, column, kind, target, origin=None):
        return pltpu.make_async_remote_copy(
            src_ref=piece(group, source, column) if origin is None else origin, dst_ref=piece(group, source, column),
            send_sem=ssem.at[group, source, column, kind], recv_sem=rsem.at[group, source, column],
            device_id=target, device_id_type=MESH)

    def to_right(group, source, origin=None):
        return send(group, source, r, 0, {"fsdp": z + 1}, origin)

    def to_left(group, source, origin=None):
        return send(group, source, r, 1, {"fsdp": z - 1}, origin)

    def own(group):
        return stage.at[group, :, pl.ds(pl.multiple_of(r * part, 128), part)]

    def share(group, source, column, level):
        return send(group, source, column, 2 + level, {"replica": r ^ bits[level]})

    def arrived(group, source, column):
        send(group, source, column, 0, {"replica": r ^ bits[0]}).wait_recv()

    def small_to(hop):
        return pltpu.make_async_remote_copy(
            src_ref=small, dst_ref=S.at[z], send_sem=small_send.at[hop],
            recv_sem=small_recv.at[z], device_id={"fsdp": lax.rem(z + hop, n)}, device_id_type=MESH)
    for hop in range(1, n):
        small_to(hop).start()
    for group in range(3):
        if group == 0:
            local[0].wait()
            local[1].wait()
        else:
            local[1 + group].wait()
        @pl.when(z + 1 < n)
        def _():
            to_right(group, z, own(group)).start()
        @pl.when(z > 0)
        def _():
            to_left(group, z, own(group)).start()
        keep[group].start()
    local[4].wait()
    keep[3].start()
    columns = {}
    for level, bit in enumerate(bits):
        masks = [0]
        for upper in bits[:level]:
            masks = masks + [m | upper for m in masks]
        columns[level] = [bit | m for m in masks]
    steps = [(hop, group) for hop in range(1, n) for group in range(3)]
    for turn in range(len(steps) + len(bits)):
        for level in range(-1, len(bits)):
            place = turn - 1 - level
            if place < 0 or place >= len(steps):
                continue
            hop, group = steps[place]
            for sign in (-1, 1):
                source = z + sign * hop
                @pl.when((source >= 0) & (source < n))
                def _():
                    if level < 0:
                        arrived(group, source, r)
                        for lower in range(len(bits)):
                            share(group, source, r, lower).start()
                        if sign < 0:
                            @pl.when(z + 1 < n)
                            def _():
                                to_right(group, source).start()
                        else:
                            @pl.when(z > 0)
                            def _():
                                to_left(group, source).start()
                    else:
                        for mask in columns[level]:
                            arrived(group, source, r ^ mask)
                            for lower in range(level + 1, len(bits)):
                                share(group, source, r ^ mask, lower).start()
    for copy in keep:
        copy.wait()
    for hop in range(1, n):
        pltpu.make_async_remote_copy(
            src_ref=small, dst_ref=S.at[lax.rem(z + hop, n)], send_sem=small_send.at[hop],
            recv_sem=small_recv.at[lax.rem(z + hop, n)], device_id={"fsdp": lax.rem(z + hop, n)}, device_id_type=MESH).wait_recv()
        small_to(hop).wait_send()
    for group in range(3):
        for source in range(n):
            @pl.when((source <= z) & (z + 1 < n))
            def _():
                to_right(group, source).wait_send()
            @pl.when((source >= z) & (z > 0))
            def _():
                to_left(group, source).wait_send()
            @pl.when(source != z)
            def _():
                for level in range(len(bits)):
                    share(group, source, r, level).wait_send()
                for level in range(len(bits)):
                    for mask in columns[level]:
                        for lower in range(level + 1, len(bits)):
                            share(group, source, r ^ mask, lower).wait_send()

def gather_weights(n, R, qkv, out, up, down, small):
    rows, wide = up.shape
    kinds = 2 + len(powers(R))
    return pl.pallas_call(
        functools.partial(gather_kernel, n, R),
        out_shape=(jax.ShapeDtypeStruct((3, n * rows, wide), qkv.dtype),
                   jax.ShapeDtypeStruct((n,) + small.shape, small.dtype)),
        in_specs=[pl.BlockSpec(memory_space=pl.ANY)] * 5,
        out_specs=(pl.BlockSpec(memory_space=pl.ANY),) * 2,
        scratch_shapes=[
            pltpu.VMEM((3, rows, wide), qkv.dtype),
            pltpu.VMEM(small.shape, small.dtype),
            pltpu.SemaphoreType.DMA((9,)),
            pltpu.SemaphoreType.DMA((3, n, R, kinds)),
            pltpu.SemaphoreType.DMA((3, n, R)),
            pltpu.SemaphoreType.DMA((n,)),
            pltpu.SemaphoreType.DMA((n,)),
        ],
        compiler_params=pltpu.CompilerParams(collective_id=0, has_side_effects=True, vmem_limit_bytes=32 * 1024 * 1024),
    )(qkv, out, up, down, small)


ORDER = (2, 1, 0)


def plan(R, part, D):
    found = []
    for place in range(3):
        edges = (3 * D, 4 * D) if ORDER[place] == 0 else ()
        sizes, at = [], 0
        while at < part:
            size = min(max(12 // R, 1) * 128, part - at)
            while any(p * part + at < edge < p * part + at + size for p in range(R) for edge in edges):
                size -= 128
            sizes.append(size)
            at += size
        if place == 0 and sizes[0] == 384:
            sizes[:1] = [128, 256]
        if place == 2 and sizes[-1] > 128:
            sizes[-1:] = [sizes[-1] - 128, 128]
        at = 0
        for size in sizes:
            found.append((place, at, size))
            at += size
    return found


def ahead_of_pairs(k, L):
    return L >= 2 and k % 3 == 2


def places(chunks, L):
    every, kind, counts = [], [], [0, 0, 0]
    for k, (_, _, size) in enumerate(chunks):
        which = int(ahead_of_pairs(k, L))
        every.append(counts[2])
        kind.append(counts[which])
        counts[which] += size
        counts[2] += size
    return every, kind, counts


def reduce_kernel(n, R, chunks, small_in, n1, c, n2, eb, dqkv, low, du, g, F, small_out, *scratch):
    L = R.bit_length() - 1
    bits = [1 << level for level in range(L)]
    held = scratch[:L]
    (X, left, stage, right, flow, flow_two, pair, small_z, small_r, small_sum, rsem, lsem, send_sem, recv_sem, zsend, zrecv,
     psend, precv, fsend, frecv, fkeep, ss_z, sr_z, ss_r, sr_r, ss_l) = scratch[L:]
    z = lax.axis_index("fsdp")
    r = lax.axis_index("replica")
    tokens, D = n1.shape
    full = D
    rows = full // n
    wide = F.shape[2]
    part = wide // R
    K = len(chunks)
    every, kind, _ = places(chunks, L)
    barrier = pltpu.get_barrier_semaphore()
    for hop in range(1, n):
        pl.semaphore_signal(barrier, inc=1, device_id={"fsdp": lax.rem(z + hop, n)}, device_id_type=MESH)
    for hop in range(1, R):
        pl.semaphore_signal(barrier, inc=1, device_id={"replica": lax.rem(r + hop, R)}, device_id_type=MESH)

    def group(k):
        return ORDER[chunks[k][0]]

    def columns(k, p):
        return pl.ds(pl.multiple_of(p * part + chunks[k][1], 128), chunks[k][2])

    def part_lanes(k, p):
        return pl.ds(pl.multiple_of(p * chunks[k][2], 128), chunks[k][2])

    def block(t):
        return pl.ds(pl.multiple_of(t * rows, 16), rows)

    def kept(level, j):
        return (r & ((2 << level) - 1)) | (j << (level + 1))

    def factors(k, p):
        a, sub = p * part + chunks[k][1], chunks[k][2]
        if group(k) == 2:
            return 0, g.at[:, pl.ds(a, sub)]
        if group(k) == 1:
            return 1, du.at[:, pl.ds(a, sub)]
        if a < 3 * D:
            return 0, dqkv.at[:, pl.ds(a, sub)]
        if a < 4 * D:
            return 1, low.at[:, pl.ds(a - 3 * D, sub)]
        return None, None

    def fetch(k, p):
        return pltpu.make_async_copy(factors(k, p)[1], right.at[:, pl.ds(p * chunks[k][2], chunks[k][2])], rsem.at[p])

    def fetch_all(k):
        for p in range(R):
            if factors(k, p)[1] is not None:
                fetch(k, p).start()

    def fetch_left(which):
        return pltpu.make_async_copy((eb, n2, n1, c)[which], stage, lsem)

    def turn_left(which):
        fetch_left(which).wait()
        for a in range(0, D, 128):
            left[which % 2, a:a + 128, :] = stage[:, a:a + 128].T
        if which < 3:
            fetch_left(which + 1).start()

    def own(k):
        if k >= 2:
            for j in range(R // 2):
                give(0, k - 2, j).wait_send()
        if chunks[k][1] == 0:
            turn_left(chunks[k][0])
            if chunks[k][0] == 2:
                turn_left(3)
        size = chunks[k][2]
        runs = []
        for p in range(R):
            slot, source = factors(k, p)
            if source is None:
                continue
            fetch(k, p).wait()
            if runs and runs[-1][0] == slot:
                runs[-1][2] = p + 1
            else:
                runs.append([slot, p, p + 1])
        for slot, first, end in runs:
            def body(i, carry):
                at = pl.ds(pl.multiple_of(i * 288, 16), 288)
                X[k % 2, at, first * size:end * size] = mul(
                    left[slot, at, :], right[:, first * size:end * size]).astype(X.dtype)
                return carry
            lax.fori_loop(0, full // 288, body, 0)
        if k + 1 < K:
            fetch_all(k + 1)
        for j in range(R // 2):
            give(0, k, j).start()

    def store(level, k, j):
        return held[level].at[j, :, pl.ds(kind[k] if level == L - 1 else every[k], chunks[k][2])]

    def give(level, k, j):
        if level == 0:
            source = X.at[k % 2, :, part_lanes(k, ((r ^ 1) & 1) | (j << 1))]
        else:
            source = store(level - 1, k, 2 * j + (((r >> level) & 1) ^ 1))
        return pltpu.make_async_remote_copy(
            src_ref=source, dst_ref=store(level, k, j), send_sem=send_sem.at[level, k, j],
            recv_sem=recv_sem.at[level, k, j], device_id={"replica": r ^ bits[level]}, device_id_type=MESH)

    STEP = 96

    def merge(level, k):
        for j in range(R >> (level + 1)):
            give(level, k, j).wait_recv()
            mine = store(level, k, j)
            other = X.at[k % 2, :, part_lanes(k, kept(0, j))] if level == 0 else store(level - 1, k, 2 * j + ((r >> level) & 1))

            def body(i, carry):
                at = pl.ds(pl.multiple_of(i * STEP, 16), STEP)
                mine[at, :] = (mine[at, :].astype(F32) + other[at, :].astype(F32)).astype(mine.dtype)
                return carry
            lax.fori_loop(0, full // STEP, body, 0)
        if level + 1 < last(k):
            for j in range(R >> (level + 2)):
                give(level + 1, k, j).start()

    def last(k):
        return L - 1 if ahead_of_pairs(k, L) else L

    def lanes(k):
        return range(2) if ahead_of_pairs(k, L) else range(1)

    def total(k, j):
        return store(L - 2, k, j) if ahead_of_pairs(k, L) else store(L - 1, k, 0)

    def moving(k, side, t, j):
        place = t - 1 if side == 0 else t
        at = pl.ds(kind[k], chunks[k][2])
        return flow_two.at[side, place, j, :, at] if ahead_of_pairs(k, L) else flow.at[side, place, :, at]

    def pass_on(k, t, side, j, source):
        return pltpu.make_async_remote_copy(
            src_ref=source, dst_ref=moving(k, side, t, j), send_sem=zsend.at[k, side, t, j], recv_sem=zrecv.at[k, side, t, j],
            device_id={"fsdp": z + 1 if side == 0 else z - 1}, device_id_type=MESH)

    def launch(k):
        @pl.when(z == 0)
        def _():
            for t in range(n - 1, 0, -1):
                for j in lanes(k):
                    pass_on(k, t, 0, j, total(k, j).at[block(t), :]).start()
        @pl.when(z == n - 1)
        def _():
            for t in range(n - 1):
                for j in lanes(k):
                    pass_on(k, t, 1, j, total(k, j).at[block(t), :]).start()

    RSTEP = 96 if rows % 96 == 0 else 16

    def add_block(target, other, at_other):
        def body(i, carry):
            at = pl.ds(pl.multiple_of(i * RSTEP, 16), RSTEP)
            there = pl.ds(pl.multiple_of(at_other + i * RSTEP, 16), RSTEP)
            target[at, :] = (target[at, :].astype(F32) + other[there, :].astype(F32)).astype(target.dtype)
            return carry
        lax.fori_loop(0, rows // RSTEP, body, 0)

    def flows(k, hop):
        @pl.when(z == hop)
        def _():
            for t in range(n - 1, hop - 1, -1):
                for j in lanes(k):
                    here = moving(k, 0, t, j)
                    pass_on(k, t, 0, j, here).wait_recv()
                    add_block(here, total(k, j), t * rows)
                    if t > hop:
                        pass_on(k, t, 0, j, here).start()
        @pl.when(z == n - 1 - hop)
        def _():
            for t in range(n - hop):
                for j in lanes(k):
                    here = moving(k, 1, t, j)
                    pass_on(k, t, 1, j, here).wait_recv()
                    if t < n - 1 - hop or hop == n - 1:
                        add_block(here, total(k, j), t * rows)
                    if t < n - 1 - hop:
                        pass_on(k, t, 1, j, here).start()
        if hop == n - 1:
            for j in lanes(k):
                @pl.when((z > 0) & (z < n - 1))
                def _():
                    add_block(moving(k, 1, z, j), moving(k, 0, z, j), 0)

    def both_ends(act):
        @pl.when(z < n - 1)
        def _():
            act(1)
        @pl.when(z == n - 1)
        def _():
            act(0)

    def bit(k):
        return (r >> (L - 1)) & 1

    def trade(k, side):
        return pltpu.make_async_remote_copy(
            src_ref=moving(k, side, z, 1 - bit(k)), dst_ref=pair.at[:, pl.ds(kind[k], chunks[k][2])], send_sem=psend.at[k],
            recv_sem=precv.at[k], device_id={"replica": r ^ bits[L - 1]}, device_id_type=MESH)

    def complete(k):
        def act(side):
            trade(k, side).wait_recv()
            add_block(moving(k, side, z, bit(k)), pair.at[:, pl.ds(kind[k], chunks[k][2])], 0)
        both_ends(act)

    def finished(k, p):
        return F.at[group(k), :, columns(k, p)]

    def share(k, p, level, source=None):
        return pltpu.make_async_remote_copy(
            src_ref=finished(k, p) if source is None else source, dst_ref=finished(k, p),
            send_sem=fsend.at[k, p, level], recv_sem=frecv.at[k, p], device_id={"replica": r ^ bits[level]}, device_id_type=MESH)

    def done(k, side):
        return moving(k, side, z, bit(k) if ahead_of_pairs(k, L) else 0)

    def keep(k, side):
        return pltpu.make_async_copy(done(k, side), finished(k, r), fkeep.at[k])

    def publish(k):
        def act(side):
            for level in reversed(range(L)):
                share(k, r, level, done(k, side)).start()
            keep(k, side).start()
        both_ends(act)

    def masks(level):
        found = [0]
        for upper in range(level + 1, L):
            found = found + [m | bits[upper] for m in found]
        return [m | bits[level] for m in found]

    def collect(level, k):
        for mask in masks(level):
            p = r ^ mask
            share(k, p, level).wait_recv()
            for lower in reversed(range(level)):
                share(k, p, lower).start()

    def small_to_z(t):
        return pltpu.make_async_remote_copy(
            src_ref=small_in.at[t], dst_ref=small_z.at[z], send_sem=ss_z.at[t], recv_sem=sr_z.at[z],
            device_id={"fsdp": t}, device_id_type=MESH)

    def small_to_r(p):
        return pltpu.make_async_remote_copy(
            src_ref=small_sum, dst_ref=small_r.at[r], send_sem=ss_r.at[p], recv_sem=sr_r.at[r],
            device_id={"replica": p}, device_id_type=MESH)

    fetch_left(0).start()
    fetch_all(0)
    pl.semaphore_wait(barrier, n - 1 + R - 1)
    own_small = pltpu.make_async_copy(small_in.at[z], small_z.at[z], ss_l)
    own_small.start()
    own(0)
    for hop in range(1, n):
        small_to_z(lax.rem(z + hop, n)).start()
    stages = L + n + L
    for turn in range(K + stages - 1):
        for stage_index in [1, 0] + list(range(2, stages)):
            k = turn - stage_index
            if k < 0 or k >= K:
                continue
            hop = stage_index - last(k)
            if stage_index == 0:
                if k > 0:
                    own(k)
            elif stage_index <= last(k):
                merge(stage_index - 1, k)
                if stage_index == last(k):
                    launch(k)
            elif hop < n:
                flows(k, hop)
                if hop == n - 1:
                    if ahead_of_pairs(k, L):
                        both_ends(lambda side: trade(k, side).start())
                    else:
                        publish(k)
            elif stage_index == L + n - 1:
                complete(k)
                publish(k)
            else:
                collect(L - 1 - (stage_index - L - n), k)
        if turn == 1:
            own_small.wait()
            for hop in range(1, n):
                source = lax.rem(z + hop, n)
                pltpu.make_async_remote_copy(
                    src_ref=small_in.at[source], dst_ref=small_z.at[source], send_sem=ss_z.at[source],
                    recv_sem=sr_z.at[source], device_id={"fsdp": source}, device_id_type=MESH).wait_recv()
            together = small_z[0]
            for t in range(1, n):
                together = together + small_z[t]
            small_sum[...] = together
            small_r[r] = together
            for hop in range(1, R):
                small_to_r(lax.rem(r + hop, R)).start()
    for hop in range(1, R):
        p = lax.rem(r + hop, R)
        pltpu.make_async_remote_copy(
            src_ref=small_sum, dst_ref=small_r.at[p], send_sem=ss_r.at[p], recv_sem=sr_r.at[p],
            device_id={"replica": p}, device_id_type=MESH).wait_recv()
    together = small_r[0]
    for p in range(1, R):
        together = together + small_r[p]
    small_out[...] = together
    for hop in range(1, R):
        small_to_r(lax.rem(r + hop, R)).wait_send()
    for hop in range(1, n):
        small_to_z(lax.rem(z + hop, n)).wait_send()
    for k in range(K):
        for level in range(last(k)):
            if level == 0 and k < K - 2:
                continue
            for j in range(R >> (level + 1)):
                give(level, k, j).wait_send()
        for t in range(n):
            for j in lanes(k):
                if t > 0:
                    @pl.when(t > z)
                    def _():
                        pass_on(k, t, 0, j, moving(k, 0, t, j)).wait_send()
                if t < n - 1:
                    @pl.when(t < z)
                    def _():
                        pass_on(k, t, 1, j, moving(k, 1, t, j)).wait_send()
        if ahead_of_pairs(k, L):
            both_ends(lambda side: trade(k, side).wait_send())
        both_ends(lambda side: keep(k, side).wait())
        for level in range(L):
            share(k, r, level).wait_send()
            for mask in masks(level):
                for lower in range(level):
                    share(k, r ^ mask, lower).wait_send()


def reduce_grads(n, R, wide, small, n1, c, n2, eb, dqkv, low, du, g):
    tokens, D = n1.shape
    rows = D // n
    part = wide // R
    chunks = plan(R, part, D)
    K = len(chunks)
    most = max(size for _, _, size in chunks)
    L = R.bit_length() - 1
    one, two, both = places(chunks, L)[2]
    two = max(two, 128)
    dma = pltpu.SemaphoreType.DMA
    return pl.pallas_call(
        functools.partial(reduce_kernel, n, R, chunks),
        out_shape=(jax.ShapeDtypeStruct((3, rows, wide), HALF),
                   jax.ShapeDtypeStruct(small.shape[1:], small.dtype)),
        in_specs=[pl.BlockSpec(memory_space=pltpu.VMEM)] + [ANY] * 8,
        out_specs=(ANY, pl.BlockSpec(memory_space=pltpu.VMEM)),
        scratch_shapes=[pltpu.VMEM((R >> (level + 1), D, one if level == L - 1 else both), HALF) for level in range(L)] + [
            pltpu.VMEM((2, D, R * most), HALF),
            pltpu.VMEM((2, D, tokens), HALF),
            pltpu.VMEM((tokens, D), HALF),
            pltpu.VMEM((tokens, R * most), HALF),
            pltpu.VMEM((2, n - 1, rows, one), HALF),
            pltpu.VMEM((2, n - 1, 2, rows, two), HALF),
            pltpu.VMEM((rows, two), HALF),
            pltpu.VMEM((n,) + small.shape[1:], small.dtype),
            pltpu.VMEM((R,) + small.shape[1:], small.dtype),
            pltpu.VMEM(small.shape[1:], small.dtype),
            dma((R,)), dma(()),
            dma((L, K, R // 2)), dma((L, K, R // 2)),
            dma((K, 2, n, 2)), dma((K, 2, n, 2)),
            dma((K,)), dma((K,)),
            dma((K, R, L)), dma((K, R)), dma((K,)),
            dma((n,)), dma((n,)), dma((R,)), dma((R,)), dma(()),
        ],
        compiler_params=pltpu.CompilerParams(collective_id=1, has_side_effects=True, vmem_limit_bytes=62 * 1024 * 1024),
    )(small, n1, c, n2, eb, dqkv, low, du, g)


def shifted(value, axis, steps):
    count = lax.axis_size(axis)
    first, last = (max(0, -steps), min(count, count - steps))
    return lax.ppermute(value, axis, [(source, source + steps) for source in range(first, last)])


def pad_columns(value, wide):
    return jnp.pad(value, ((0, 0), (0, wide - value.shape[1])))


def on_device(ends, first_gain, first_shift, qkv_weight, qv_bias, out_weight, out_bias, second_gain, second_shift,
              up_weight, up_bias, down_weight, down_bias):
    n, R = lax.axis_size("fsdp"), lax.axis_size("replica")
    section = lax.axis_index("section")
    at_first = section == 0
    _, images, tok, D = ends.shape
    hidden = up_weight.shape[2]
    piece = D // n
    unit = 128 * R
    filled = -(-hidden // LANES) * LANES
    wide = max(-(-4 * D // unit), -(-filled // unit)) * unit

    vector = jnp.concatenate([first_gain[0], first_shift[0], qv_bias[0, 0], qv_bias[0, 1], out_bias[0], second_gain[0],
                              second_shift[0], down_bias[0], up_bias[0]])
    lanes = -(-vector.shape[0] // (16 * 128)) * 128
    small = jnp.pad(vector, (0, 16 * lanes - vector.shape[0])).reshape(16, lanes)
    G, S = gather_weights(n, R, qkv_weight[0], out_weight[0], pad_columns(up_weight[0], wide),
                          pad_columns(down_weight[0].T, wide), small)
    S = S.reshape(n, -1).astype(F32)
    vec = S[:, : 8 * piece].reshape(n, 8, piece).transpose(1, 0, 2).reshape(8, D)
    ub = pad_columns(S[:, 8 * piece : 8 * piece + hidden // n].reshape(1, hidden), filled)
    qb = jnp.concatenate([vec[2], jnp.zeros_like(vec[2]), vec[3]])[None]

    rows = ends[0].reshape(images * tok, D)
    T = images // MICRO * tok
    total = MICRO * T
    parts = [rows[m * T : (m + 1) * T] for m in range(MICRO)]
    here = section.astype(jnp.int32)

    def turn(micro, where):
        return jnp.stack([jnp.int32(micro), (here == where).astype(jnp.int32)])

    kept = (None,) * 9
    sent = []
    for micro in range(MICRO):
        *kept, y = f_layer(turn(micro, 0), total, wide, parts[micro], vec, qb, ub, G, tok, kept)
        sent.append(shifted(y, "section", 1))
    for micro in range(MICRO):
        *kept, y = f_layer(turn(micro, 1), total, wide, sent[micro], vec, qb, ub, G, tok, kept)
    n1, qkv, probs, c, r1, n2, g, gp, result = kept

    kept = (None, None, None, result)
    back = []
    stats, sums = [], []
    for where in (1, 0):
        for micro in range(MICRO):
            e, x = (parts[micro], sent[micro]) if where else (back[micro], parts[micro])
            *kept, dx, stat, part = d_layer(turn(micro, where), total, wide, where == 0, e, x, vec, G, gp, r1, qkv, probs, tok, kept)
            stats.append(stat)
            sums.append(part)
            if where:
                back.append(shifted(dx, "section", -1))
    du, low, dqkv, result = kept
    stats = sum(jnp.where(at_first, below, above) for above, below in zip(stats[:MICRO], stats[MICRO:]))
    sums = sum(jnp.where(at_first, below, above) for above, below in zip(sums[:MICRO], sums[MICRO:]))
    eb = jnp.where(at_first, jnp.concatenate(back), rows)

    stats = stats.sum(axis=1)
    vectors = jnp.stack([stats[4], stats[5], stats[6], stats[7], stats[2], stats[0], stats[1], stats[3]])
    vectors = vectors.reshape(8, n, piece).transpose(1, 0, 2).reshape(n, 8 * piece)
    vectors = jnp.concatenate([vectors, sums[0, :hidden].reshape(n, hidden // n)], axis=1)
    lanes = -(-vectors.shape[1] // (16 * 128)) * 128
    small = jnp.pad(vectors, ((0, 0), (0, 16 * lanes - vectors.shape[1]))).reshape(n, 16, lanes)
    F, s = reduce_grads(n, R, wide, small, n1, c, n2, eb, dqkv, low, du, g)
    s = s.reshape(-1)
    v = s[: 8 * piece].reshape(8, piece)
    return (
        result.reshape(1, images, tok, D),
        v[0][None],
        v[1][None],
        F[0, :, : 3 * D].astype(F32)[None],
        v[2:4][None],
        F[0, :, 3 * D : 4 * D].astype(F32)[None],
        v[4][None],
        v[5][None],
        v[6][None],
        F[1, :, :hidden].astype(F32)[None],
        s[8 * piece : 8 * piece + hidden // n][None],
        F[2, :, :hidden].T.astype(F32)[None],
        v[7][None],
    )


def solution(mesh):
    placed = (
        P("section", ("fsdp", "replica"), None, None),
        P("section", "fsdp"),
        P("section", "fsdp"),
        P("section", "fsdp", None),
        P("section", None, "fsdp"),
        P("section", "fsdp", None),
        P("section", "fsdp"),
        P("section", "fsdp"),
        P("section", "fsdp"),
        P("section", "fsdp", None),
        P("section", "fsdp"),
        P("section", None, "fsdp"),
        P("section", "fsdp"),
    )
    return jax.shard_map(on_device, mesh=mesh, in_specs=placed, out_specs=placed, check_vma=False)
```

```python
import functools
import math

import jax
import jax.numpy as jnp
from jax import lax
from jax.experimental import pallas as pl
from jax.experimental.pallas import tpu as pltpu
from jax.sharding import PartitionSpec as P

MESH = pl.DeviceIdType.MESH
HEADS = 16
HEAD_DIM = 72
MICRO = 3
F32 = jnp.float32
HALF = jnp.bfloat16
EPS = 1e-06
ANY = pl.BlockSpec(memory_space=pl.ANY)
NN = (((1,), (0,)), ((), ()))
NT = (((1,), (1,)), ((), ()))
TN = (((0,), (0,)), ((), ()))
FOLD = 8


def mul(left, right, dims=NN):
    return lax.dot_general(left, right, dims, preferred_element_type=F32)


def row_loop(count, step, body):
    def run(i, carry):
        body(pl.ds(pl.multiple_of(i * step, step), step))
        return carry
    lax.fori_loop(0, count // step, run, 0)


def normal(value):
    center = value - jnp.mean(value, axis=-1, keepdims=True)
    scale = lax.rsqrt(jnp.mean(center * center, axis=-1, keepdims=True) + EPS)
    return center * scale, scale


def fold(value):
    return value.reshape(value.shape[0] // 8, 8, value.shape[1]).sum(axis=0)


def norm_back(value, grad, gain):
    hat, scale = normal(value)
    d = grad * gain
    low = d - jnp.mean(d, axis=-1, keepdims=True) - hat * jnp.mean(d * hat, axis=-1, keepdims=True)
    return low * scale, hat


def params(limit=56, **kw):
    return pltpu.CompilerParams(vmem_limit_bytes=limit * 1024 * 1024, **kw)


def shape(rows, columns, dtype):
    return jax.ShapeDtypeStruct((rows, columns), dtype)


def spans(h):
    a, b = h * HEAD_DIM, (h + 1) * HEAD_DIM
    lo = a // 128 * 128
    hi = -(-b // 128) * 128
    return a, b, lo, hi

def head_mask(h, rows):
    a, b, lo, hi = spans(h)
    lane = lax.broadcasted_iota(jnp.int32, (rows, hi - lo), 1) + lo
    return (lane >= a) & (lane < b)

FOLD = 8


def attn_image(qkv, P, c, D, tok, factor):
    for first in range(0, HEADS, FOLD):
        heads = range(first, first + FOLD)
        held = []
        for h in heads:
            a, b, lo, hi = spans(h)
            held.append(mul(qkv[:, D + lo:D + hi], jnp.where(head_mask(h, tok), qkv[:, lo:hi], 0), NT))
        probs = []
        for h, s in zip(heads, held):
            e = jnp.exp2((s - jnp.max(s, axis=0, keepdims=True)) * factor)
            p = (e * (1.0 / jnp.sum(e, axis=0, keepdims=True))).astype(HALF)
            P[h] = p
            probs.append(p)
        for h, p in zip(heads, probs):
            a, b, lo, hi = spans(h)
            o = mul(p, qkv[:, 2 * D + lo:2 * D + hi], TN).astype(HALF)
            c[:, lo:hi] = jnp.where(head_mask(h, tok), o, c[:, lo:hi]) if a > lo else o


def attn_back_image(qkv, P, dc, out, D, tok, factor):
    for first in range(0, HEADS, FOLD):
        heads = range(first, first + FOLD)
        held = []
        for h in heads:
            a, b, lo, hi = spans(h)
            held.append(mul(qkv[:, 2 * D + lo:2 * D + hi], jnp.where(head_mask(h, tok), dc[:, lo:hi], 0), NT))
        grads = []
        for h, dp in zip(heads, held):
            wide = P[h].astype(F32)
            grads.append((wide * (dp - jnp.sum(wide * dp, axis=0, keepdims=True)) * factor).astype(HALF))
        for h, ds in zip(heads, grads):
            a, b, lo, hi = spans(h)
            mask = head_mask(h, tok)
            dv = mul(P[h], dc[:, lo:hi]).astype(HALF)
            dk = mul(ds, qkv[:, lo:hi]).astype(HALF)
            dq = mul(ds, qkv[:, D + lo:D + hi], TN).astype(HALF)
            for base, value in ((0, dq), (D, dk), (2 * D, dv)):
                at = slice(base + lo, base + hi)
                out[:, at] = jnp.where(mask, value, out[:, at]) if a > lo else value


TILE = 512
LANES = 256


def pieces(width, step):
    return [(a, min(step, width - a)) for a in range(0, width, step)]


def tiles(width, step, body):
    whole = width // step
    def run(i, carry):
        body(pl.multiple_of(i * step, step), step)
        return carry
    lax.fori_loop(0, whole, run, 0)
    if width % step:
        body(whole * step, width % step)


def f_layer(slots, total, wide, final, x, vec, qb, ub, G, tok, kept):
    T, D = x.shape
    hidden = ub.shape[1]
    images = T // tok
    factor = HEAD_DIM ** (-0.5) * math.log2(math.e)
    root = math.sqrt(2.0 / math.pi)
    cut = pieces(4 * D, 768)
    plain, spare = 5, sum(b is not None for b in kept)
    chunk = T // 2 if T % 32 == 0 else T

    def kernel(slot, *refs):
        @pl.when(slot[1] == 1)
        def _():
            work(slot, *refs)

    def work(slot, *refs):
        x, vec, qb, ub, G = refs[:plain]
        (n1o, qkvo, Po, co, r1o, n2o, go, gpo, reso, y,
         wa, wb, n1, qkv, P, c, r1, n2, g, gp, res, wsem, psem, gsem, osem) = refs[plain + spare:]
        save = pl.ds(pl.multiple_of(slot[0] * T, 16), T)

        def weight(j):
            a, w = cut[j]
            return pltpu.make_async_copy(G.at[0, :, pl.ds(a, w)], wa.at[:, pl.ds(a, w)], wsem.at[j])
        up = pltpu.make_async_copy(G.at[1, :, pl.ds(0, hidden)], wb, wsem.at[len(cut)])
        down = pltpu.make_async_copy(G.at[2, :, pl.ds(0, hidden)], wa.at[:, pl.ds(0, hidden)], wsem.at[len(cut) + 1])
        for j in range(len(cut)):
            weight(j).start()
        up.start()

        def out(source, target, at, k):
            return pltpu.make_async_copy(source, target.at[at], osem.at[k])
        outs = [out(n1, n1o, save, 0), out(qkv, qkvo, save, 1), out(c, co, save, 2), out(r1, r1o, save, 3),
                out(n2, n2o, save, 4), out(g, go, (save, pl.ds(0, hidden)), 5)]
        if final:
            outs.append(out(res, reso, save, 6))

        def first(at):
            n1[at, :] = (normal(x[at, :].astype(F32))[0] * vec[0:1, :] + vec[1:2, :]).astype(HALF)
        row_loop(T, tok, first)
        outs[0].start()
        for j, (a, w) in enumerate(cut):
            weight(j).wait()
            if a < 3 * D:
                b = min(a + w, 3 * D)
                qkv[:, a:b] = (mul(n1[...], wa[:, a:b]) + qb[:, a:b]).astype(HALF)
        outs[1].start()

        def probs(i):
            return pltpu.make_async_copy(P.at[i % 2], Po.at[slot[0] * images + i], psem.at[i % 2])

        def image(i, carry):
            @pl.when(i >= 2)
            def _():
                probs(i - 2).wait()
            rows = pl.ds(pl.multiple_of(i * tok, 16), tok)
            attn_image(qkv.at[rows], P.at[i % 2], c.at[rows], D, tok, factor)
            probs(i).start()
            return carry
        lax.fori_loop(0, images, image, 0)
        outs[2].start()
        r1[...] = mul(c[...], wa[:, 3 * D:4 * D])
        down.start()

        def second(at):
            value = r1[at, :] + vec[4:5, :] + x[at, :].astype(F32)
            r1[at, :] = value
            n2[at, :] = (normal(value)[0] * vec[5:6, :] + vec[6:7, :]).astype(HALF)
        row_loop(T, tok, second)
        outs[3].start()
        outs[4].start()
        up.wait()

        def slope(i, size):
            return pltpu.make_async_copy(
                gp.at[lax.rem(i, 2), :, pl.ds(0, size)], gpo.at[save, pl.ds(pl.multiple_of(i * TILE, 128), size)],
                gsem.at[lax.rem(i, 2)])

        def rise(start, size):
            i = start // TILE
            @pl.when(i >= 2)
            def _():
                slope(i - 2, TILE).wait()
            at = pl.ds(start, size)
            for a in range(0, T, chunk):
                u = mul(n2[a:a + chunk, :], wb[:, at]) + ub[:, at]
                square = u * u
                t = jnp.tanh(u * (root + (root * 0.044715) * square))
                half = 0.5 + 0.5 * t
                g[a:a + chunk, at] = (u * half).astype(HALF)
                gp[lax.rem(i, 2), a:a + chunk, 0:size] = (
                    half + (0.5 * u) * (1.0 - t * t) * (root + (3.0 * root * 0.044715) * square)).astype(HALF)
            slope(i, size).start()
        tiles(hidden, TILE, rise)
        outs[5].start()
        down.wait()
        for a, w in pieces(D, LANES):
            at = slice(a, a + w)
            value = mul(g[...], wa[a:a + w, 0:hidden], NT) + (r1[:, at] + vec[7:8, at])
            if final:
                res[:, at] = value
            y[:, at] = value.astype(HALF)
        if final:
            outs[6].start()
        for copy in outs:
            copy.wait()
        for i in range(max(0, images - 2), images):
            probs(i).wait()
        count = -(-hidden // TILE)
        for i in range(max(0, count - 2), count):
            slope(i, min(TILE, hidden - i * TILE)).wait()

    aliases = {}
    ins = [x, vec, qb, ub, G]
    for index, buffer in enumerate(kept):
        if buffer is not None:
            aliases[1 + len(ins)] = index
            ins.append(buffer)
    dma = pltpu.SemaphoreType.DMA
    whole = pl.BlockSpec(memory_space=pltpu.VMEM)
    return pl.pallas_call(
        kernel,
        out_shape=(shape(total, D, HALF), shape(total, 3 * D, HALF),
                   jax.ShapeDtypeStruct((total // tok, HEADS, tok, tok), HALF), shape(total, D, HALF), shape(total, D, F32),
                   shape(total, D, HALF), shape(total, wide, HALF), shape(total, hidden, HALF), shape(total, D, F32),
                   shape(T, D, HALF)),
        grid_spec=pltpu.PrefetchScalarGridSpec(
            num_scalar_prefetch=1, grid=(1,), in_specs=[whole] * 4 + [ANY] * (1 + spare), out_specs=(ANY,) * 9 + (whole,),
            scratch_shapes=[
                pltpu.VMEM((D, 4 * D), HALF), pltpu.VMEM((D, hidden), HALF), pltpu.VMEM((T, D), HALF),
                pltpu.VMEM((T, 3 * D), HALF), pltpu.VMEM((2, HEADS, tok, tok), HALF), pltpu.VMEM((T, D), HALF),
                pltpu.VMEM((T, D), F32), pltpu.VMEM((T, D), HALF), pltpu.VMEM((T, hidden), HALF),
                pltpu.VMEM((2, T, TILE), HALF), pltpu.VMEM((T, D), F32),
                dma((len(cut) + 2,)), dma((2,)), dma((2,)), dma((7,))]),
        input_output_aliases=aliases,
        compiler_params=params(60),
        cost_estimate=pl.CostEstimate(flops=T * D, bytes_accessed=T * D, transcendentals=0),
    )(slots, *ins)


def d_layer(slots, total, wide, final, e, x, vec, G, GP, R1, QKV, PP, tok, kept):
    T, D = x.shape
    hidden = GP.shape[1]
    images = T // tok
    scale = HEAD_DIM ** (-0.5)
    plain, spare = 8, sum(b is not None for b in kept)
    chunk = T // 2 if T % 32 == 0 else T

    def kernel(slot, *refs):
        @pl.when(slot[1] == 1)
        def _():
            work(slot, *refs)

    def work(slot, *refs):
        e, x, vec, G, GP, R1, QKV, PP = refs[:plain]
        (duo, lowo, dqkvo, reso, dx, stats, sums,
         wa, wb, gp, r1, qkv, P, du, grad, dr1, low, dc, dqkv, wsem, psem, isem, osem) = refs[plain + spare:]
        save = pl.ds(pl.multiple_of(slot[0] * T, 16), T)
        cuts = pieces(hidden, 2 * TILE)
        down = [pltpu.make_async_copy(G.at[2, :, pl.ds(a, w)], wa.at[:, pl.ds(a, w)], wsem.at[2 + j]) for j, (a, w) in enumerate(cuts)]
        slope = [pltpu.make_async_copy(GP.at[save, pl.ds(a, w)], gp.at[:, pl.ds(a, w)], isem.at[2 + j]) for j, (a, w) in enumerate(cuts)]
        up = pltpu.make_async_copy(G.at[1, :, pl.ds(0, hidden)], wb, wsem.at[0])
        rest = pltpu.make_async_copy(G.at[0, :, pl.ds(0, 4 * D)], wa, wsem.at[1])
        loads = [pltpu.make_async_copy(R1.at[save], r1, isem.at[0]), pltpu.make_async_copy(QKV.at[save], qkv, isem.at[1])]
        for weight, factor in zip(down, slope):
            weight.start()
            factor.start()
        up.start()
        for copy in loads:
            copy.start()

        def out(source, target, at, k):
            return pltpu.make_async_copy(source, target.at[at], osem.at[k])
        outs = [out(du, duo, (save, pl.ds(0, hidden)), 0), out(low, lowo, save, 1), out(dqkv, dqkvo, save, 2)]
        if final:
            outs.append(out(dr1, reso, save, 3))

        def probs(i):
            return pltpu.make_async_copy(PP.at[slot[0] * images + i], P.at[i % 2], psem.at[i % 2])
        for i in range(min(2, images)):
            probs(i).start()
        stats[...] = jnp.zeros_like(stats)

        def fall(start, size):
            at = pl.ds(start, size)
            total = None
            for a in range(0, T, chunk):
                d = (mul(e[a:a + chunk, :], wa[:, at]) * gp[a:a + chunk, at].astype(F32)).astype(HALF)
                du[a:a + chunk, at] = d
                part = jnp.sum(d.astype(F32), axis=0, keepdims=True)
                total = part if total is None else total + part
            sums[:, at] = total
        for j, (a, w) in enumerate(cuts):
            down[j].wait()
            slope[j].wait()
            for b in range(a, a + w, TILE):
                fall(b, min(TILE, a + w - b))
        rest.start()
        outs[0].start()
        up.wait()
        for a, w in pieces(D, LANES):
            grad[:, a:a + w] = mul(du[...], wb[a:a + w, :], NT)
        loads[0].wait()

        def second(at):
            g = grad[at, :]
            part, hat = norm_back(r1[at, :], g, vec[5:6, :])
            eb = e[at, :].astype(F32)
            value = eb + part
            rounded = value.astype(HALF)
            dr1[at, :] = value
            low[at, :] = rounded
            stats[0] += fold(g * hat)
            stats[1] += fold(g)
            stats[2] += fold(rounded.astype(F32))
            stats[3] += fold(eb)
        row_loop(T, tok, second)
        outs[1].start()
        rest.wait()
        for a, w in pieces(D, LANES):
            dc[:, a:a + w] = mul(low[...], wa[a:a + w, 3 * D:4 * D], NT).astype(HALF)
        loads[1].wait()

        def image(i, carry):
            probs(i).wait()
            rows = pl.ds(pl.multiple_of(i * tok, 16), tok)
            attn_back_image(qkv.at[rows], P.at[i % 2], dc.at[rows], dqkv.at[rows], D, tok, scale)
            @pl.when(i + 2 < images)
            def _():
                probs(i + 2).start()
            return carry
        lax.fori_loop(0, images, image, 0)
        outs[2].start()
        for a, w in pieces(D, LANES):
            grad[:, a:a + w] = mul(dqkv[...], wa[a:a + w, 0:3 * D], NT)

        def first(at):
            g = grad[at, :]
            part, hat = norm_back(x[at, :].astype(F32), g, vec[0:1, :])
            value = dr1[at, :] + part
            dr1[at, :] = value
            dx[at, :] = value.astype(HALF)
            stats[4] += fold(g * hat)
            stats[5] += fold(g)
            stats[6] += fold(dqkv[at, 0:D].astype(F32))
            stats[7] += fold(dqkv[at, 2 * D:3 * D].astype(F32))
        row_loop(T, tok, first)
        if final:
            outs[3].start()
        for copy in outs:
            copy.wait()

    aliases = {}
    ins = [e, x, vec, G, GP, R1, QKV, PP]
    for index, buffer in enumerate(kept):
        if buffer is not None:
            aliases[1 + len(ins)] = index
            ins.append(buffer)
    dma = pltpu.SemaphoreType.DMA
    whole = pl.BlockSpec(memory_space=pltpu.VMEM)
    return pl.pallas_call(
        kernel,
        out_shape=(shape(total, wide, HALF), shape(total, D, HALF), shape(total, 3 * D, HALF), shape(total, D, F32),
                   shape(T, D, HALF), jax.ShapeDtypeStruct((8, 8, D), F32), shape(1, hidden, F32)),
        grid_spec=pltpu.PrefetchScalarGridSpec(
            num_scalar_prefetch=1, grid=(1,), in_specs=[whole] * 3 + [ANY] * (5 + spare), out_specs=(ANY,) * 4 + (whole,) * 3,
            scratch_shapes=[
                pltpu.VMEM((D, 4 * D), HALF), pltpu.VMEM((D, hidden), HALF), pltpu.VMEM((T, hidden), HALF),
                pltpu.VMEM((T, D), F32), pltpu.VMEM((T, 3 * D), HALF), pltpu.VMEM((2, HEADS, tok, tok), HALF),
                pltpu.VMEM((T, hidden), HALF), pltpu.VMEM((T, D), F32), pltpu.VMEM((T, D), F32), pltpu.VMEM((T, D), HALF),
                pltpu.VMEM((T, D), HALF), pltpu.VMEM((T, 3 * D), HALF),
                dma((2 + len(pieces(hidden, 2 * TILE)),)), dma((2,)), dma((2 + len(pieces(hidden, 2 * TILE)),)), dma((4,))]),
        input_output_aliases=aliases,
        compiler_params=params(60),
        cost_estimate=pl.CostEstimate(flops=T * D, bytes_accessed=T * D, transcendentals=0),
    )(slots, *ins)


def powers(count):
    bits = []
    bit = count // 2
    while bit:
        bits.append(bit)
        bit //= 2
    return bits

def gather_kernel(n, R, halves, qkv, out, up, down, *refs):
    (gain_one, shift_one, bias_qv, bias_out, gain_two, shift_two, bias_down, bias_up,
     G, vec, qb, ub, stage, S, lsem, ssem, rsem, small_send, small_recv) = refs
    z = lax.axis_index("fsdp")
    r = lax.axis_index("replica")
    rows, wide = up.shape
    part = wide // R
    some = rows // halves
    bits = powers(R)
    barrier = pltpu.get_barrier_semaphore()
    for hop in range(1, n):
        pl.semaphore_signal(barrier, inc=1, device_id={"fsdp": lax.rem(z + hop, n)}, device_id_type=MESH)
    for bit in bits:
        pl.semaphore_signal(barrier, inc=1, device_id={"replica": r ^ bit}, device_id_type=MESH)
    mine = pl.ds(pl.multiple_of(z * rows, 16), rows)
    first = qkv.shape[1]
    local = [
        pltpu.make_async_copy(qkv, stage.at[0, :, pl.ds(0, first)], lsem.at[0]),
        pltpu.make_async_copy(out, stage.at[0, :, pl.ds(first, out.shape[1])], lsem.at[1]),
        pltpu.make_async_copy(up, stage.at[1], lsem.at[2]),
        pltpu.make_async_copy(down, stage.at[2], lsem.at[3]),
    ]
    for copy in local:
        copy.start()
    keep = [pltpu.make_async_copy(stage.at[group], G.at[group, mine], lsem.at[4 + group]) for group in range(3)]

    for row, value in enumerate((gain_one, shift_one, None, None, bias_out, gain_two, shift_two, bias_down, bias_up)):
        value = bias_qv[row - 2:row - 1, :] if value is None else value[...]
        S[z, row:row + 1, 0:value.shape[1]] = value.astype(F32)
    pl.semaphore_wait(barrier, n - 1 + len(bits))

    def piece(unit, source, column):
        group, half = unit // halves, unit % halves
        return G.at[group, pl.ds(pl.multiple_of(source * rows + half * some, 16), some),
                    pl.ds(pl.multiple_of(column * part, 128), part)]

    def send(unit, source, column, kind, target, origin=None):
        return pltpu.make_async_remote_copy(
            src_ref=piece(unit, source, column) if origin is None else origin, dst_ref=piece(unit, source, column),
            send_sem=ssem.at[unit, source, column, kind], recv_sem=rsem.at[unit, source, column],
            device_id=target, device_id_type=MESH)

    def to_right(unit, source, origin=None):
        return send(unit, source, r, 0, {"fsdp": z + 1}, origin)

    def to_left(unit, source, origin=None):
        return send(unit, source, r, 1, {"fsdp": z - 1}, origin)

    def own(unit):
        return stage.at[unit // halves, pl.ds(unit % halves * some, some), pl.ds(pl.multiple_of(r * part, 128), part)]

    def share(unit, source, column, level):
        return send(unit, source, column, 2 + level, {"replica": r ^ bits[level]})

    def arrived(unit, source, column):
        send(unit, source, column, 0, {"replica": r ^ bits[0]}).wait_recv()

    def small_to(hop):
        return pltpu.make_async_remote_copy(
            src_ref=S.at[z], dst_ref=S.at[z], send_sem=small_send.at[hop],
            recv_sem=small_recv.at[z], device_id={"fsdp": lax.rem(z + hop, n)}, device_id_type=MESH)
    for hop in range(1, n):
        small_to(hop).start()
    for group in range(3):
        if group == 0:
            local[0].wait()
            local[1].wait()
        else:
            local[1 + group].wait()
        for unit in range(group * halves, (group + 1) * halves):
            @pl.when(z + 1 < n)
            def _():
                to_right(unit, z, own(unit)).start()
            @pl.when(z > 0)
            def _():
                to_left(unit, z, own(unit)).start()
        keep[group].start()
    columns = {}
    for level, bit in enumerate(bits):
        masks = [0]
        for upper in bits[:level]:
            masks = masks + [m | upper for m in masks]
        columns[level] = [bit | m for m in masks]
    units = 3 * halves
    steps = [(hop, unit) for hop in range(1, n) for unit in range(units)]
    for turn in range(len(steps) + len(bits)):
        for level in range(-1, len(bits)):
            place = turn - 1 - level
            if place < 0 or place >= len(steps):
                continue
            hop, unit = steps[place]
            for sign in (-1, 1):
                source = z + sign * hop
                @pl.when((source >= 0) & (source < n))
                def _():
                    if level < 0:
                        arrived(unit, source, r)
                        for lower in range(len(bits)):
                            share(unit, source, r, lower).start()
                        if sign < 0:
                            @pl.when(z + 1 < n)
                            def _():
                                to_right(unit, source).start()
                        else:
                            @pl.when(z > 0)
                            def _():
                                to_left(unit, source).start()
                    else:
                        for mask in columns[level]:
                            arrived(unit, source, r ^ mask)
                            for lower in range(level + 1, len(bits)):
                                share(unit, source, r ^ mask, lower).start()
    for copy in keep:
        copy.wait()
    for hop in range(1, n):
        source = lax.rem(z + hop, n)
        pltpu.make_async_remote_copy(
            src_ref=S.at[source], dst_ref=S.at[source], send_sem=small_send.at[hop],
            recv_sem=small_recv.at[source], device_id={"fsdp": source}, device_id_type=MESH).wait_recv()
        small_to(hop).wait_send()
    D = vec.shape[1]
    few = bias_up.shape[1]
    ub[...] = jnp.zeros_like(ub)
    for source in range(n):
        vec[:, source * rows:(source + 1) * rows] = S[source, 0:8, 0:rows]
        ub[:, source * few:(source + 1) * few] = S[source, 8:9, 0:few]
    qb[:, 0:D] = vec[2:3, :]
    qb[:, D:2 * D] = jnp.zeros((1, D), F32)
    qb[:, 2 * D:3 * D] = vec[3:4, :]
    for unit in range(units):
        for source in range(n):
            @pl.when((source <= z) & (z + 1 < n))
            def _():
                to_right(unit, source).wait_send()
            @pl.when((source >= z) & (z > 0))
            def _():
                to_left(unit, source).wait_send()
            @pl.when(source != z)
            def _():
                for level in range(len(bits)):
                    share(unit, source, r, level).wait_send()
                for level in range(len(bits)):
                    for mask in columns[level]:
                        for lower in range(level + 1, len(bits)):
                            share(unit, source, r ^ mask, lower).wait_send()


def gather_weights(n, R, filled, qkv, out, up, down, vectors):
    rows, wide = up.shape
    kinds = 2 + len(powers(R))
    halves = 2 if rows % 32 == 0 else 1
    lanes = -(-max(v.shape[1] for v in vectors) // 128) * 128
    dma = pltpu.SemaphoreType.DMA
    whole = pl.BlockSpec(memory_space=pltpu.VMEM)
    D = n * rows
    return pl.pallas_call(
        functools.partial(gather_kernel, n, R, halves),
        out_shape=(jax.ShapeDtypeStruct((3, D, wide), qkv.dtype), shape(8, D, F32), shape(1, 3 * D, F32),
                   shape(1, filled, F32)),
        in_specs=[ANY] * 4 + [whole] * len(vectors),
        out_specs=(ANY,) + (whole,) * 3,
        scratch_shapes=[
            pltpu.VMEM((3, rows, wide), qkv.dtype),
            pltpu.VMEM((n, 16, lanes), F32),
            dma((7,)),
            dma((3 * halves, n, R, kinds)),
            dma((3 * halves, n, R)),
            dma((n,)),
            dma((n,)),
        ],
        compiler_params=pltpu.CompilerParams(collective_id=0, has_side_effects=True, vmem_limit_bytes=32 * 1024 * 1024),
    )(qkv, out, up, down, *vectors)


ORDER = (2, 1, 0)
SCRATCH = 26


def plan(R, part, D):
    found = []
    for place in range(3):
        edges = (3 * D, 4 * D) if ORDER[place] == 0 else ()
        sizes, at = [], 0
        while at < part:
            size = min(max(12 // R, 1) * 128, part - at)
            while any(p * part + at < edge < p * part + at + size for p in range(R) for edge in edges):
                size -= 128
            sizes.append(size)
            at += size
        if place == 0 and sizes[0] == 384:
            sizes[:1] = [128, 256]
        if place == 2 and sizes[-1] > 128:
            sizes[-1:] = [sizes[-1] - 128, 128]
        at = 0
        for size in sizes:
            found.append((place, at, size))
            at += size
    return found


def ahead_of_pairs(k, L):
    return L >= 2 and k % 3 == 2


def places(chunks, L):
    every, kind, counts = [], [], [0, 0, 0]
    for k, (_, _, size) in enumerate(chunks):
        which = int(ahead_of_pairs(k, L))
        every.append(counts[2])
        kind.append(counts[which])
        counts[which] += size
        counts[2] += size
    return every, kind, counts


def reduce_kernel(n, R, chunks, small_in, n1, c, n2, rows_in, dqkv, low, du, g, *refs):
    back = refs[:-2 - SCRATCH - (R.bit_length() - 1)]
    F, small_out, *scratch = refs[len(back):]
    L = R.bit_length() - 1
    bits = [1 << level for level in range(L)]
    held = scratch[:L]
    (X, left, stage, right, flow, flow_two, pair, small_z, small_r, small_sum, rsem, lsem, send_sem, recv_sem, zsend, zrecv,
     psend, precv, fsend, frecv, fkeep, ss_z, sr_z, ss_r, sr_r, ss_l) = scratch[L:]
    z = lax.axis_index("fsdp")
    r = lax.axis_index("replica")
    tokens, D = n1.shape
    full = D
    rows = full // n
    wide = F.shape[2]
    part = wide // R
    K = len(chunks)
    every, kind, _ = places(chunks, L)
    barrier = pltpu.get_barrier_semaphore()
    for hop in range(1, n):
        pl.semaphore_signal(barrier, inc=1, device_id={"fsdp": lax.rem(z + hop, n)}, device_id_type=MESH)
    for hop in range(1, R):
        pl.semaphore_signal(barrier, inc=1, device_id={"replica": lax.rem(r + hop, R)}, device_id_type=MESH)

    def group(k):
        return ORDER[chunks[k][0]]

    def columns(k, p):
        return pl.ds(pl.multiple_of(p * part + chunks[k][1], 128), chunks[k][2])

    def part_lanes(k, p):
        return pl.ds(pl.multiple_of(p * chunks[k][2], 128), chunks[k][2])

    def block(t):
        return pl.ds(pl.multiple_of(t * rows, 16), rows)

    def kept(level, j):
        return (r & ((2 << level) - 1)) | (j << (level + 1))

    def factors(k, p):
        a, sub = p * part + chunks[k][1], chunks[k][2]
        if group(k) == 2:
            return 0, g.at[:, pl.ds(a, sub)]
        if group(k) == 1:
            return 1, du.at[:, pl.ds(a, sub)]
        if a < 3 * D:
            return 0, dqkv.at[:, pl.ds(a, sub)]
        if a < 4 * D:
            return 1, low.at[:, pl.ds(a - 3 * D, sub)]
        return None, None

    def fetch(k, p):
        return pltpu.make_async_copy(factors(k, p)[1], right.at[:, pl.ds(p * chunks[k][2], chunks[k][2])], rsem.at[p])

    def fetch_all(k):
        for p in range(R):
            if factors(k, p)[1] is not None:
                fetch(k, p).start()

    def fetch_left(which):
        return pltpu.make_async_copy((rows_in, n2, n1, c)[which], stage, lsem.at[0])

    def fetch_back(m):
        some = tokens // len(back)
        return pltpu.make_async_copy(back[m], stage.at[pl.ds(m * some, some), :], lsem.at[m])

    def first_left(act):
        @pl.when(lax.axis_index("section") == 0)
        def _():
            for m in range(len(back)):
                act(fetch_back(m))
        @pl.when(lax.axis_index("section") != 0)
        def _():
            act(fetch_left(0))

    def turn_left(which):
        if which == 0:
            first_left(lambda copy: copy.wait())
        else:
            fetch_left(which).wait()
        for a in range(0, D, 128):
            left[which % 2, a:a + 128, :] = stage[:, a:a + 128].T
        if which < 3:
            fetch_left(which + 1).start()

    def own(k):
        if k >= 2:
            for j in range(R // 2):
                give(0, k - 2, j).wait_send()
        if chunks[k][1] == 0:
            turn_left(chunks[k][0])
            if chunks[k][0] == 2:
                turn_left(3)
        size = chunks[k][2]
        runs = []
        for p in range(R):
            slot, source = factors(k, p)
            if source is None:
                continue
            fetch(k, p).wait()
            if runs and runs[-1][0] == slot:
                runs[-1][2] = p + 1
            else:
                runs.append([slot, p, p + 1])
        for slot, first, end in runs:
            def body(i, carry):
                at = pl.ds(pl.multiple_of(i * 288, 16), 288)
                X[k % 2, at, first * size:end * size] = mul(
                    left[slot, at, :], right[:, first * size:end * size]).astype(X.dtype)
                return carry
            lax.fori_loop(0, full // 288, body, 0)
        if k + 1 < K:
            fetch_all(k + 1)
        for j in range(R // 2):
            give(0, k, j).start()

    def store(level, k, j):
        return held[level].at[j, :, pl.ds(kind[k] if level == L - 1 else every[k], chunks[k][2])]

    def give(level, k, j):
        if level == 0:
            source = X.at[k % 2, :, part_lanes(k, ((r ^ 1) & 1) | (j << 1))]
        else:
            source = store(level - 1, k, 2 * j + (((r >> level) & 1) ^ 1))
        return pltpu.make_async_remote_copy(
            src_ref=source, dst_ref=store(level, k, j), send_sem=send_sem.at[level, k, j],
            recv_sem=recv_sem.at[level, k, j], device_id={"replica": r ^ bits[level]}, device_id_type=MESH)

    STEP = 96

    def merge(level, k):
        for j in range(R >> (level + 1)):
            give(level, k, j).wait_recv()
            mine = store(level, k, j)
            other = X.at[k % 2, :, part_lanes(k, kept(0, j))] if level == 0 else store(level - 1, k, 2 * j + ((r >> level) & 1))

            def body(i, carry):
                at = pl.ds(pl.multiple_of(i * STEP, 16), STEP)
                mine[at, :] = (mine[at, :].astype(F32) + other[at, :].astype(F32)).astype(mine.dtype)
                return carry
            lax.fori_loop(0, full // STEP, body, 0)
        if level + 1 < last(k):
            for j in range(R >> (level + 2)):
                give(level + 1, k, j).start()

    def last(k):
        return L - 1 if ahead_of_pairs(k, L) else L

    def lanes(k):
        return range(2) if ahead_of_pairs(k, L) else range(1)

    def total(k, j):
        return store(L - 2, k, j) if ahead_of_pairs(k, L) else store(L - 1, k, 0)

    def moving(k, side, t, j):
        place = t - 1 if side == 0 else t
        at = pl.ds(kind[k], chunks[k][2])
        return flow_two.at[side, place, j, :, at] if ahead_of_pairs(k, L) else flow.at[side, place, :, at]

    def pass_on(k, t, side, j, source):
        return pltpu.make_async_remote_copy(
            src_ref=source, dst_ref=moving(k, side, t, j), send_sem=zsend.at[k, side, t, j], recv_sem=zrecv.at[k, side, t, j],
            device_id={"fsdp": z + 1 if side == 0 else z - 1}, device_id_type=MESH)

    def launch(k):
        @pl.when(z == 0)
        def _():
            for t in range(n - 1, 0, -1):
                for j in lanes(k):
                    pass_on(k, t, 0, j, total(k, j).at[block(t), :]).start()
        @pl.when(z == n - 1)
        def _():
            for t in range(n - 1):
                for j in lanes(k):
                    pass_on(k, t, 1, j, total(k, j).at[block(t), :]).start()

    RSTEP = 96 if rows % 96 == 0 else 16

    def add_block(target, other, at_other):
        def body(i, carry):
            at = pl.ds(pl.multiple_of(i * RSTEP, 16), RSTEP)
            there = pl.ds(pl.multiple_of(at_other + i * RSTEP, 16), RSTEP)
            target[at, :] = (target[at, :].astype(F32) + other[there, :].astype(F32)).astype(target.dtype)
            return carry
        lax.fori_loop(0, rows // RSTEP, body, 0)

    def flows(k, hop):
        @pl.when(z == hop)
        def _():
            for t in range(n - 1, hop - 1, -1):
                for j in lanes(k):
                    here = moving(k, 0, t, j)
                    pass_on(k, t, 0, j, here).wait_recv()
                    add_block(here, total(k, j), t * rows)
                    if t > hop:
                        pass_on(k, t, 0, j, here).start()
        @pl.when(z == n - 1 - hop)
        def _():
            for t in range(n - hop):
                for j in lanes(k):
                    here = moving(k, 1, t, j)
                    pass_on(k, t, 1, j, here).wait_recv()
                    if t < n - 1 - hop or hop == n - 1:
                        add_block(here, total(k, j), t * rows)
                    if t < n - 1 - hop:
                        pass_on(k, t, 1, j, here).start()
        if hop == n - 1:
            for j in lanes(k):
                @pl.when((z > 0) & (z < n - 1))
                def _():
                    add_block(moving(k, 1, z, j), moving(k, 0, z, j), 0)

    def both_ends(act):
        @pl.when(z < n - 1)
        def _():
            act(1)
        @pl.when(z == n - 1)
        def _():
            act(0)

    def bit(k):
        return (r >> (L - 1)) & 1

    def trade(k, side):
        return pltpu.make_async_remote_copy(
            src_ref=moving(k, side, z, 1 - bit(k)), dst_ref=pair.at[:, pl.ds(kind[k], chunks[k][2])], send_sem=psend.at[k],
            recv_sem=precv.at[k], device_id={"replica": r ^ bits[L - 1]}, device_id_type=MESH)

    def complete(k):
        def act(side):
            trade(k, side).wait_recv()
            add_block(moving(k, side, z, bit(k)), pair.at[:, pl.ds(kind[k], chunks[k][2])], 0)
        both_ends(act)

    def finished(k, p):
        return F.at[group(k), :, columns(k, p)]

    def share(k, p, level, source=None):
        return pltpu.make_async_remote_copy(
            src_ref=finished(k, p) if source is None else source, dst_ref=finished(k, p),
            send_sem=fsend.at[k, p, level], recv_sem=frecv.at[k, p], device_id={"replica": r ^ bits[level]}, device_id_type=MESH)

    def done(k, side):
        return moving(k, side, z, bit(k) if ahead_of_pairs(k, L) else 0)

    def keep(k, side):
        return pltpu.make_async_copy(done(k, side), finished(k, r), fkeep.at[k])

    def publish(k):
        def act(side):
            for level in reversed(range(L)):
                share(k, r, level, done(k, side)).start()
            keep(k, side).start()
        both_ends(act)

    def masks(level):
        found = [0]
        for upper in range(level + 1, L):
            found = found + [m | bits[upper] for m in found]
        return [m | bits[level] for m in found]

    def collect(level, k):
        for mask in masks(level):
            p = r ^ mask
            share(k, p, level).wait_recv()
            for lower in reversed(range(level)):
                share(k, p, lower).start()

    def small_to_z(t):
        return pltpu.make_async_remote_copy(
            src_ref=small_in.at[t], dst_ref=small_z.at[z], send_sem=ss_z.at[t], recv_sem=sr_z.at[z],
            device_id={"fsdp": t}, device_id_type=MESH)

    def small_to_r(p):
        return pltpu.make_async_remote_copy(
            src_ref=small_sum, dst_ref=small_r.at[r], send_sem=ss_r.at[p], recv_sem=sr_r.at[r],
            device_id={"replica": p}, device_id_type=MESH)

    first_left(lambda copy: copy.start())
    fetch_all(0)
    pl.semaphore_wait(barrier, n - 1 + R - 1)
    own_small = pltpu.make_async_copy(small_in.at[z], small_z.at[z], ss_l)
    own_small.start()
    own(0)
    for hop in range(1, n):
        small_to_z(lax.rem(z + hop, n)).start()
    stages = L + n + L
    for turn in range(K + stages - 1):
        for stage_index in [1, 0] + list(range(2, stages)):
            k = turn - stage_index
            if k < 0 or k >= K:
                continue
            hop = stage_index - last(k)
            if stage_index == 0:
                if k > 0:
                    own(k)
            elif stage_index <= last(k):
                merge(stage_index - 1, k)
                if stage_index == last(k):
                    launch(k)
            elif hop < n:
                flows(k, hop)
                if hop == n - 1:
                    if ahead_of_pairs(k, L):
                        both_ends(lambda side: trade(k, side).start())
                    else:
                        publish(k)
            elif stage_index == L + n - 1:
                complete(k)
                publish(k)
            else:
                collect(L - 1 - (stage_index - L - n), k)
        if turn == 1:
            own_small.wait()
            for hop in range(1, n):
                source = lax.rem(z + hop, n)
                pltpu.make_async_remote_copy(
                    src_ref=small_in.at[source], dst_ref=small_z.at[source], send_sem=ss_z.at[source],
                    recv_sem=sr_z.at[source], device_id={"fsdp": source}, device_id_type=MESH).wait_recv()
            together = small_z[0]
            for t in range(1, n):
                together = together + small_z[t]
            small_sum[...] = together
            small_r[r] = together
            for hop in range(1, R):
                small_to_r(lax.rem(r + hop, R)).start()
    for hop in range(1, R):
        p = lax.rem(r + hop, R)
        pltpu.make_async_remote_copy(
            src_ref=small_sum, dst_ref=small_r.at[p], send_sem=ss_r.at[p], recv_sem=sr_r.at[p],
            device_id={"replica": p}, device_id_type=MESH).wait_recv()
    together = small_r[0]
    for p in range(1, R):
        together = together + small_r[p]
    small_out[...] = together
    for hop in range(1, R):
        small_to_r(lax.rem(r + hop, R)).wait_send()
    for hop in range(1, n):
        small_to_z(lax.rem(z + hop, n)).wait_send()
    for k in range(K):
        for level in range(last(k)):
            if level == 0 and k < K - 2:
                continue
            for j in range(R >> (level + 1)):
                give(level, k, j).wait_send()
        for t in range(n):
            for j in lanes(k):
                if t > 0:
                    @pl.when(t > z)
                    def _():
                        pass_on(k, t, 0, j, moving(k, 0, t, j)).wait_send()
                if t < n - 1:
                    @pl.when(t < z)
                    def _():
                        pass_on(k, t, 1, j, moving(k, 1, t, j)).wait_send()
        if ahead_of_pairs(k, L):
            both_ends(lambda side: trade(k, side).wait_send())
        both_ends(lambda side: keep(k, side).wait())
        for level in range(L):
            share(k, r, level).wait_send()
            for mask in masks(level):
                for lower in range(level):
                    share(k, r ^ mask, lower).wait_send()


def reduce_grads(n, R, wide, small, n1, c, n2, rows_in, dqkv, low, du, g, back):
    tokens, D = n1.shape
    rows = D // n
    part = wide // R
    chunks = plan(R, part, D)
    K = len(chunks)
    most = max(size for _, _, size in chunks)
    L = R.bit_length() - 1
    one, two, both = places(chunks, L)[2]
    two = max(two, 128)
    dma = pltpu.SemaphoreType.DMA
    return pl.pallas_call(
        functools.partial(reduce_kernel, n, R, chunks),
        out_shape=(jax.ShapeDtypeStruct((3, rows, wide), HALF),
                   jax.ShapeDtypeStruct(small.shape[1:], small.dtype)),
        in_specs=[pl.BlockSpec(memory_space=pltpu.VMEM)] + [ANY] * (8 + len(back)),
        out_specs=(ANY, pl.BlockSpec(memory_space=pltpu.VMEM)),
        scratch_shapes=[pltpu.VMEM((R >> (level + 1), D, one if level == L - 1 else both), HALF) for level in range(L)] + [
            pltpu.VMEM((2, D, R * most), HALF),
            pltpu.VMEM((2, D, tokens), HALF),
            pltpu.VMEM((tokens, D), HALF),
            pltpu.VMEM((tokens, R * most), HALF),
            pltpu.VMEM((2, n - 1, rows, one), HALF),
            pltpu.VMEM((2, n - 1, 2, rows, two), HALF),
            pltpu.VMEM((rows, two), HALF),
            pltpu.VMEM((n,) + small.shape[1:], small.dtype),
            pltpu.VMEM((R,) + small.shape[1:], small.dtype),
            pltpu.VMEM(small.shape[1:], small.dtype),
            dma((R,)), dma((len(back),)),
            dma((L, K, R // 2)), dma((L, K, R // 2)),
            dma((K, 2, n, 2)), dma((K, 2, n, 2)),
            dma((K,)), dma((K,)),
            dma((K, R, L)), dma((K, R)), dma((K,)),
            dma((n,)), dma((n,)), dma((R,)), dma((R,)), dma(()),
        ],
        compiler_params=pltpu.CompilerParams(collective_id=1, has_side_effects=True, vmem_limit_bytes=62 * 1024 * 1024),
    )(small, n1, c, n2, rows_in, dqkv, low, du, g, *back)


def shifted(value, axis, steps):
    count = lax.axis_size(axis)
    first, last = (max(0, -steps), min(count, count - steps))
    return lax.ppermute(value, axis, [(source, source + steps) for source in range(first, last)])


def pad_columns(value, wide):
    return jnp.pad(value, ((0, 0), (0, wide - value.shape[1])))


def on_device(ends, first_gain, first_shift, qkv_weight, qv_bias, out_weight, out_bias, second_gain, second_shift,
              up_weight, up_bias, down_weight, down_bias):
    n, R = lax.axis_size("fsdp"), lax.axis_size("replica")
    section = lax.axis_index("section")
    at_first = section == 0
    _, images, tok, D = ends.shape
    hidden = up_weight.shape[2]
    piece = D // n
    unit = 128 * R
    filled = -(-hidden // LANES) * LANES
    wide = max(-(-4 * D // unit), -(-filled // unit)) * unit

    G, vec, qb, ub = gather_weights(
        n, R, filled, qkv_weight[0], out_weight[0], pad_columns(up_weight[0], wide), pad_columns(down_weight[0].T, wide),
        (first_gain, first_shift, qv_bias[0], out_bias, second_gain, second_shift, down_bias, up_bias))

    rows = ends[0].reshape(images * tok, D)
    T = images // MICRO * tok
    total = MICRO * T
    parts = [rows[m * T : (m + 1) * T] for m in range(MICRO)]
    here = section.astype(jnp.int32)

    def turn(micro, where):
        return jnp.stack([jnp.int32(micro), (here == where).astype(jnp.int32)])

    kept = (None,) * 9
    sent = []
    for micro in range(MICRO):
        *kept, y = f_layer(turn(micro, 0), total, wide, False, parts[micro], vec, qb, ub, G, tok, kept)
        sent.append(shifted(y, "section", 1))
    for micro in range(MICRO):
        *kept, y = f_layer(turn(micro, 1), total, wide, True, sent[micro], vec, qb, ub, G, tok, kept)
    n1, qkv, probs, c, r1, n2, g, gp, result = kept

    kept = (None, None, None, result)
    back = []
    stats, sums = [], []
    for where in (1, 0):
        for micro in range(MICRO):
            e, x = (parts[micro], sent[micro]) if where else (back[micro], parts[micro])
            *kept, dx, stat, part = d_layer(turn(micro, where), total, wide, where == 0, e, x, vec, G, gp, r1, qkv, probs, tok, kept)
            stats.append(stat)
            sums.append(part)
            if where:
                back.append(shifted(dx, "section", -1))
    du, low, dqkv, result = kept
    stats = sum(jnp.where(at_first, below, above) for above, below in zip(stats[:MICRO], stats[MICRO:]))
    sums = sum(jnp.where(at_first, below, above) for above, below in zip(sums[:MICRO], sums[MICRO:]))

    stats = stats.sum(axis=1)
    vectors = jnp.stack([stats[4], stats[5], stats[6], stats[7], stats[2], stats[0], stats[1], stats[3]])
    vectors = vectors.reshape(8, n, piece).transpose(1, 0, 2).reshape(n, 8 * piece)
    vectors = jnp.concatenate([vectors, sums[0, :hidden].reshape(n, hidden // n)], axis=1)
    lanes = -(-vectors.shape[1] // (16 * 128)) * 128
    small = jnp.pad(vectors, ((0, 0), (0, 16 * lanes - vectors.shape[1]))).reshape(n, 16, lanes)
    F, s = reduce_grads(n, R, wide, small, n1, c, n2, rows, dqkv, low, du, g, back)
    s = s.reshape(-1)
    v = s[: 8 * piece].reshape(8, piece)
    return (
        result.reshape(1, images, tok, D),
        v[0][None],
        v[1][None],
        F[0, :, : 3 * D].astype(F32)[None],
        v[2:4][None],
        F[0, :, 3 * D : 4 * D].astype(F32)[None],
        v[4][None],
        v[5][None],
        v[6][None],
        F[1, :, :hidden].astype(F32)[None],
        s[8 * piece : 8 * piece + hidden // n][None],
        F[2, :, :hidden].T.astype(F32)[None],
        v[7][None],
    )


def solution(mesh):
    placed = (
        P("section", ("fsdp", "replica"), None, None),
        P("section", "fsdp"),
        P("section", "fsdp"),
        P("section", "fsdp", None),
        P("section", None, "fsdp"),
        P("section", "fsdp", None),
        P("section", "fsdp"),
        P("section", "fsdp"),
        P("section", "fsdp"),
        P("section", "fsdp", None),
        P("section", "fsdp"),
        P("section", None, "fsdp"),
        P("section", "fsdp"),
    )
    return jax.shard_map(on_device, mesh=mesh, in_specs=placed, out_specs=placed, check_vma=False)
```

```python
import functools
import math

import jax
import jax.numpy as jnp
from jax import lax
from jax.experimental import pallas as pl
from jax.experimental.pallas import tpu as pltpu
from jax.sharding import PartitionSpec as P

MESH = pl.DeviceIdType.MESH
HEADS = 16
HEAD_DIM = 72
MICRO = 3
F32 = jnp.float32
HALF = jnp.bfloat16
EPS = 1e-06
ANY = pl.BlockSpec(memory_space=pl.ANY)
NN = (((1,), (0,)), ((), ()))
NT = (((1,), (1,)), ((), ()))
TN = (((0,), (0,)), ((), ()))
FOLD = 8


def mul(left, right, dims=NN):
    return lax.dot_general(left, right, dims, preferred_element_type=F32)


def row_loop(count, step, body):
    def run(i, carry):
        body(pl.ds(pl.multiple_of(i * step, step), step))
        return carry
    lax.fori_loop(0, count // step, run, 0)


def normal(value):
    center = value - jnp.mean(value, axis=-1, keepdims=True)
    scale = lax.rsqrt(jnp.mean(center * center, axis=-1, keepdims=True) + EPS)
    return center * scale, scale


def fold(value):
    return value.reshape(value.shape[0] // 8, 8, value.shape[1]).sum(axis=0)


def norm_back(value, grad, gain):
    hat, scale = normal(value)
    d = grad * gain
    low = d - jnp.mean(d, axis=-1, keepdims=True) - hat * jnp.mean(d * hat, axis=-1, keepdims=True)
    return low * scale, hat


def params(limit=56, **kw):
    return pltpu.CompilerParams(vmem_limit_bytes=limit * 1024 * 1024, **kw)


def shape(rows, columns, dtype):
    return jax.ShapeDtypeStruct((rows, columns), dtype)


def spans(h):
    a, b = h * HEAD_DIM, (h + 1) * HEAD_DIM
    lo = a // 128 * 128
    hi = -(-b // 128) * 128
    return a, b, lo, hi

def head_mask(h, rows):
    a, b, lo, hi = spans(h)
    lane = lax.broadcasted_iota(jnp.int32, (rows, hi - lo), 1) + lo
    return (lane >= a) & (lane < b)

FOLD = 8


def attn_image(qkv, P, c, D, tok, factor):
    for first in range(0, HEADS, FOLD):
        heads = range(first, first + FOLD)
        held = []
        for h in heads:
            a, b, lo, hi = spans(h)
            held.append(mul(qkv[:, D + lo:D + hi], jnp.where(head_mask(h, tok), qkv[:, lo:hi], 0), NT))
        probs = []
        for h, s in zip(heads, held):
            e = jnp.exp2((s - jnp.max(s, axis=0, keepdims=True)) * factor)
            p = (e * (1.0 / jnp.sum(e, axis=0, keepdims=True))).astype(HALF)
            P[h] = p
            probs.append(p)
        for h, p in zip(heads, probs):
            a, b, lo, hi = spans(h)
            o = mul(p, qkv[:, 2 * D + lo:2 * D + hi], TN).astype(HALF)
            c[:, lo:hi] = jnp.where(head_mask(h, tok), o, c[:, lo:hi]) if a > lo else o


def attn_back_image(qkv, P, dc, out, D, tok, factor):
    for first in range(0, HEADS, FOLD):
        heads = range(first, first + FOLD)
        held = []
        for h in heads:
            a, b, lo, hi = spans(h)
            held.append(mul(qkv[:, 2 * D + lo:2 * D + hi], jnp.where(head_mask(h, tok), dc[:, lo:hi], 0), NT))
        grads = []
        for h, dp in zip(heads, held):
            wide = P[h].astype(F32)
            grads.append((wide * (dp - jnp.sum(wide * dp, axis=0, keepdims=True)) * factor).astype(HALF))
        for h, ds in zip(heads, grads):
            a, b, lo, hi = spans(h)
            mask = head_mask(h, tok)
            dv = mul(P[h], dc[:, lo:hi]).astype(HALF)
            dk = mul(ds, qkv[:, lo:hi]).astype(HALF)
            dq = mul(ds, qkv[:, D + lo:D + hi], TN).astype(HALF)
            for base, value in ((0, dq), (D, dk), (2 * D, dv)):
                at = slice(base + lo, base + hi)
                out[:, at] = jnp.where(mask, value, out[:, at]) if a > lo else value


TILE = 512
LANES = 256


def pieces(width, step):
    return [(a, min(step, width - a)) for a in range(0, width, step)]


def tiles(width, step, body):
    whole = width // step
    def run(i, carry):
        body(pl.multiple_of(i * step, step), step)
        return carry
    lax.fori_loop(0, whole, run, 0)
    if width % step:
        body(whole * step, width % step)


def f_layer(slots, total, final, x, vec, qb, ub, G, base, tok, kept):
    T, D = x.shape
    hidden = ub.shape[1]
    images = T // tok
    factor = HEAD_DIM ** (-0.5) * math.log2(math.e)
    root = math.sqrt(2.0 / math.pi)
    cut = pieces(4 * D, 768)
    plain, spare = 5, sum(b is not None for b in kept)
    chunk = T // 2 if T % 32 == 0 else T

    def kernel(slot, *refs):
        @pl.when(slot[1] == 1)
        def _():
            work(slot, *refs)

    def work(slot, *refs):
        x_in, vec, qb, ub, G = refs[:plain]
        (n1o, qkvo, Po, co, r1o, n2o, go, gpo, reso, y,
         x, wa, wb, n1, qkv, P, c, r1, n2, g, gp, res, wsem, psem, gsem, osem) = refs[plain + spare:]
        save = pl.ds(pl.multiple_of(slot[0] * T, 16), T)

        def weight(j):
            a, w = cut[j]
            return pltpu.make_async_copy(G.at[:, pl.ds(a, w)], wa.at[:, pl.ds(a, w)], wsem.at[j])
        up = pltpu.make_async_copy(G.at[:, pl.ds(base, hidden)], wb, wsem.at[len(cut)])
        down = pltpu.make_async_copy(G.at[:, pl.ds(base + hidden, hidden)], wa.at[:, pl.ds(0, hidden)], wsem.at[len(cut) + 1])
        tokens = pltpu.make_async_copy(x_in, x, wsem.at[len(cut) + 2])
        tokens.start()
        for j in range(len(cut)):
            weight(j).start()
        up.start()

        def out(source, target, at, k):
            return pltpu.make_async_copy(source, target.at[at], osem.at[k])
        outs = [out(n1, n1o, save, 0), out(qkv, qkvo, save, 1), out(c, co, save, 2), out(r1, r1o, save, 3),
                out(n2, n2o, save, 4), out(g, go, save, 5)]
        if final:
            outs.append(out(res, reso, save, 6))

        def first(at):
            n1[at, :] = (normal(x[at, :].astype(F32))[0] * vec[0:1, :] + vec[1:2, :]).astype(HALF)
        tokens.wait()
        row_loop(T, tok, first)
        outs[0].start()
        for j, (a, w) in enumerate(cut):
            weight(j).wait()
            if a < 3 * D:
                b = min(a + w, 3 * D)
                qkv[:, a:b] = (mul(n1[...], wa[:, a:b]) + qb[:, a:b]).astype(HALF)
        outs[1].start()

        def probs(i):
            return pltpu.make_async_copy(P.at[i % 2], Po.at[slot[0] * images + i], psem.at[i % 2])

        def image(i, carry):
            @pl.when(i >= 2)
            def _():
                probs(i - 2).wait()
            rows = pl.ds(pl.multiple_of(i * tok, 16), tok)
            attn_image(qkv.at[rows], P.at[i % 2], c.at[rows], D, tok, factor)
            probs(i).start()
            return carry
        lax.fori_loop(0, images, image, 0)
        outs[2].start()
        r1[...] = mul(c[...], wa[:, 3 * D:4 * D])
        down.start()

        def second(at):
            value = r1[at, :] + vec[4:5, :] + x[at, :].astype(F32)
            r1[at, :] = value
            n2[at, :] = (normal(value)[0] * vec[5:6, :] + vec[6:7, :]).astype(HALF)
        row_loop(T, tok, second)
        outs[3].start()
        outs[4].start()
        up.wait()

        def slope(i, size):
            return pltpu.make_async_copy(
                gp.at[lax.rem(i, 2), :, pl.ds(0, size)], gpo.at[save, pl.ds(pl.multiple_of(i * TILE, 128), size)],
                gsem.at[lax.rem(i, 2)])

        def rise(start, size):
            i = start // TILE
            @pl.when(i >= 2)
            def _():
                slope(i - 2, TILE).wait()
            at = pl.ds(start, size)
            for a in range(0, T, chunk):
                u = mul(n2[a:a + chunk, :], wb[:, at]) + ub[:, at]
                square = u * u
                t = jnp.tanh(u * (root + (root * 0.044715) * square))
                half = 0.5 + 0.5 * t
                g[a:a + chunk, at] = (u * half).astype(HALF)
                gp[lax.rem(i, 2), a:a + chunk, 0:size] = (
                    half + (0.5 * u) * (1.0 - t * t) * (root + (3.0 * root * 0.044715) * square)).astype(HALF)
            slope(i, size).start()
        tiles(hidden, TILE, rise)
        outs[5].start()
        down.wait()
        for a, w in pieces(D, LANES):
            at = slice(a, a + w)
            value = mul(g[...], wa[a:a + w, 0:hidden], NT) + (r1[:, at] + vec[7:8, at])
            if final:
                res[:, at] = value
            y[:, at] = value.astype(HALF)
        if final:
            outs[6].start()
        for copy in outs:
            copy.wait()
        for i in range(max(0, images - 2), images):
            probs(i).wait()
        count = -(-hidden // TILE)
        for i in range(max(0, count - 2), count):
            slope(i, min(TILE, hidden - i * TILE)).wait()

    aliases = {}
    ins = [x, vec, qb, ub, G]
    for index, buffer in enumerate(kept):
        if buffer is not None:
            aliases[1 + len(ins)] = index
            ins.append(buffer)
    dma = pltpu.SemaphoreType.DMA
    whole = pl.BlockSpec(memory_space=pltpu.VMEM)
    return pl.pallas_call(
        kernel,
        out_shape=(shape(total, D, HALF), shape(total, 3 * D, HALF),
                   jax.ShapeDtypeStruct((total // tok, HEADS, tok, tok), HALF), shape(total, D, HALF), shape(total, D, F32),
                   shape(total, D, HALF), shape(total, hidden, HALF), shape(total, hidden, HALF), shape(total, D, F32),
                   shape(T, D, HALF)),
        grid_spec=pltpu.PrefetchScalarGridSpec(
            num_scalar_prefetch=1, grid=(1,), in_specs=[ANY] + [whole] * 3 + [ANY] + [ANY] * spare, out_specs=(ANY,) * 9 + (whole,),
            scratch_shapes=[
                pltpu.VMEM((T, D), HALF), pltpu.VMEM((D, 4 * D), HALF), pltpu.VMEM((D, hidden), HALF), pltpu.VMEM((T, D), HALF),
                pltpu.VMEM((T, 3 * D), HALF), pltpu.VMEM((2, HEADS, tok, tok), HALF), pltpu.VMEM((T, D), HALF),
                pltpu.VMEM((T, D), F32), pltpu.VMEM((T, D), HALF), pltpu.VMEM((T, hidden), HALF),
                pltpu.VMEM((2, T, TILE), HALF), pltpu.VMEM((T, D), F32),
                dma((len(cut) + 3,)), dma((2,)), dma((2,)), dma((7,))]),
        input_output_aliases=aliases,
        compiler_params=params(60),
        cost_estimate=pl.CostEstimate(flops=T * D, bytes_accessed=T * D, transcendentals=0),
    )(slots, *ins)


def d_layer(slots, total, final, e, x, vec, G, base, GP, R1, QKV, PP, tok, kept):
    T, D = x.shape
    hidden = GP.shape[1]
    images = T // tok
    scale = HEAD_DIM ** (-0.5)
    plain, spare = 8, sum(b is not None for b in kept)
    chunk = T // 2 if T % 32 == 0 else T

    def kernel(slot, *refs):
        @pl.when(slot[1] == 1)
        def _():
            work(slot, *refs)

    def work(slot, *refs):
        e_in, x_in, vec, G, GP, R1, QKV, PP = refs[:plain]
        (duo, lowo, dqkvo, reso, dx, stats, sums,
         e, x, wa, wb, gp, r1, qkv, P, du, grad, dr1, low, dc, dqkv, wsem, psem, isem, osem) = refs[plain + spare:]
        save = pl.ds(pl.multiple_of(slot[0] * T, 16), T)
        cuts = pieces(hidden, 2 * TILE)
        down = [pltpu.make_async_copy(G.at[:, pl.ds(base + hidden + a, w)], wa.at[:, pl.ds(a, w)], wsem.at[2 + j]) for j, (a, w) in enumerate(cuts)]
        slope = [pltpu.make_async_copy(GP.at[save, pl.ds(a, w)], gp.at[:, pl.ds(a, w)], isem.at[2 + j]) for j, (a, w) in enumerate(cuts)]
        up = pltpu.make_async_copy(G.at[:, pl.ds(base, hidden)], wb, wsem.at[0])
        rest = pltpu.make_async_copy(G.at[:, pl.ds(0, 4 * D)], wa, wsem.at[1])
        loads = [pltpu.make_async_copy(R1.at[save], r1, isem.at[0]), pltpu.make_async_copy(QKV.at[save], qkv, isem.at[1])]
        count = len(cuts)
        cotangent = pltpu.make_async_copy(e_in, e, isem.at[2 + count])
        tokens = pltpu.make_async_copy(x_in, x, isem.at[3 + count])
        cotangent.start()
        for weight, factor in zip(down, slope):
            weight.start()
            factor.start()
        up.start()
        tokens.start()
        for copy in loads:
            copy.start()

        def out(source, target, at, k):
            return pltpu.make_async_copy(source, target.at[at], osem.at[k])
        outs = [out(du, duo, save, 0), out(low, lowo, save, 1), out(dqkv, dqkvo, save, 2)]
        if final:
            outs.append(out(dr1, reso, save, 3))

        def probs(i):
            return pltpu.make_async_copy(PP.at[slot[0] * images + i], P.at[i % 2], psem.at[i % 2])
        for i in range(min(2, images)):
            probs(i).start()
        stats[...] = jnp.zeros_like(stats)

        def fall(start, size):
            at = pl.ds(start, size)
            total = None
            for a in range(0, T, chunk):
                d = (mul(e[a:a + chunk, :], wa[:, at]) * gp[a:a + chunk, at].astype(F32)).astype(HALF)
                du[a:a + chunk, at] = d
                part = jnp.sum(d.astype(F32), axis=0, keepdims=True)
                total = part if total is None else total + part
            sums[:, at] = total
        cotangent.wait()
        for j, (a, w) in enumerate(cuts):
            down[j].wait()
            slope[j].wait()
            for b in range(a, a + w, TILE):
                fall(b, min(TILE, a + w - b))
        rest.start()
        outs[0].start()
        up.wait()
        for a, w in pieces(D, LANES):
            grad[:, a:a + w] = mul(du[...], wb[a:a + w, :], NT)
        loads[0].wait()

        def second(at):
            g = grad[at, :]
            part, hat = norm_back(r1[at, :], g, vec[5:6, :])
            eb = e[at, :].astype(F32)
            value = eb + part
            rounded = value.astype(HALF)
            dr1[at, :] = value
            low[at, :] = rounded
            stats[0] += fold(g * hat)
            stats[1] += fold(g)
            stats[2] += fold(rounded.astype(F32))
            stats[3] += fold(eb)
        row_loop(T, tok, second)
        outs[1].start()
        rest.wait()
        for a, w in pieces(D, LANES):
            dc[:, a:a + w] = mul(low[...], wa[a:a + w, 3 * D:4 * D], NT).astype(HALF)
        loads[1].wait()

        def image(i, carry):
            probs(i).wait()
            rows = pl.ds(pl.multiple_of(i * tok, 16), tok)
            attn_back_image(qkv.at[rows], P.at[i % 2], dc.at[rows], dqkv.at[rows], D, tok, scale)
            @pl.when(i + 2 < images)
            def _():
                probs(i + 2).start()
            return carry
        lax.fori_loop(0, images, image, 0)
        outs[2].start()
        tokens.wait()
        for a, w in pieces(D, LANES):
            grad[:, a:a + w] = mul(dqkv[...], wa[a:a + w, 0:3 * D], NT)

        def first(at):
            g = grad[at, :]
            part, hat = norm_back(x[at, :].astype(F32), g, vec[0:1, :])
            value = dr1[at, :] + part
            dr1[at, :] = value
            dx[at, :] = value.astype(HALF)
            stats[4] += fold(g * hat)
            stats[5] += fold(g)
            stats[6] += fold(dqkv[at, 0:D].astype(F32))
            stats[7] += fold(dqkv[at, 2 * D:3 * D].astype(F32))
        row_loop(T, tok, first)
        if final:
            outs[3].start()
        for copy in outs:
            copy.wait()

    aliases = {}
    ins = [e, x, vec, G, GP, R1, QKV, PP]
    for index, buffer in enumerate(kept):
        if buffer is not None:
            aliases[1 + len(ins)] = index
            ins.append(buffer)
    dma = pltpu.SemaphoreType.DMA
    whole = pl.BlockSpec(memory_space=pltpu.VMEM)
    return pl.pallas_call(
        kernel,
        out_shape=(shape(total, hidden, HALF), shape(total, D, HALF), shape(total, 3 * D, HALF), shape(total, D, F32),
                   shape(T, D, HALF), jax.ShapeDtypeStruct((8, 8, D), F32), shape(1, hidden, F32)),
        grid_spec=pltpu.PrefetchScalarGridSpec(
            num_scalar_prefetch=1, grid=(1,), in_specs=[ANY] * 2 + [whole] + [ANY] + [ANY] * (4 + spare), out_specs=(ANY,) * 4 + (whole,) * 3,
            scratch_shapes=[
                pltpu.VMEM((T, D), HALF), pltpu.VMEM((T, D), HALF),
                pltpu.VMEM((D, 4 * D), HALF), pltpu.VMEM((D, hidden), HALF), pltpu.VMEM((T, hidden), HALF),
                pltpu.VMEM((T, D), F32), pltpu.VMEM((T, 3 * D), HALF), pltpu.VMEM((2, HEADS, tok, tok), HALF),
                pltpu.VMEM((T, hidden), HALF), pltpu.VMEM((T, D), F32), pltpu.VMEM((T, D), F32), pltpu.VMEM((T, D), HALF),
                pltpu.VMEM((T, D), HALF), pltpu.VMEM((T, 3 * D), HALF),
                dma((2 + len(pieces(hidden, 2 * TILE)),)), dma((2,)), dma((4 + len(pieces(hidden, 2 * TILE)),)), dma((4,))]),
        input_output_aliases=aliases,
        compiler_params=params(60),
        cost_estimate=pl.CostEstimate(flops=T * D, bytes_accessed=T * D, transcendentals=0),
    )(slots, *ins)


def powers(count):
    bits = []
    bit = count // 2
    while bit:
        bits.append(bit)
        bit //= 2
    return bits

def gather_kernel(n, R, halves, qkv, out, up, down, *refs):
    (gain_one, shift_one, bias_qv, bias_out, gain_two, shift_two, bias_down, bias_up,
     G, vec, qb, ub, stage_a, stage_b, S, lsem, ssem, rsem, small_send, small_recv) = refs
    z = lax.axis_index("fsdp")
    r = lax.axis_index("replica")
    rows, filled = up.shape
    stage = (stage_a, stage_b)
    part = [ref.shape[1] // R for ref in stage]
    base = (0, stage_a.shape[1])
    some = rows // halves
    bits = powers(R)
    barrier = pltpu.get_barrier_semaphore()
    for hop in range(1, n):
        pl.semaphore_signal(barrier, inc=1, device_id={"fsdp": lax.rem(z + hop, n)}, device_id_type=MESH)
    for bit in bits:
        pl.semaphore_signal(barrier, inc=1, device_id={"replica": r ^ bit}, device_id_type=MESH)
    mine = pl.ds(pl.multiple_of(z * rows, 16), rows)
    first = qkv.shape[1]
    local = [
        pltpu.make_async_copy(qkv, stage_a.at[:, pl.ds(0, first)], lsem.at[0]),
        pltpu.make_async_copy(out, stage_a.at[:, pl.ds(first, out.shape[1])], lsem.at[1]),
        pltpu.make_async_copy(up, stage_b.at[:, pl.ds(0, filled)], lsem.at[2]),
        pltpu.make_async_copy(down, stage_b.at[:, pl.ds(filled, filled)], lsem.at[3]),
    ]
    for copy in local:
        copy.start()
    keep = [pltpu.make_async_copy(stage[group], G.at[mine, pl.ds(base[group], stage[group].shape[1])], lsem.at[4 + group]) for group in range(2)]

    for row, value in enumerate((gain_one, shift_one, None, None, bias_out, gain_two, shift_two, bias_down, bias_up)):
        value = bias_qv[row - 2:row - 1, :] if value is None else value[...]
        S[z, row:row + 1, 0:value.shape[1]] = value.astype(F32)
    pl.semaphore_wait(barrier, n - 1 + len(bits))

    def piece(unit, source, column):
        group, half = unit // halves, unit % halves
        return G.at[pl.ds(pl.multiple_of(source * rows + half * some, 16), some),
                    pl.ds(pl.multiple_of(base[group] + column * part[group], 128), part[group])]

    def send(unit, source, column, kind, target, origin=None):
        return pltpu.make_async_remote_copy(
            src_ref=piece(unit, source, column) if origin is None else origin, dst_ref=piece(unit, source, column),
            send_sem=ssem.at[unit, source, column, kind], recv_sem=rsem.at[unit, source, column],
            device_id=target, device_id_type=MESH)

    def to_right(unit, source, origin=None):
        return send(unit, source, r, 0, {"fsdp": z + 1}, origin)

    def to_left(unit, source, origin=None):
        return send(unit, source, r, 1, {"fsdp": z - 1}, origin)

    def own(unit):
        wide = part[unit // halves]
        return stage[unit // halves].at[pl.ds(unit % halves * some, some), pl.ds(pl.multiple_of(r * wide, 128), wide)]

    def share(unit, source, column, level):
        return send(unit, source, column, 2 + level, {"replica": r ^ bits[level]})

    def arrived(unit, source, column):
        send(unit, source, column, 0, {"replica": r ^ bits[0]}).wait_recv()

    def small_to(hop):
        return pltpu.make_async_remote_copy(
            src_ref=S.at[z], dst_ref=S.at[z], send_sem=small_send.at[hop],
            recv_sem=small_recv.at[z], device_id={"fsdp": lax.rem(z + hop, n)}, device_id_type=MESH)
    for hop in range(1, n):
        small_to(hop).start()
    order = [0] + list(range(halves, 2 * halves)) + list(range(1, halves))
    for unit in order:
        group = unit // halves
        if unit % halves == 0:
            local[2 * group].wait()
            local[2 * group + 1].wait()
            keep[group].start()
        @pl.when(z + 1 < n)
        def _():
            to_right(unit, z, own(unit)).start()
        @pl.when(z > 0)
        def _():
            to_left(unit, z, own(unit)).start()
    columns = {}
    for level, bit in enumerate(bits):
        masks = [0]
        for upper in bits[:level]:
            masks = masks + [m | upper for m in masks]
        columns[level] = [bit | m for m in masks]
    units = 2 * halves
    steps = [(hop, unit) for hop in range(1, n) for unit in order]
    for turn in range(len(steps) + len(bits)):
        for level in range(-1, len(bits)):
            place = turn - 1 - level
            if place < 0 or place >= len(steps):
                continue
            hop, unit = steps[place]
            for sign in (-1, 1):
                source = z + sign * hop
                @pl.when((source >= 0) & (source < n))
                def _():
                    if level < 0:
                        arrived(unit, source, r)
                        for lower in range(len(bits)):
                            share(unit, source, r, lower).start()
                        if sign < 0:
                            @pl.when(z + 1 < n)
                            def _():
                                to_right(unit, source).start()
                        else:
                            @pl.when(z > 0)
                            def _():
                                to_left(unit, source).start()
                    else:
                        for mask in columns[level]:
                            arrived(unit, source, r ^ mask)
                            for lower in range(level + 1, len(bits)):
                                share(unit, source, r ^ mask, lower).start()
    for copy in keep:
        copy.wait()
    for hop in range(1, n):
        source = lax.rem(z + hop, n)
        pltpu.make_async_remote_copy(
            src_ref=S.at[source], dst_ref=S.at[source], send_sem=small_send.at[hop],
            recv_sem=small_recv.at[source], device_id={"fsdp": source}, device_id_type=MESH).wait_recv()
        small_to(hop).wait_send()
    D = vec.shape[1]
    few = bias_up.shape[1]
    ub[...] = jnp.zeros_like(ub)
    for source in range(n):
        vec[:, source * rows:(source + 1) * rows] = S[source, 0:8, 0:rows]
        ub[:, source * few:(source + 1) * few] = S[source, 8:9, 0:few]
    qb[:, 0:D] = vec[2:3, :]
    qb[:, D:2 * D] = jnp.zeros((1, D), F32)
    qb[:, 2 * D:3 * D] = vec[3:4, :]
    for unit in range(units):
        for source in range(n):
            @pl.when((source <= z) & (z + 1 < n))
            def _():
                to_right(unit, source).wait_send()
            @pl.when((source >= z) & (z > 0))
            def _():
                to_left(unit, source).wait_send()
            @pl.when(source != z)
            def _():
                for level in range(len(bits)):
                    share(unit, source, r, level).wait_send()
                for level in range(len(bits)):
                    for mask in columns[level]:
                        for lower in range(level + 1, len(bits)):
                            share(unit, source, r ^ mask, lower).wait_send()


def gather_weights(n, R, wide, filled, qkv, out, up, down, vectors):
    rows = up.shape[0]
    kinds = 2 + len(powers(R))
    halves = 3 if rows % 48 == 0 else 1
    lanes = -(-max(v.shape[1] for v in vectors) // 128) * 128
    dma = pltpu.SemaphoreType.DMA
    whole = pl.BlockSpec(memory_space=pltpu.VMEM)
    D = n * rows
    return pl.pallas_call(
        functools.partial(gather_kernel, n, R, halves),
        out_shape=(shape(D, sum(wide), HALF), shape(8, D, F32), shape(1, 3 * D, F32),
                   shape(1, filled, F32)),
        in_specs=[ANY] * 4 + [whole] * len(vectors),
        out_specs=(ANY,) + (whole,) * 3,
        scratch_shapes=[
            pltpu.VMEM((rows, wide[0]), HALF),
            pltpu.VMEM((rows, wide[1]), HALF),
            pltpu.VMEM((n, 16, lanes), F32),
            dma((6,)),
            dma((2 * halves, n, R, kinds)),
            dma((2 * halves, n, R)),
            dma((n,)),
            dma((n,)),
        ],
        compiler_params=pltpu.CompilerParams(collective_id=0, has_side_effects=True, vmem_limit_bytes=32 * 1024 * 1024),
    )(qkv, out, up, down, *vectors)


ORDER = (1, 0)
SCRATCH = 26


def plan(R, parts, D, filled):
    found = []
    for place, group in enumerate(ORDER):
        edges = (filled, 2 * filled) if group else (3 * D, 4 * D)
        part = parts[group]
        sizes, at = [], 0
        while at < part:
            size = min(max(12 // R, 1) * 128, part - at)
            while any(p * part + at < edge < p * part + at + size for p in range(R) for edge in edges):
                size -= 128
            sizes.append(size)
            at += size
        if place == 0 and sizes[0] == 384:
            sizes[:1] = [128, 256]
        if place == 1 and sizes[-1] > 128:
            sizes[-1:] = [sizes[-1] - 128, 128]
        at = 0
        for size in sizes:
            found.append((place, at, size))
            at += size
    return found


def ahead_of_pairs(k, L):
    return L >= 2 and k % 3 == 2


def places(chunks, L):
    every, kind, counts = [], [], [0, 0, 0]
    for k, (_, _, size) in enumerate(chunks):
        which = int(ahead_of_pairs(k, L))
        every.append(counts[2])
        kind.append(counts[which])
        counts[which] += size
        counts[2] += size
    return every, kind, counts


def reduce_kernel(n, R, chunks, small_in, n1, c, n2, rows_in, dqkv, low, du, g, *refs):
    back = refs[:-3 - SCRATCH - (R.bit_length() - 1)]
    F_a, F_b, small_out, *scratch = refs[len(back):]
    F = (F_a, F_b)
    L = R.bit_length() - 1
    bits = [1 << level for level in range(L)]
    held = scratch[:L]
    (X, left, stage, right, flow, flow_two, pair, small_z, small_r, small_sum, rsem, lsem, send_sem, recv_sem, zsend, zrecv,
     psend, precv, fsend, frecv, fkeep, ss_z, sr_z, ss_r, sr_r, ss_l) = scratch[L:]
    z = lax.axis_index("fsdp")
    r = lax.axis_index("replica")
    tokens, D = n1.shape
    full = D
    rows = full // n
    filled = g.shape[1]
    part = [ref.shape[1] // R for ref in F]
    K = len(chunks)
    every, kind, _ = places(chunks, L)
    barrier = pltpu.get_barrier_semaphore()
    for hop in range(1, n):
        pl.semaphore_signal(barrier, inc=1, device_id={"fsdp": lax.rem(z + hop, n)}, device_id_type=MESH)
    for hop in range(1, R):
        pl.semaphore_signal(barrier, inc=1, device_id={"replica": lax.rem(r + hop, R)}, device_id_type=MESH)

    def group(k):
        return ORDER[chunks[k][0]]

    def columns(k, p):
        return pl.ds(pl.multiple_of(p * part[group(k)] + chunks[k][1], 128), chunks[k][2])

    def part_lanes(k, p):
        return pl.ds(pl.multiple_of(p * chunks[k][2], 128), chunks[k][2])

    def block(t):
        return pl.ds(pl.multiple_of(t * rows, 16), rows)

    def kept(level, j):
        return (r & ((2 << level) - 1)) | (j << (level + 1))

    def factors(k, p):
        a, sub = p * part[group(k)] + chunks[k][1], chunks[k][2]
        if group(k) == 1:
            if a < filled:
                return 1, du.at[:, pl.ds(a, sub)]
            if a < 2 * filled:
                return 0, g.at[:, pl.ds(a - filled, sub)]
            return None, None
        if a < 3 * D:
            return 0, dqkv.at[:, pl.ds(a, sub)]
        if a < 4 * D:
            return 1, low.at[:, pl.ds(a - 3 * D, sub)]
        return None, None

    def fetch(k, p):
        return pltpu.make_async_copy(factors(k, p)[1], right.at[:, pl.ds(p * chunks[k][2], chunks[k][2])], rsem.at[p])

    def fetch_all(k):
        for p in range(R):
            if factors(k, p)[1] is not None:
                fetch(k, p).start()

    def fetch_left(which):
        return pltpu.make_async_copy((rows_in, n2, n1, c)[which], stage.at[which % 2], lsem.at[which])

    def fetch_back(m):
        some = tokens // len(back)
        return pltpu.make_async_copy(back[m], stage.at[0, pl.ds(m * some, some), :], lsem.at[4 + m])

    def first_left(act):
        @pl.when(lax.axis_index("section") == 0)
        def _():
            for m in range(len(back)):
                act(fetch_back(m))
        @pl.when(lax.axis_index("section") != 0)
        def _():
            act(fetch_left(0))

    def turn_left(which):
        if which == 0:
            first_left(lambda copy: copy.wait())
        else:
            fetch_left(which).wait()
        for a in range(0, D, 128):
            left[which % 2, a:a + 128, :] = stage[which % 2, :, a:a + 128].T
        if which < 2:
            fetch_left(which + 2).start()

    def own(k):
        if k >= 2:
            for j in range(R // 2):
                give(0, k - 2, j).wait_send()
        if chunks[k][1] == 0:
            turn_left(2 * chunks[k][0])
            turn_left(2 * chunks[k][0] + 1)
        size = chunks[k][2]
        runs = []
        for p in range(R):
            slot, source = factors(k, p)
            if source is None:
                continue
            fetch(k, p).wait()
            if runs and runs[-1][0] == slot:
                runs[-1][2] = p + 1
            else:
                runs.append([slot, p, p + 1])
        for slot, first, end in runs:
            def body(i, carry):
                at = pl.ds(pl.multiple_of(i * 288, 16), 288)
                X[k % 2, at, first * size:end * size] = mul(
                    left[slot, at, :], right[:, first * size:end * size]).astype(X.dtype)
                return carry
            lax.fori_loop(0, full // 288, body, 0)
        if k + 1 < K:
            fetch_all(k + 1)
        for j in range(R // 2):
            give(0, k, j).start()

    def store(level, k, j):
        return held[level].at[j, :, pl.ds(kind[k] if level == L - 1 else every[k], chunks[k][2])]

    def give(level, k, j):
        if level == 0:
            source = X.at[k % 2, :, part_lanes(k, ((r ^ 1) & 1) | (j << 1))]
        else:
            source = store(level - 1, k, 2 * j + (((r >> level) & 1) ^ 1))
        return pltpu.make_async_remote_copy(
            src_ref=source, dst_ref=store(level, k, j), send_sem=send_sem.at[level, k, j],
            recv_sem=recv_sem.at[level, k, j], device_id={"replica": r ^ bits[level]}, device_id_type=MESH)

    STEP = 96

    def merge(level, k):
        for j in range(R >> (level + 1)):
            give(level, k, j).wait_recv()
            mine = store(level, k, j)
            other = X.at[k % 2, :, part_lanes(k, kept(0, j))] if level == 0 else store(level - 1, k, 2 * j + ((r >> level) & 1))

            def body(i, carry):
                at = pl.ds(pl.multiple_of(i * STEP, 16), STEP)
                mine[at, :] = (mine[at, :].astype(F32) + other[at, :].astype(F32)).astype(mine.dtype)
                return carry
            lax.fori_loop(0, full // STEP, body, 0)
        if level + 1 < last(k):
            for j in range(R >> (level + 2)):
                give(level + 1, k, j).start()

    def last(k):
        return L - 1 if ahead_of_pairs(k, L) else L

    def lanes(k):
        return range(2) if ahead_of_pairs(k, L) else range(1)

    def total(k, j):
        return store(L - 2, k, j) if ahead_of_pairs(k, L) else store(L - 1, k, 0)

    def moving(k, side, t, j):
        place = t - 1 if side == 0 else t
        at = pl.ds(kind[k], chunks[k][2])
        return flow_two.at[side, place, j, :, at] if ahead_of_pairs(k, L) else flow.at[side, place, :, at]

    def pass_on(k, t, side, j, source):
        return pltpu.make_async_remote_copy(
            src_ref=source, dst_ref=moving(k, side, t, j), send_sem=zsend.at[k, side, t, j], recv_sem=zrecv.at[k, side, t, j],
            device_id={"fsdp": z + 1 if side == 0 else z - 1}, device_id_type=MESH)

    def launch(k):
        @pl.when(z == 0)
        def _():
            for t in range(n - 1, 0, -1):
                for j in lanes(k):
                    pass_on(k, t, 0, j, total(k, j).at[block(t), :]).start()
        @pl.when(z == n - 1)
        def _():
            for t in range(n - 1):
                for j in lanes(k):
                    pass_on(k, t, 1, j, total(k, j).at[block(t), :]).start()

    RSTEP = 96 if rows % 96 == 0 else 16

    def add_block(target, other, at_other):
        def body(i, carry):
            at = pl.ds(pl.multiple_of(i * RSTEP, 16), RSTEP)
            there = pl.ds(pl.multiple_of(at_other + i * RSTEP, 16), RSTEP)
            target[at, :] = (target[at, :].astype(F32) + other[there, :].astype(F32)).astype(target.dtype)
            return carry
        lax.fori_loop(0, rows // RSTEP, body, 0)

    def flows(k, hop):
        @pl.when(z == hop)
        def _():
            for t in range(n - 1, hop - 1, -1):
                for j in lanes(k):
                    here = moving(k, 0, t, j)
                    pass_on(k, t, 0, j, here).wait_recv()
                    add_block(here, total(k, j), t * rows)
                    if t > hop:
                        pass_on(k, t, 0, j, here).start()
        @pl.when(z == n - 1 - hop)
        def _():
            for t in range(n - hop):
                for j in lanes(k):
                    here = moving(k, 1, t, j)
                    pass_on(k, t, 1, j, here).wait_recv()
                    if t < n - 1 - hop or hop == n - 1:
                        add_block(here, total(k, j), t * rows)
                    if t < n - 1 - hop:
                        pass_on(k, t, 1, j, here).start()
        if hop == n - 1:
            for j in lanes(k):
                @pl.when((z > 0) & (z < n - 1))
                def _():
                    add_block(moving(k, 1, z, j), moving(k, 0, z, j), 0)

    def both_ends(act):
        @pl.when(z < n - 1)
        def _():
            act(1)
        @pl.when(z == n - 1)
        def _():
            act(0)

    def bit(k):
        return (r >> (L - 1)) & 1

    def trade(k, side):
        return pltpu.make_async_remote_copy(
            src_ref=moving(k, side, z, 1 - bit(k)), dst_ref=pair.at[:, pl.ds(kind[k], chunks[k][2])], send_sem=psend.at[k],
            recv_sem=precv.at[k], device_id={"replica": r ^ bits[L - 1]}, device_id_type=MESH)

    def complete(k):
        def act(side):
            trade(k, side).wait_recv()
            add_block(moving(k, side, z, bit(k)), pair.at[:, pl.ds(kind[k], chunks[k][2])], 0)
        both_ends(act)

    def finished(k, p):
        return F[group(k)].at[:, columns(k, p)]

    def share(k, p, level, source=None):
        return pltpu.make_async_remote_copy(
            src_ref=finished(k, p) if source is None else source, dst_ref=finished(k, p),
            send_sem=fsend.at[k, p, level], recv_sem=frecv.at[k, p], device_id={"replica": r ^ bits[level]}, device_id_type=MESH)

    def done(k, side):
        return moving(k, side, z, bit(k) if ahead_of_pairs(k, L) else 0)

    def keep(k, side):
        return pltpu.make_async_copy(done(k, side), finished(k, r), fkeep.at[k])

    def publish(k):
        def act(side):
            for level in reversed(range(L)):
                share(k, r, level, done(k, side)).start()
            keep(k, side).start()
        both_ends(act)

    def masks(level):
        found = [0]
        for upper in range(level + 1, L):
            found = found + [m | bits[upper] for m in found]
        return [m | bits[level] for m in found]

    def collect(level, k):
        for mask in masks(level):
            p = r ^ mask
            share(k, p, level).wait_recv()
            for lower in reversed(range(level)):
                share(k, p, lower).start()

    def small_to_z(t):
        return pltpu.make_async_remote_copy(
            src_ref=small_in.at[t], dst_ref=small_z.at[z], send_sem=ss_z.at[t], recv_sem=sr_z.at[z],
            device_id={"fsdp": t}, device_id_type=MESH)

    def small_to_r(p):
        return pltpu.make_async_remote_copy(
            src_ref=small_sum, dst_ref=small_r.at[r], send_sem=ss_r.at[p], recv_sem=sr_r.at[r],
            device_id={"replica": p}, device_id_type=MESH)

    first_left(lambda copy: copy.start())
    fetch_left(1).start()
    fetch_all(0)
    pl.semaphore_wait(barrier, n - 1 + R - 1)
    own_small = pltpu.make_async_copy(small_in.at[z], small_z.at[z], ss_l)
    own_small.start()
    own(0)
    for hop in range(1, n):
        small_to_z(lax.rem(z + hop, n)).start()
    stages = L + n + L
    for turn in range(K + stages - 1):
        for stage_index in [1, 0] + list(range(2, stages)):
            k = turn - stage_index
            if k < 0 or k >= K:
                continue
            hop = stage_index - last(k)
            if stage_index == 0:
                if k > 0:
                    own(k)
            elif stage_index <= last(k):
                merge(stage_index - 1, k)
                if stage_index == last(k):
                    launch(k)
            elif hop < n:
                flows(k, hop)
                if hop == n - 1:
                    if ahead_of_pairs(k, L):
                        both_ends(lambda side: trade(k, side).start())
                    else:
                        publish(k)
            elif stage_index == L + n - 1:
                complete(k)
                publish(k)
            else:
                collect(L - 1 - (stage_index - L - n), k)
        if turn == 1:
            own_small.wait()
            for hop in range(1, n):
                source = lax.rem(z + hop, n)
                pltpu.make_async_remote_copy(
                    src_ref=small_in.at[source], dst_ref=small_z.at[source], send_sem=ss_z.at[source],
                    recv_sem=sr_z.at[source], device_id={"fsdp": source}, device_id_type=MESH).wait_recv()
            together = small_z[0]
            for t in range(1, n):
                together = together + small_z[t]
            small_sum[...] = together
            small_r[r] = together
            for hop in range(1, R):
                small_to_r(lax.rem(r + hop, R)).start()
    for hop in range(1, R):
        p = lax.rem(r + hop, R)
        pltpu.make_async_remote_copy(
            src_ref=small_sum, dst_ref=small_r.at[p], send_sem=ss_r.at[p], recv_sem=sr_r.at[p],
            device_id={"replica": p}, device_id_type=MESH).wait_recv()
    together = small_r[0]
    for p in range(1, R):
        together = together + small_r[p]
    small_out[...] = together
    for hop in range(1, R):
        small_to_r(lax.rem(r + hop, R)).wait_send()
    for hop in range(1, n):
        small_to_z(lax.rem(z + hop, n)).wait_send()
    for k in range(K):
        for level in range(last(k)):
            if level == 0 and k < K - 2:
                continue
            for j in range(R >> (level + 1)):
                give(level, k, j).wait_send()
        for t in range(n):
            for j in lanes(k):
                if t > 0:
                    @pl.when(t > z)
                    def _():
                        pass_on(k, t, 0, j, moving(k, 0, t, j)).wait_send()
                if t < n - 1:
                    @pl.when(t < z)
                    def _():
                        pass_on(k, t, 1, j, moving(k, 1, t, j)).wait_send()
        if ahead_of_pairs(k, L):
            both_ends(lambda side: trade(k, side).wait_send())
        both_ends(lambda side: keep(k, side).wait())
        for level in range(L):
            share(k, r, level).wait_send()
            for mask in masks(level):
                for lower in range(level):
                    share(k, r ^ mask, lower).wait_send()


def reduce_grads(n, R, wide, small, n1, c, n2, rows_in, dqkv, low, du, g, back):
    tokens, D = n1.shape
    rows = D // n
    chunks = plan(R, [w // R for w in wide], D, g.shape[1])
    K = len(chunks)
    most = max(size for _, _, size in chunks)
    L = R.bit_length() - 1
    one, two, both = places(chunks, L)[2]
    two = max(two, 128)
    dma = pltpu.SemaphoreType.DMA
    return pl.pallas_call(
        functools.partial(reduce_kernel, n, R, chunks),
        out_shape=(shape(rows, wide[0], HALF), shape(rows, wide[1], HALF),
                   jax.ShapeDtypeStruct(small.shape[1:], small.dtype)),
        in_specs=[pl.BlockSpec(memory_space=pltpu.VMEM)] + [ANY] * (8 + len(back)),
        out_specs=(ANY, ANY, pl.BlockSpec(memory_space=pltpu.VMEM)),
        scratch_shapes=[pltpu.VMEM((R >> (level + 1), D, one if level == L - 1 else both), HALF) for level in range(L)] + [
            pltpu.VMEM((2, D, R * most), HALF),
            pltpu.VMEM((2, D, tokens), HALF),
            pltpu.VMEM((2, tokens, D), HALF),
            pltpu.VMEM((tokens, R * most), HALF),
            pltpu.VMEM((2, n - 1, rows, one), HALF),
            pltpu.VMEM((2, n - 1, 2, rows, two), HALF),
            pltpu.VMEM((rows, two), HALF),
            pltpu.VMEM((n,) + small.shape[1:], small.dtype),
            pltpu.VMEM((R,) + small.shape[1:], small.dtype),
            pltpu.VMEM(small.shape[1:], small.dtype),
            dma((R,)), dma((4 + len(back),)),
            dma((L, K, R // 2)), dma((L, K, R // 2)),
            dma((K, 2, n, 2)), dma((K, 2, n, 2)),
            dma((K,)), dma((K,)),
            dma((K, R, L)), dma((K, R)), dma((K,)),
            dma((n,)), dma((n,)), dma((R,)), dma((R,)), dma(()),
        ],
        compiler_params=pltpu.CompilerParams(collective_id=1, has_side_effects=True, vmem_limit_bytes=62 * 1024 * 1024),
    )(small, n1, c, n2, rows_in, dqkv, low, du, g, *back)


def shifted(value, axis, steps):
    count = lax.axis_size(axis)
    first, last = (max(0, -steps), min(count, count - steps))
    return lax.ppermute(value, axis, [(source, source + steps) for source in range(first, last)])


def pad_columns(value, wide):
    return jnp.pad(value, ((0, 0), (0, wide - value.shape[1])))


def on_device(ends, first_gain, first_shift, qkv_weight, qv_bias, out_weight, out_bias, second_gain, second_shift,
              up_weight, up_bias, down_weight, down_bias):
    n, R = lax.axis_size("fsdp"), lax.axis_size("replica")
    section = lax.axis_index("section")
    at_first = section == 0
    _, images, tok, D = ends.shape
    hidden = up_weight.shape[2]
    piece = D // n
    unit = 128 * R
    filled = -(-hidden // LANES) * LANES
    wide = [-(-columns // unit) * unit for columns in (4 * D, 2 * filled)]

    G, vec, qb, ub = gather_weights(
        n, R, wide, filled, qkv_weight[0], out_weight[0], pad_columns(up_weight[0], filled), pad_columns(down_weight[0].T, filled),
        (first_gain, first_shift, qv_bias[0], out_bias, second_gain, second_shift, down_bias, up_bias))

    rows = ends[0].reshape(images * tok, D)
    T = images // MICRO * tok
    total = MICRO * T
    parts = [rows[m * T : (m + 1) * T] for m in range(MICRO)]
    here = section.astype(jnp.int32)

    def turn(micro, where):
        return jnp.stack([jnp.int32(micro), (here == where).astype(jnp.int32)])

    kept = (None,) * 9
    sent = []
    for micro in range(MICRO):
        *kept, y = f_layer(turn(micro, 0), total, False, parts[micro], vec, qb, ub, G, wide[0], tok, kept)
        sent.append(shifted(y, "section", 1))
    for micro in range(MICRO):
        *kept, y = f_layer(turn(micro, 1), total, True, sent[micro], vec, qb, ub, G, wide[0], tok, kept)
    n1, qkv, probs, c, r1, n2, g, gp, result = kept

    kept = (None, None, None, result)
    back = []
    stats, sums = [], []
    for where in (1, 0):
        for micro in range(MICRO):
            e, x = (parts[micro], sent[micro]) if where else (back[micro], parts[micro])
            *kept, dx, stat, part = d_layer(turn(micro, where), total, where == 0, e, x, vec, G, wide[0], gp, r1, qkv, probs, tok, kept)
            stats.append(stat)
            sums.append(part)
            if where:
                back.append(shifted(dx, "section", -1))
    du, low, dqkv, result = kept
    stats = sum(jnp.where(at_first, below, above) for above, below in zip(stats[:MICRO], stats[MICRO:]))
    sums = sum(jnp.where(at_first, below, above) for above, below in zip(sums[:MICRO], sums[MICRO:]))

    stats = stats.sum(axis=1)
    vectors = jnp.stack([stats[4], stats[5], stats[6], stats[7], stats[2], stats[0], stats[1], stats[3]])
    vectors = vectors.reshape(8, n, piece).transpose(1, 0, 2).reshape(n, 8 * piece)
    vectors = jnp.concatenate([vectors, sums[0, :hidden].reshape(n, hidden // n)], axis=1)
    lanes = -(-vectors.shape[1] // (16 * 128)) * 128
    small = jnp.pad(vectors, ((0, 0), (0, 16 * lanes - vectors.shape[1]))).reshape(n, 16, lanes)
    F_a, F_b, s = reduce_grads(n, R, wide, small, n1, c, n2, rows, dqkv, low, du, g, back)
    s = s.reshape(-1)
    v = s[: 8 * piece].reshape(8, piece)
    return (
        result.reshape(1, images, tok, D),
        v[0][None],
        v[1][None],
        F_a[:, : 3 * D].astype(F32)[None],
        v[2:4][None],
        F_a[:, 3 * D : 4 * D].astype(F32)[None],
        v[4][None],
        v[5][None],
        v[6][None],
        F_b[:, :hidden].astype(F32)[None],
        s[8 * piece : 8 * piece + hidden // n][None],
        F_b[:, filled : filled + hidden].T.astype(F32)[None],
        v[7][None],
    )


def solution(mesh):
    placed = (
        P("section", ("fsdp", "replica"), None, None),
        P("section", "fsdp"),
        P("section", "fsdp"),
        P("section", "fsdp", None),
        P("section", None, "fsdp"),
        P("section", "fsdp", None),
        P("section", "fsdp"),
        P("section", "fsdp"),
        P("section", "fsdp"),
        P("section", "fsdp", None),
        P("section", "fsdp"),
        P("section", None, "fsdp"),
        P("section", "fsdp"),
    )
    return jax.shard_map(on_device, mesh=mesh, in_specs=placed, out_specs=placed, check_vma=False)
```

```python
import functools
import math

import jax
import jax.numpy as jnp
from jax import lax
from jax.experimental import pallas as pl
from jax.experimental.pallas import tpu as pltpu
from jax.sharding import PartitionSpec as P

MESH = pl.DeviceIdType.MESH
HEADS = 16
HEAD_DIM = 72
MICRO = 3
F32 = jnp.float32
HALF = jnp.bfloat16
EPS = 1e-06
ANY = pl.BlockSpec(memory_space=pl.ANY)
NN = (((1,), (0,)), ((), ()))
NT = (((1,), (1,)), ((), ()))
TN = (((0,), (0,)), ((), ()))
FOLD = 8


def mul(left, right, dims=NN):
    return lax.dot_general(left, right, dims, preferred_element_type=F32)


def row_loop(count, step, body):
    def run(i, carry):
        body(pl.ds(pl.multiple_of(i * step, step), step))
        return carry
    lax.fori_loop(0, count // step, run, 0)


def normal(value):
    center = value - jnp.mean(value, axis=-1, keepdims=True)
    scale = lax.rsqrt(jnp.mean(center * center, axis=-1, keepdims=True) + EPS)
    return center * scale, scale


def fold(value):
    return value.reshape(value.shape[0] // 8, 8, value.shape[1]).sum(axis=0)


def norm_back(value, grad, gain):
    hat, scale = normal(value)
    d = grad * gain
    low = d - jnp.mean(d, axis=-1, keepdims=True) - hat * jnp.mean(d * hat, axis=-1, keepdims=True)
    return low * scale, hat


def params(limit=56, **kw):
    return pltpu.CompilerParams(vmem_limit_bytes=limit * 1024 * 1024, **kw)


def shape(rows, columns, dtype):
    return jax.ShapeDtypeStruct((rows, columns), dtype)


def spans(h):
    a, b = h * HEAD_DIM, (h + 1) * HEAD_DIM
    lo = a // 128 * 128
    hi = -(-b // 128) * 128
    return a, b, lo, hi

def head_mask(h, rows):
    a, b, lo, hi = spans(h)
    lane = lax.broadcasted_iota(jnp.int32, (rows, hi - lo), 1) + lo
    return (lane >= a) & (lane < b)

FOLD = 8


def attn_image(qkv, P, c, D, tok, factor):
    for first in range(0, HEADS, FOLD):
        heads = range(first, first + FOLD)
        held = []
        for h in heads:
            a, b, lo, hi = spans(h)
            held.append(mul(qkv[:, D + lo:D + hi], jnp.where(head_mask(h, tok), qkv[:, lo:hi], 0), NT))
        probs = []
        for h, s in zip(heads, held):
            e = jnp.exp2((s - jnp.max(s, axis=0, keepdims=True)) * factor)
            p = (e * (1.0 / jnp.sum(e, axis=0, keepdims=True))).astype(HALF)
            P[h] = p
            probs.append(p)
        for h, p in zip(heads, probs):
            a, b, lo, hi = spans(h)
            o = mul(p, qkv[:, 2 * D + lo:2 * D + hi], TN).astype(HALF)
            c[:, lo:hi] = jnp.where(head_mask(h, tok), o, c[:, lo:hi]) if a > lo else o


def attn_back_image(qkv, P, dc, out, D, tok, factor):
    for first in range(0, HEADS, FOLD):
        heads = range(first, first + FOLD)
        held = []
        for h in heads:
            a, b, lo, hi = spans(h)
            held.append(mul(qkv[:, 2 * D + lo:2 * D + hi], jnp.where(head_mask(h, tok), dc[:, lo:hi], 0), NT))
        grads = []
        for h, dp in zip(heads, held):
            wide = P[h].astype(F32)
            grads.append((wide * (dp - jnp.sum(wide * dp, axis=0, keepdims=True)) * factor).astype(HALF))
        for h, ds in zip(heads, grads):
            a, b, lo, hi = spans(h)
            mask = head_mask(h, tok)
            dv = mul(P[h], dc[:, lo:hi]).astype(HALF)
            dk = mul(ds, qkv[:, lo:hi]).astype(HALF)
            dq = mul(ds, qkv[:, D + lo:D + hi], TN).astype(HALF)
            for base, value in ((0, dq), (D, dk), (2 * D, dv)):
                at = slice(base + lo, base + hi)
                out[:, at] = jnp.where(mask, value, out[:, at]) if a > lo else value


TILE = 512
LANES = 256


def pieces(width, step):
    return [(a, min(step, width - a)) for a in range(0, width, step)]


def tiles(width, step, body):
    whole = width // step
    def run(i, carry):
        body(pl.multiple_of(i * step, step), step)
        return carry
    lax.fori_loop(0, whole, run, 0)
    if width % step:
        body(whole * step, width % step)


def f_layer(slots, total, final, x, vec, qb, ub, G, base, tok, kept):
    T, D = x.shape
    hidden = ub.shape[1]
    images = T // tok
    factor = HEAD_DIM ** (-0.5) * math.log2(math.e)
    root = math.sqrt(2.0 / math.pi)
    cut = pieces(4 * D, 768)
    plain, spare = 5, sum(b is not None for b in kept)
    chunk = T // 2 if T % 32 == 0 else T

    def kernel(slot, *refs):
        @pl.when(slot[1] == 1)
        def _():
            work(slot, *refs)

    def work(slot, *refs):
        x_in, vec, qb, ub, G = refs[:plain]
        (n1o, qkvo, Po, co, r1o, n2o, go, gpo, reso, y,
         x, wa, wb, n1, qkv, P, c, r1, n2, g, gp, res, wsem, psem, gsem, osem) = refs[plain + spare:]
        save = pl.ds(pl.multiple_of(slot[0] * T, 16), T)

        def weight(j):
            a, w = cut[j]
            return pltpu.make_async_copy(G.at[:, pl.ds(a, w)], wa.at[:, pl.ds(a, w)], wsem.at[j])
        up = pltpu.make_async_copy(G.at[:, pl.ds(base, hidden)], wb, wsem.at[len(cut)])
        down = pltpu.make_async_copy(G.at[:, pl.ds(base + hidden, hidden)], wa.at[:, pl.ds(0, hidden)], wsem.at[len(cut) + 1])
        tokens = pltpu.make_async_copy(x_in, x, wsem.at[len(cut) + 2])
        tokens.start()
        for j in range(len(cut)):
            weight(j).start()
        up.start()

        def out(source, target, at, k):
            return pltpu.make_async_copy(source, target.at[at], osem.at[k])
        outs = [out(n1, n1o, save, 0), out(qkv, qkvo, save, 1), out(c, co, save, 2), out(r1, r1o, save, 3),
                out(n2, n2o, save, 4), out(g, go, save, 5)]

        def first(at):
            n1[at, :] = (normal(x[at, :].astype(F32))[0] * vec[0:1, :] + vec[1:2, :]).astype(HALF)
        tokens.wait()
        row_loop(T, tok, first)
        outs[0].start()
        for j, (a, w) in enumerate(cut):
            weight(j).wait()
            if a < 3 * D:
                b = min(a + w, 3 * D)
                qkv[:, a:b] = (mul(n1[...], wa[:, a:b]) + qb[:, a:b]).astype(HALF)
        outs[1].start()

        def probs(i):
            return pltpu.make_async_copy(P.at[i % 2], Po.at[slot[0] * images + i], psem.at[i % 2])

        def image(i, carry):
            @pl.when(i >= 2)
            def _():
                probs(i - 2).wait()
            rows = pl.ds(pl.multiple_of(i * tok, 16), tok)
            attn_image(qkv.at[rows], P.at[i % 2], c.at[rows], D, tok, factor)
            probs(i).start()
            return carry
        lax.fori_loop(0, images, image, 0)
        outs[2].start()
        r1[...] = mul(c[...], wa[:, 3 * D:4 * D])
        down.start()

        def second(at):
            value = r1[at, :] + vec[4:5, :] + x[at, :].astype(F32)
            r1[at, :] = value
            n2[at, :] = (normal(value)[0] * vec[5:6, :] + vec[6:7, :]).astype(HALF)
        row_loop(T, tok, second)
        outs[3].start()
        outs[4].start()
        up.wait()

        def slope(i, size):
            return pltpu.make_async_copy(
                gp.at[lax.rem(i, 2), :, pl.ds(0, size)], gpo.at[save, pl.ds(pl.multiple_of(i * TILE, 128), size)],
                gsem.at[lax.rem(i, 2)])

        def rise(start, size):
            i = start // TILE
            @pl.when(i >= 2)
            def _():
                slope(i - 2, TILE).wait()
            at = pl.ds(start, size)
            for a in range(0, T, chunk):
                u = mul(n2[a:a + chunk, :], wb[:, at]) + ub[:, at]
                square = u * u
                t = jnp.tanh(u * (root + (root * 0.044715) * square))
                half = 0.5 + 0.5 * t
                g[a:a + chunk, at] = (u * half).astype(HALF)
                gp[lax.rem(i, 2), a:a + chunk, 0:size] = (
                    half + (0.5 * u) * (1.0 - t * t) * (root + (3.0 * root * 0.044715) * square)).astype(HALF)
            slope(i, size).start()
        tiles(hidden, TILE, rise)
        outs[5].start()
        down.wait()
        for a, w in pieces(D, LANES):
            at = slice(a, a + w)
            value = mul(g[...], wa[a:a + w, 0:hidden], NT) + (r1[:, at] + vec[7:8, at])
            if final:
                res[:, at] = value
                outs.append(out(res.at[:, pl.ds(a, w)], reso, (save, pl.ds(a, w)), 6 + a // LANES))
                outs[-1].start()
            y[:, at] = value.astype(HALF)
        for copy in outs:
            copy.wait()
        for i in range(max(0, images - 2), images):
            probs(i).wait()
        count = -(-hidden // TILE)
        for i in range(max(0, count - 2), count):
            slope(i, min(TILE, hidden - i * TILE)).wait()

    aliases = {}
    ins = [x, vec, qb, ub, G]
    for index, buffer in enumerate(kept):
        if buffer is not None:
            aliases[1 + len(ins)] = index
            ins.append(buffer)
    dma = pltpu.SemaphoreType.DMA
    whole = pl.BlockSpec(memory_space=pltpu.VMEM)
    return pl.pallas_call(
        kernel,
        out_shape=(shape(total, D, HALF), shape(total, 3 * D, HALF),
                   jax.ShapeDtypeStruct((total // tok, HEADS, tok, tok), HALF), shape(total, D, HALF), shape(total, D, F32),
                   shape(total, D, HALF), shape(total, hidden, HALF), shape(total, hidden, HALF), shape(total, D, F32),
                   shape(T, D, HALF)),
        grid_spec=pltpu.PrefetchScalarGridSpec(
            num_scalar_prefetch=1, grid=(1,), in_specs=[ANY] + [whole] * 3 + [ANY] + [ANY] * spare, out_specs=(ANY,) * 9 + (whole,),
            scratch_shapes=[
                pltpu.VMEM((T, D), HALF), pltpu.VMEM((D, 4 * D), HALF), pltpu.VMEM((D, hidden), HALF), pltpu.VMEM((T, D), HALF),
                pltpu.VMEM((T, 3 * D), HALF), pltpu.VMEM((2, HEADS, tok, tok), HALF), pltpu.VMEM((T, D), HALF),
                pltpu.VMEM((T, D), F32), pltpu.VMEM((T, D), HALF), pltpu.VMEM((T, hidden), HALF),
                pltpu.VMEM((2, T, TILE), HALF), pltpu.VMEM((T, D), F32),
                dma((len(cut) + 3,)), dma((2,)), dma((2,)), dma((6 + len(pieces(D, LANES)),))]),
        input_output_aliases=aliases,
        compiler_params=params(64),
        cost_estimate=pl.CostEstimate(flops=T * D, bytes_accessed=T * D, transcendentals=0),
    )(slots, *ins)


def d_layer(slots, total, final, e, x, vec, G, base, GP, R1, QKV, PP, tok, kept):
    T, D = x.shape
    hidden = GP.shape[1]
    images = T // tok
    scale = HEAD_DIM ** (-0.5)
    plain, spare = 8, sum(b is not None for b in kept)
    chunk = T // 2 if T % 32 == 0 else T

    def kernel(slot, *refs):
        @pl.when(slot[1] == 1)
        def _():
            work(slot, *refs)

    def work(slot, *refs):
        e_in, x_in, vec, G, GP, R1, QKV, PP = refs[:plain]
        (duo, lowo, dqkvo, reso, dx, stats, sums,
         e, x, wa, wb, gp, r1, qkv, P, du, grad, dr1, low, dc, dqkv, wsem, psem, isem, osem) = refs[plain + spare:]
        save = pl.ds(pl.multiple_of(slot[0] * T, 16), T)
        cuts = pieces(hidden, 2 * TILE)
        down = [pltpu.make_async_copy(G.at[:, pl.ds(base + hidden + a, w)], wa.at[:, pl.ds(a, w)], wsem.at[2 + j]) for j, (a, w) in enumerate(cuts)]
        slope = [pltpu.make_async_copy(GP.at[save, pl.ds(a, w)], gp.at[:, pl.ds(a, w)], isem.at[2 + j]) for j, (a, w) in enumerate(cuts)]
        up = pltpu.make_async_copy(G.at[:, pl.ds(base, hidden)], wb, wsem.at[0])
        rest = pltpu.make_async_copy(G.at[:, pl.ds(0, 4 * D)], wa, wsem.at[1])
        loads = [pltpu.make_async_copy(R1.at[save], r1, isem.at[0]), pltpu.make_async_copy(QKV.at[save], qkv, isem.at[1])]
        count = len(cuts)
        cotangent = pltpu.make_async_copy(e_in, e, isem.at[2 + count])
        tokens = pltpu.make_async_copy(x_in, x, isem.at[3 + count])
        cotangent.start()
        for weight, factor in zip(down, slope):
            weight.start()
            factor.start()
        up.start()
        tokens.start()
        for copy in loads:
            copy.start()

        def out(source, target, at, k):
            return pltpu.make_async_copy(source, target.at[at], osem.at[k])
        outs = [out(du, duo, save, 0), out(low, lowo, save, 1), out(dqkv, dqkvo, save, 2)]

        def probs(i):
            return pltpu.make_async_copy(PP.at[slot[0] * images + i], P.at[i % 2], psem.at[i % 2])
        for i in range(min(2, images)):
            probs(i).start()
        stats[...] = jnp.zeros_like(stats)

        def fall(start, size):
            at = pl.ds(start, size)
            total = None
            for a in range(0, T, chunk):
                d = (mul(e[a:a + chunk, :], wa[:, at]) * gp[a:a + chunk, at].astype(F32)).astype(HALF)
                du[a:a + chunk, at] = d
                part = jnp.sum(d.astype(F32), axis=0, keepdims=True)
                total = part if total is None else total + part
            sums[:, at] = total
        cotangent.wait()
        for j, (a, w) in enumerate(cuts):
            down[j].wait()
            slope[j].wait()
            for b in range(a, a + w, TILE):
                fall(b, min(TILE, a + w - b))
        rest.start()
        outs[0].start()
        up.wait()
        for a, w in pieces(D, LANES):
            grad[:, a:a + w] = mul(du[...], wb[a:a + w, :], NT)
        loads[0].wait()

        def second(at):
            g = grad[at, :]
            part, hat = norm_back(r1[at, :], g, vec[5:6, :])
            eb = e[at, :].astype(F32)
            value = eb + part
            rounded = value.astype(HALF)
            dr1[at, :] = value
            low[at, :] = rounded
            stats[0] += fold(g * hat)
            stats[1] += fold(g)
            stats[2] += fold(rounded.astype(F32))
            stats[3] += fold(eb)
        row_loop(T, tok, second)
        outs[1].start()
        rest.wait()
        for a, w in pieces(D, LANES):
            dc[:, a:a + w] = mul(low[...], wa[a:a + w, 3 * D:4 * D], NT).astype(HALF)
        loads[1].wait()

        def image(i, carry):
            probs(i).wait()
            rows = pl.ds(pl.multiple_of(i * tok, 16), tok)
            attn_back_image(qkv.at[rows], P.at[i % 2], dc.at[rows], dqkv.at[rows], D, tok, scale)
            @pl.when(i + 2 < images)
            def _():
                probs(i + 2).start()
            return carry
        lax.fori_loop(0, images, image, 0)
        outs[2].start()
        tokens.wait()
        for a, w in pieces(D, LANES):
            grad[:, a:a + w] = mul(dqkv[...], wa[a:a + w, 0:3 * D], NT)

        def first(at):
            g = grad[at, :]
            part, hat = norm_back(x[at, :].astype(F32), g, vec[0:1, :])
            value = dr1[at, :] + part
            dr1[at, :] = value
            dx[at, :] = value.astype(HALF)
            stats[4] += fold(g * hat)
            stats[5] += fold(g)
            stats[6] += fold(dqkv[at, 0:D].astype(F32))
            stats[7] += fold(dqkv[at, 2 * D:3 * D].astype(F32))
        for i in range(images):
            at = pl.ds(i * tok, tok)
            first(at)
            if final:
                outs.append(out(dr1.at[at], reso, pl.ds(pl.multiple_of(slot[0] * T + i * tok, 16), tok), 3 + i))
                outs[-1].start()
        for copy in outs:
            copy.wait()

    aliases = {}
    ins = [e, x, vec, G, GP, R1, QKV, PP]
    for index, buffer in enumerate(kept):
        if buffer is not None:
            aliases[1 + len(ins)] = index
            ins.append(buffer)
    dma = pltpu.SemaphoreType.DMA
    whole = pl.BlockSpec(memory_space=pltpu.VMEM)
    return pl.pallas_call(
        kernel,
        out_shape=(shape(total, hidden, HALF), shape(total, D, HALF), shape(total, 3 * D, HALF), shape(total, D, F32),
                   shape(T, D, HALF), jax.ShapeDtypeStruct((8, 8, D), F32), shape(1, hidden, F32)),
        grid_spec=pltpu.PrefetchScalarGridSpec(
            num_scalar_prefetch=1, grid=(1,), in_specs=[ANY] * 2 + [whole] + [ANY] + [ANY] * (4 + spare), out_specs=(ANY,) * 4 + (whole,) * 3,
            scratch_shapes=[
                pltpu.VMEM((T, D), HALF), pltpu.VMEM((T, D), HALF),
                pltpu.VMEM((D, 4 * D), HALF), pltpu.VMEM((D, hidden), HALF), pltpu.VMEM((T, hidden), HALF),
                pltpu.VMEM((T, D), F32), pltpu.VMEM((T, 3 * D), HALF), pltpu.VMEM((2, HEADS, tok, tok), HALF),
                pltpu.VMEM((T, hidden), HALF), pltpu.VMEM((T, D), F32), pltpu.VMEM((T, D), F32), pltpu.VMEM((T, D), HALF),
                pltpu.VMEM((T, D), HALF), pltpu.VMEM((T, 3 * D), HALF),
                dma((2 + len(pieces(hidden, 2 * TILE)),)), dma((2,)), dma((4 + len(pieces(hidden, 2 * TILE)),)), dma((3 + images,))]),
        input_output_aliases=aliases,
        compiler_params=params(64),
        cost_estimate=pl.CostEstimate(flops=T * D, bytes_accessed=T * D, transcendentals=0),
    )(slots, *ins)


def powers(count):
    bits = []
    bit = count // 2
    while bit:
        bits.append(bit)
        bit //= 2
    return bits

def gather_kernel(n, R, halves, qkv, out, up, down, *refs):
    (gain_one, shift_one, bias_qv, bias_out, gain_two, shift_two, bias_down, bias_up,
     G, vec, qb, ub, stage_a, stage_b, S, lsem, ssem, rsem, small_send, small_recv) = refs
    z = lax.axis_index("fsdp")
    r = lax.axis_index("replica")
    rows, filled = up.shape
    stage = (stage_a, stage_b)
    part = [ref.shape[1] // R for ref in stage]
    base = (0, stage_a.shape[1])
    some = rows // halves
    bits = powers(R)
    barrier = pltpu.get_barrier_semaphore()
    for hop in range(1, n):
        pl.semaphore_signal(barrier, inc=1, device_id={"fsdp": lax.rem(z + hop, n)}, device_id_type=MESH)
    for bit in bits:
        pl.semaphore_signal(barrier, inc=1, device_id={"replica": r ^ bit}, device_id_type=MESH)
    mine = pl.ds(pl.multiple_of(z * rows, 16), rows)
    first = qkv.shape[1]
    local = [
        pltpu.make_async_copy(qkv, stage_a.at[:, pl.ds(0, first)], lsem.at[0]),
        pltpu.make_async_copy(out, stage_a.at[:, pl.ds(first, out.shape[1])], lsem.at[1]),
        pltpu.make_async_copy(up, stage_b.at[:, pl.ds(0, filled)], lsem.at[2]),
        pltpu.make_async_copy(down, stage_b.at[:, pl.ds(filled, filled)], lsem.at[3]),
    ]
    for copy in local:
        copy.start()
    keep = [pltpu.make_async_copy(stage[group], G.at[mine, pl.ds(base[group], stage[group].shape[1])], lsem.at[4 + group]) for group in range(2)]

    for row, value in enumerate((gain_one, shift_one, None, None, bias_out, gain_two, shift_two, bias_down, bias_up)):
        value = bias_qv[row - 2:row - 1, :] if value is None else value[...]
        S[z, row:row + 1, 0:value.shape[1]] = value.astype(F32)
    pl.semaphore_wait(barrier, n - 1 + len(bits))

    def piece(unit, source, column):
        group, half = unit // halves, unit % halves
        return G.at[pl.ds(pl.multiple_of(source * rows + half * some, 16), some),
                    pl.ds(pl.multiple_of(base[group] + column * part[group], 128), part[group])]

    def send(unit, source, column, kind, target, origin=None):
        return pltpu.make_async_remote_copy(
            src_ref=piece(unit, source, column) if origin is None else origin, dst_ref=piece(unit, source, column),
            send_sem=ssem.at[unit, source, column, kind], recv_sem=rsem.at[unit, source, column],
            device_id=target, device_id_type=MESH)

    def to_right(unit, source, origin=None):
        return send(unit, source, r, 0, {"fsdp": z + 1}, origin)

    def to_left(unit, source, origin=None):
        return send(unit, source, r, 1, {"fsdp": z - 1}, origin)

    def own(unit):
        wide = part[unit // halves]
        return stage[unit // halves].at[pl.ds(unit % halves * some, some), pl.ds(pl.multiple_of(r * wide, 128), wide)]

    def share(unit, source, column, level):
        return send(unit, source, column, 2 + level, {"replica": r ^ bits[level]})

    def arrived(unit, source, column):
        send(unit, source, column, 0, {"replica": r ^ bits[0]}).wait_recv()

    def small_to(hop):
        return pltpu.make_async_remote_copy(
            src_ref=S.at[z], dst_ref=S.at[z], send_sem=small_send.at[hop],
            recv_sem=small_recv.at[z], device_id={"fsdp": lax.rem(z + hop, n)}, device_id_type=MESH)
    for hop in range(1, n):
        small_to(hop).start()
    order = [0] + list(range(halves, 2 * halves)) + list(range(1, halves))
    for unit in order:
        group = unit // halves
        if unit % halves == 0:
            local[2 * group].wait()
            local[2 * group + 1].wait()
            keep[group].start()
        @pl.when(z + 1 < n)
        def _():
            to_right(unit, z, own(unit)).start()
        @pl.when(z > 0)
        def _():
            to_left(unit, z, own(unit)).start()
    columns = {}
    for level, bit in enumerate(bits):
        masks = [0]
        for upper in bits[:level]:
            masks = masks + [m | upper for m in masks]
        columns[level] = [bit | m for m in masks]
    units = 2 * halves
    steps = [(hop, unit) for hop in range(1, n) for unit in order]
    for turn in range(len(steps) + len(bits)):
        for level in range(-1, len(bits)):
            place = turn - 1 - level
            if place < 0 or place >= len(steps):
                continue
            hop, unit = steps[place]
            for sign in (-1, 1):
                source = z + sign * hop
                @pl.when((source >= 0) & (source < n))
                def _():
                    if level < 0:
                        arrived(unit, source, r)
                        for lower in range(len(bits)):
                            share(unit, source, r, lower).start()
                        if sign < 0:
                            @pl.when(z + 1 < n)
                            def _():
                                to_right(unit, source).start()
                        else:
                            @pl.when(z > 0)
                            def _():
                                to_left(unit, source).start()
                    else:
                        for mask in columns[level]:
                            arrived(unit, source, r ^ mask)
                            for lower in range(level + 1, len(bits)):
                                share(unit, source, r ^ mask, lower).start()
    for copy in keep:
        copy.wait()
    for hop in range(1, n):
        source = lax.rem(z + hop, n)
        pltpu.make_async_remote_copy(
            src_ref=S.at[source], dst_ref=S.at[source], send_sem=small_send.at[hop],
            recv_sem=small_recv.at[source], device_id={"fsdp": source}, device_id_type=MESH).wait_recv()
        small_to(hop).wait_send()
    D = vec.shape[1]
    few = bias_up.shape[1]
    ub[...] = jnp.zeros_like(ub)
    for source in range(n):
        vec[:, source * rows:(source + 1) * rows] = S[source, 0:8, 0:rows]
        ub[:, source * few:(source + 1) * few] = S[source, 8:9, 0:few]
    qb[:, 0:D] = vec[2:3, :]
    qb[:, D:2 * D] = jnp.zeros((1, D), F32)
    qb[:, 2 * D:3 * D] = vec[3:4, :]
    for unit in range(units):
        for source in range(n):
            @pl.when((source <= z) & (z + 1 < n))
            def _():
                to_right(unit, source).wait_send()
            @pl.when((source >= z) & (z > 0))
            def _():
                to_left(unit, source).wait_send()
            @pl.when(source != z)
            def _():
                for level in range(len(bits)):
                    share(unit, source, r, level).wait_send()
                for level in range(len(bits)):
                    for mask in columns[level]:
                        for lower in range(level + 1, len(bits)):
                            share(unit, source, r ^ mask, lower).wait_send()


def gather_weights(n, R, wide, filled, qkv, out, up, down, vectors):
    rows = up.shape[0]
    kinds = 2 + len(powers(R))
    halves = 3 if rows % 48 == 0 else 1
    lanes = -(-max(v.shape[1] for v in vectors) // 128) * 128
    dma = pltpu.SemaphoreType.DMA
    whole = pl.BlockSpec(memory_space=pltpu.VMEM)
    D = n * rows
    return pl.pallas_call(
        functools.partial(gather_kernel, n, R, halves),
        out_shape=(shape(D, sum(wide), HALF), shape(8, D, F32), shape(1, 3 * D, F32),
                   shape(1, filled, F32)),
        in_specs=[ANY] * 4 + [whole] * len(vectors),
        out_specs=(ANY,) + (whole,) * 3,
        scratch_shapes=[
            pltpu.VMEM((rows, wide[0]), HALF),
            pltpu.VMEM((rows, wide[1]), HALF),
            pltpu.VMEM((n, 16, lanes), F32),
            dma((6,)),
            dma((2 * halves, n, R, kinds)),
            dma((2 * halves, n, R)),
            dma((n,)),
            dma((n,)),
        ],
        compiler_params=pltpu.CompilerParams(collective_id=0, has_side_effects=True, vmem_limit_bytes=32 * 1024 * 1024),
    )(qkv, out, up, down, *vectors)


ORDER = (1, 0)
SCRATCH = 26


def plan(R, parts, D, filled):
    found = []
    for place, group in enumerate(ORDER):
        edges = (filled, 2 * filled) if group else (3 * D, 4 * D)
        part = parts[group]
        sizes, at = [], 0
        while at < part:
            size = min(max(12 // R, 1) * 128, part - at)
            while any(p * part + at < edge < p * part + at + size for p in range(R) for edge in edges):
                size -= 128
            sizes.append(size)
            at += size
        if place == 0 and sizes[0] == 384:
            sizes[:1] = [128, 256]
        if place == 1 and sizes[-1] > 128:
            sizes[-1:] = [sizes[-1] - 128, 128]
        at = 0
        for size in sizes:
            found.append((place, at, size))
            at += size
    return found


def ahead_of_pairs(k, L):
    return L >= 2 and k % 3 == 2


def places(chunks, L):
    every, kind, counts = [], [], [0, 0, 0]
    for k, (_, _, size) in enumerate(chunks):
        which = int(ahead_of_pairs(k, L))
        every.append(counts[2])
        kind.append(counts[which])
        counts[which] += size
        counts[2] += size
    return every, kind, counts


def reduce_kernel(n, R, chunks, small_in, n1, c, n2, rows_in, dqkv, low, du, g, *refs):
    back = refs[:-3 - SCRATCH - (R.bit_length() - 1)]
    F_a, F_b, small_out, *scratch = refs[len(back):]
    F = (F_a, F_b)
    L = R.bit_length() - 1
    bits = [1 << level for level in range(L)]
    held = scratch[:L]
    (X, left, stage, right, flow, flow_two, pair, small_z, small_r, small_sum, rsem, lsem, send_sem, recv_sem, zsend, zrecv,
     psend, precv, fsend, frecv, fkeep, ss_z, sr_z, ss_r, sr_r, ss_l) = scratch[L:]
    z = lax.axis_index("fsdp")
    r = lax.axis_index("replica")
    tokens, D = n1.shape
    full = D
    rows = full // n
    filled = g.shape[1]
    part = [ref.shape[1] // R for ref in F]
    K = len(chunks)
    every, kind, _ = places(chunks, L)
    barrier = pltpu.get_barrier_semaphore()
    for hop in range(1, n):
        pl.semaphore_signal(barrier, inc=1, device_id={"fsdp": lax.rem(z + hop, n)}, device_id_type=MESH)
    for hop in range(1, R):
        pl.semaphore_signal(barrier, inc=1, device_id={"replica": lax.rem(r + hop, R)}, device_id_type=MESH)

    def group(k):
        return ORDER[chunks[k][0]]

    def columns(k, p):
        return pl.ds(pl.multiple_of(p * part[group(k)] + chunks[k][1], 128), chunks[k][2])

    def part_lanes(k, p):
        return pl.ds(pl.multiple_of(p * chunks[k][2], 128), chunks[k][2])

    def block(t):
        return pl.ds(pl.multiple_of(t * rows, 16), rows)

    def kept(level, j):
        return (r & ((2 << level) - 1)) | (j << (level + 1))

    def factors(k, p):
        a, sub = p * part[group(k)] + chunks[k][1], chunks[k][2]
        if group(k) == 1:
            if a < filled:
                return 1, du.at[:, pl.ds(a, sub)]
            if a < 2 * filled:
                return 0, g.at[:, pl.ds(a - filled, sub)]
            return None, None
        if a < 3 * D:
            return 0, dqkv.at[:, pl.ds(a, sub)]
        if a < 4 * D:
            return 1, low.at[:, pl.ds(a - 3 * D, sub)]
        return None, None

    def fetch(k, p):
        return pltpu.make_async_copy(factors(k, p)[1], right.at[:, pl.ds(p * chunks[k][2], chunks[k][2])], rsem.at[p])

    def fetch_all(k):
        for p in range(R):
            if factors(k, p)[1] is not None:
                fetch(k, p).start()

    def fetch_left(which):
        return pltpu.make_async_copy((rows_in, n2, n1, c)[which], stage.at[which % 2], lsem.at[which])

    def fetch_back(m):
        some = tokens // len(back)
        return pltpu.make_async_copy(back[m], stage.at[0, pl.ds(m * some, some), :], lsem.at[4 + m])

    def first_left(act):
        @pl.when(lax.axis_index("section") == 0)
        def _():
            for m in range(len(back)):
                act(fetch_back(m))
        @pl.when(lax.axis_index("section") != 0)
        def _():
            act(fetch_left(0))

    def turn_left(which):
        if which == 0:
            first_left(lambda copy: copy.wait())
        else:
            fetch_left(which).wait()
        for a in range(0, D, 128):
            left[which % 2, a:a + 128, :] = stage[which % 2, :, a:a + 128].T
        if which < 2:
            fetch_left(which + 2).start()

    def own(k):
        if k >= 2:
            for j in range(R // 2):
                give(0, k - 2, j).wait_send()
        if chunks[k][1] == 0:
            turn_left(2 * chunks[k][0])
            turn_left(2 * chunks[k][0] + 1)
        size = chunks[k][2]
        runs = []
        for p in range(R):
            slot, source = factors(k, p)
            if source is None:
                continue
            fetch(k, p).wait()
            if runs and runs[-1][0] == slot:
                runs[-1][2] = p + 1
            else:
                runs.append([slot, p, p + 1])
        for slot, first, end in runs:
            def body(i, carry):
                at = pl.ds(pl.multiple_of(i * 288, 16), 288)
                X[k % 2, at, first * size:end * size] = mul(
                    left[slot, at, :], right[:, first * size:end * size]).astype(X.dtype)
                return carry
            lax.fori_loop(0, full // 288, body, 0)
        if k + 1 < K:
            fetch_all(k + 1)
        for j in range(R // 2):
            give(0, k, j).start()

    def store(level, k, j):
        return held[level].at[j, :, pl.ds(kind[k] if level == L - 1 else every[k], chunks[k][2])]

    def give(level, k, j):
        if level == 0:
            source = X.at[k % 2, :, part_lanes(k, ((r ^ 1) & 1) | (j << 1))]
        else:
            source = store(level - 1, k, 2 * j + (((r >> level) & 1) ^ 1))
        return pltpu.make_async_remote_copy(
            src_ref=source, dst_ref=store(level, k, j), send_sem=send_sem.at[level, k, j],
            recv_sem=recv_sem.at[level, k, j], device_id={"replica": r ^ bits[level]}, device_id_type=MESH)

    STEP = 96

    def merge(level, k):
        for j in range(R >> (level + 1)):
            give(level, k, j).wait_recv()
            mine = store(level, k, j)
            other = X.at[k % 2, :, part_lanes(k, kept(0, j))] if level == 0 else store(level - 1, k, 2 * j + ((r >> level) & 1))

            def body(i, carry):
                at = pl.ds(pl.multiple_of(i * STEP, 16), STEP)
                mine[at, :] = (mine[at, :].astype(F32) + other[at, :].astype(F32)).astype(mine.dtype)
                return carry
            lax.fori_loop(0, full // STEP, body, 0)
        if level + 1 < last(k):
            for j in range(R >> (level + 2)):
                give(level + 1, k, j).start()

    def last(k):
        return L - 1 if ahead_of_pairs(k, L) else L

    def lanes(k):
        return range(2) if ahead_of_pairs(k, L) else range(1)

    def total(k, j):
        return store(L - 2, k, j) if ahead_of_pairs(k, L) else store(L - 1, k, 0)

    def moving(k, side, t, j):
        place = t - 1 if side == 0 else t
        at = pl.ds(kind[k], chunks[k][2])
        return flow_two.at[side, place, j, :, at] if ahead_of_pairs(k, L) else flow.at[side, place, :, at]

    def pass_on(k, t, side, j, source):
        return pltpu.make_async_remote_copy(
            src_ref=source, dst_ref=moving(k, side, t, j), send_sem=zsend.at[k, side, t, j], recv_sem=zrecv.at[k, side, t, j],
            device_id={"fsdp": z + 1 if side == 0 else z - 1}, device_id_type=MESH)

    def launch(k):
        @pl.when(z == 0)
        def _():
            for t in range(n - 1, 0, -1):
                for j in lanes(k):
                    pass_on(k, t, 0, j, total(k, j).at[block(t), :]).start()
        @pl.when(z == n - 1)
        def _():
            for t in range(n - 1):
                for j in lanes(k):
                    pass_on(k, t, 1, j, total(k, j).at[block(t), :]).start()

    RSTEP = 96 if rows % 96 == 0 else 16

    def add_block(target, other, at_other):
        def body(i, carry):
            at = pl.ds(pl.multiple_of(i * RSTEP, 16), RSTEP)
            there = pl.ds(pl.multiple_of(at_other + i * RSTEP, 16), RSTEP)
            target[at, :] = (target[at, :].astype(F32) + other[there, :].astype(F32)).astype(target.dtype)
            return carry
        lax.fori_loop(0, rows // RSTEP, body, 0)

    def flows(k, hop):
        @pl.when(z == hop)
        def _():
            for t in range(n - 1, hop - 1, -1):
                for j in lanes(k):
                    here = moving(k, 0, t, j)
                    pass_on(k, t, 0, j, here).wait_recv()
                    add_block(here, total(k, j), t * rows)
                    if t > hop:
                        pass_on(k, t, 0, j, here).start()
        @pl.when(z == n - 1 - hop)
        def _():
            for t in range(n - hop):
                for j in lanes(k):
                    here = moving(k, 1, t, j)
                    pass_on(k, t, 1, j, here).wait_recv()
                    if t < n - 1 - hop or hop == n - 1:
                        add_block(here, total(k, j), t * rows)
                    if t < n - 1 - hop:
                        pass_on(k, t, 1, j, here).start()
        if hop == n - 1:
            for j in lanes(k):
                @pl.when((z > 0) & (z < n - 1))
                def _():
                    add_block(moving(k, 1, z, j), moving(k, 0, z, j), 0)

    def both_ends(act):
        @pl.when(z < n - 1)
        def _():
            act(1)
        @pl.when(z == n - 1)
        def _():
            act(0)

    def bit(k):
        return (r >> (L - 1)) & 1

    def trade(k, side):
        return pltpu.make_async_remote_copy(
            src_ref=moving(k, side, z, 1 - bit(k)), dst_ref=pair.at[:, pl.ds(kind[k], chunks[k][2])], send_sem=psend.at[k],
            recv_sem=precv.at[k], device_id={"replica": r ^ bits[L - 1]}, device_id_type=MESH)

    def complete(k):
        def act(side):
            trade(k, side).wait_recv()
            add_block(moving(k, side, z, bit(k)), pair.at[:, pl.ds(kind[k], chunks[k][2])], 0)
        both_ends(act)

    def finished(k, p):
        return F[group(k)].at[:, columns(k, p)]

    def share(k, p, level, source=None):
        return pltpu.make_async_remote_copy(
            src_ref=finished(k, p) if source is None else source, dst_ref=finished(k, p),
            send_sem=fsend.at[k, p, level], recv_sem=frecv.at[k, p], device_id={"replica": r ^ bits[level]}, device_id_type=MESH)

    def done(k, side):
        return moving(k, side, z, bit(k) if ahead_of_pairs(k, L) else 0)

    def keep(k, side):
        return pltpu.make_async_copy(done(k, side), finished(k, r), fkeep.at[k])

    def publish(k):
        def act(side):
            for level in reversed(range(L)):
                share(k, r, level, done(k, side)).start()
            keep(k, side).start()
        both_ends(act)

    def masks(level):
        found = [0]
        for upper in range(level + 1, L):
            found = found + [m | bits[upper] for m in found]
        return [m | bits[level] for m in found]

    def collect(level, k):
        for mask in masks(level):
            p = r ^ mask
            share(k, p, level).wait_recv()
            for lower in reversed(range(level)):
                share(k, p, lower).start()

    def small_to_z(t):
        return pltpu.make_async_remote_copy(
            src_ref=small_in.at[t], dst_ref=small_z.at[z], send_sem=ss_z.at[t], recv_sem=sr_z.at[z],
            device_id={"fsdp": t}, device_id_type=MESH)

    def small_to_r(p):
        return pltpu.make_async_remote_copy(
            src_ref=small_sum, dst_ref=small_r.at[r], send_sem=ss_r.at[p], recv_sem=sr_r.at[r],
            device_id={"replica": p}, device_id_type=MESH)

    first_left(lambda copy: copy.start())
    fetch_left(1).start()
    fetch_all(0)
    pl.semaphore_wait(barrier, n - 1 + R - 1)
    own_small = pltpu.make_async_copy(small_in.at[z], small_z.at[z], ss_l)
    own_small.start()
    own(0)
    for hop in range(1, n):
        small_to_z(lax.rem(z + hop, n)).start()
    stages = L + n + L
    for turn in range(K + stages - 1):
        for stage_index in [1, 0] + list(range(2, stages)):
            k = turn - stage_index
            if k < 0 or k >= K:
                continue
            hop = stage_index - last(k)
            if stage_index == 0:
                if k > 0:
                    own(k)
            elif stage_index <= last(k):
                merge(stage_index - 1, k)
                if stage_index == last(k):
                    launch(k)
            elif hop < n:
                flows(k, hop)
                if hop == n - 1:
                    if ahead_of_pairs(k, L):
                        both_ends(lambda side: trade(k, side).start())
                    else:
                        publish(k)
            elif stage_index == L + n - 1:
                complete(k)
                publish(k)
            else:
                collect(L - 1 - (stage_index - L - n), k)
        if turn == 1:
            own_small.wait()
            for hop in range(1, n):
                source = lax.rem(z + hop, n)
                pltpu.make_async_remote_copy(
                    src_ref=small_in.at[source], dst_ref=small_z.at[source], send_sem=ss_z.at[source],
                    recv_sem=sr_z.at[source], device_id={"fsdp": source}, device_id_type=MESH).wait_recv()
            together = small_z[0]
            for t in range(1, n):
                together = together + small_z[t]
            small_sum[...] = together
            small_r[r] = together
            for hop in range(1, R):
                small_to_r(lax.rem(r + hop, R)).start()
    for hop in range(1, R):
        p = lax.rem(r + hop, R)
        pltpu.make_async_remote_copy(
            src_ref=small_sum, dst_ref=small_r.at[p], send_sem=ss_r.at[p], recv_sem=sr_r.at[p],
            device_id={"replica": p}, device_id_type=MESH).wait_recv()
    together = small_r[0]
    for p in range(1, R):
        together = together + small_r[p]
    small_out[...] = together
    for hop in range(1, R):
        small_to_r(lax.rem(r + hop, R)).wait_send()
    for hop in range(1, n):
        small_to_z(lax.rem(z + hop, n)).wait_send()
    for k in range(K):
        for level in range(last(k)):
            if level == 0 and k < K - 2:
                continue
            for j in range(R >> (level + 1)):
                give(level, k, j).wait_send()
        for t in range(n):
            for j in lanes(k):
                if t > 0:
                    @pl.when(t > z)
                    def _():
                        pass_on(k, t, 0, j, moving(k, 0, t, j)).wait_send()
                if t < n - 1:
                    @pl.when(t < z)
                    def _():
                        pass_on(k, t, 1, j, moving(k, 1, t, j)).wait_send()
        if ahead_of_pairs(k, L):
            both_ends(lambda side: trade(k, side).wait_send())
        both_ends(lambda side: keep(k, side).wait())
        for level in range(L):
            share(k, r, level).wait_send()
            for mask in masks(level):
                for lower in range(level):
                    share(k, r ^ mask, lower).wait_send()


def reduce_grads(n, R, wide, small, n1, c, n2, rows_in, dqkv, low, du, g, back):
    tokens, D = n1.shape
    rows = D // n
    chunks = plan(R, [w // R for w in wide], D, g.shape[1])
    K = len(chunks)
    most = max(size for _, _, size in chunks)
    L = R.bit_length() - 1
    one, two, both = places(chunks, L)[2]
    two = max(two, 128)
    dma = pltpu.SemaphoreType.DMA
    return pl.pallas_call(
        functools.partial(reduce_kernel, n, R, chunks),
        out_shape=(shape(rows, wide[0], HALF), shape(rows, wide[1], HALF),
                   jax.ShapeDtypeStruct(small.shape[1:], small.dtype)),
        in_specs=[pl.BlockSpec(memory_space=pltpu.VMEM)] + [ANY] * (8 + len(back)),
        out_specs=(ANY, ANY, pl.BlockSpec(memory_space=pltpu.VMEM)),
        scratch_shapes=[pltpu.VMEM((R >> (level + 1), D, one if level == L - 1 else both), HALF) for level in range(L)] + [
            pltpu.VMEM((2, D, R * most), HALF),
            pltpu.VMEM((2, D, tokens), HALF),
            pltpu.VMEM((2, tokens, D), HALF),
            pltpu.VMEM((tokens, R * most), HALF),
            pltpu.VMEM((2, n - 1, rows, one), HALF),
            pltpu.VMEM((2, n - 1, 2, rows, two), HALF),
            pltpu.VMEM((rows, two), HALF),
            pltpu.VMEM((n,) + small.shape[1:], small.dtype),
            pltpu.VMEM((R,) + small.shape[1:], small.dtype),
            pltpu.VMEM(small.shape[1:], small.dtype),
            dma((R,)), dma((4 + len(back),)),
            dma((L, K, R // 2)), dma((L, K, R // 2)),
            dma((K, 2, n, 2)), dma((K, 2, n, 2)),
            dma((K,)), dma((K,)),
            dma((K, R, L)), dma((K, R)), dma((K,)),
            dma((n,)), dma((n,)), dma((R,)), dma((R,)), dma(()),
        ],
        compiler_params=pltpu.CompilerParams(collective_id=1, has_side_effects=True, vmem_limit_bytes=62 * 1024 * 1024),
    )(small, n1, c, n2, rows_in, dqkv, low, du, g, *back)


def shifted(value, axis, steps):
    count = lax.axis_size(axis)
    first, last = (max(0, -steps), min(count, count - steps))
    return lax.ppermute(value, axis, [(source, source + steps) for source in range(first, last)])


def pad_columns(value, wide):
    return jnp.pad(value, ((0, 0), (0, wide - value.shape[1])))


def on_device(ends, first_gain, first_shift, qkv_weight, qv_bias, out_weight, out_bias, second_gain, second_shift,
              up_weight, up_bias, down_weight, down_bias):
    n, R = lax.axis_size("fsdp"), lax.axis_size("replica")
    section = lax.axis_index("section")
    at_first = section == 0
    _, images, tok, D = ends.shape
    hidden = up_weight.shape[2]
    piece = D // n
    unit = 128 * R
    filled = -(-hidden // LANES) * LANES
    wide = [-(-columns // unit) * unit for columns in (4 * D, 2 * filled)]

    G, vec, qb, ub = gather_weights(
        n, R, wide, filled, qkv_weight[0], out_weight[0], pad_columns(up_weight[0], filled), pad_columns(down_weight[0].T, filled),
        (first_gain, first_shift, qv_bias[0], out_bias, second_gain, second_shift, down_bias, up_bias))

    rows = ends[0].reshape(images * tok, D)
    T = images // MICRO * tok
    total = MICRO * T
    parts = [rows[m * T : (m + 1) * T] for m in range(MICRO)]
    here = section.astype(jnp.int32)

    def turn(micro, where):
        return jnp.stack([jnp.int32(micro), (here == where).astype(jnp.int32)])

    kept = (None,) * 9
    sent = []
    for micro in range(MICRO):
        *kept, y = f_layer(turn(micro, 0), total, False, parts[micro], vec, qb, ub, G, wide[0], tok, kept)
        sent.append(shifted(y, "section", 1))
    for micro in range(MICRO):
        *kept, y = f_layer(turn(micro, 1), total, True, sent[micro], vec, qb, ub, G, wide[0], tok, kept)
    n1, qkv, probs, c, r1, n2, g, gp, result = kept

    kept = (None, None, None, result)
    back = []
    stats, sums = [], []
    for where in (1, 0):
        for micro in range(MICRO):
            e, x = (parts[micro], sent[micro]) if where else (back[micro], parts[micro])
            *kept, dx, stat, part = d_layer(turn(micro, where), total, where == 0, e, x, vec, G, wide[0], gp, r1, qkv, probs, tok, kept)
            stats.append(stat)
            sums.append(part)
            if where:
                back.append(shifted(dx, "section", -1))
    du, low, dqkv, result = kept
    stats = sum(jnp.where(at_first, below, above) for above, below in zip(stats[:MICRO], stats[MICRO:]))
    sums = sum(jnp.where(at_first, below, above) for above, below in zip(sums[:MICRO], sums[MICRO:]))

    stats = stats.sum(axis=1)
    vectors = jnp.stack([stats[4], stats[5], stats[6], stats[7], stats[2], stats[0], stats[1], stats[3]])
    vectors = vectors.reshape(8, n, piece).transpose(1, 0, 2).reshape(n, 8 * piece)
    vectors = jnp.concatenate([vectors, sums[0, :hidden].reshape(n, hidden // n)], axis=1)
    lanes = -(-vectors.shape[1] // (16 * 128)) * 128
    small = jnp.pad(vectors, ((0, 0), (0, 16 * lanes - vectors.shape[1]))).reshape(n, 16, lanes)
    F_a, F_b, s = reduce_grads(n, R, wide, small, n1, c, n2, rows, dqkv, low, du, g, back)
    s = s.reshape(-1)
    v = s[: 8 * piece].reshape(8, piece)
    return (
        result.reshape(1, images, tok, D),
        v[0][None],
        v[1][None],
        F_a[:, : 3 * D].astype(F32)[None],
        v[2:4][None],
        F_a[:, 3 * D : 4 * D].astype(F32)[None],
        v[4][None],
        v[5][None],
        v[6][None],
        F_b[:, :hidden].astype(F32)[None],
        s[8 * piece : 8 * piece + hidden // n][None],
        F_b[:, filled : filled + hidden].T.astype(F32)[None],
        v[7][None],
    )


def solution(mesh):
    placed = (
        P("section", ("fsdp", "replica"), None, None),
        P("section", "fsdp"),
        P("section", "fsdp"),
        P("section", "fsdp", None),
        P("section", None, "fsdp"),
        P("section", "fsdp", None),
        P("section", "fsdp"),
        P("section", "fsdp"),
        P("section", "fsdp"),
        P("section", "fsdp", None),
        P("section", "fsdp"),
        P("section", None, "fsdp"),
        P("section", "fsdp"),
    )
    return jax.shard_map(on_device, mesh=mesh, in_specs=placed, out_specs=placed, check_vma=False)
```
